256 devices in a mesh: batch: 2 (over z_hi), resp: 32 (over z_lo, x, core), head: 4 (over y).
Axes of the slice: x: 4, y: 4, z: 8 (z_hi: 2, z_lo: 4; z = z_hi * 4 + z_lo), core: 2. Of those that a mesh axis runs over, the one named last changes fastest.
Arguments:
- prompt_q: bfloat16 [4096, 8192], P(('batch', 'resp'), 'head'), parts along dimension 0, may hold values from -40 to 40
- prompt_kv: bfloat16 [4096, 2048], P(('batch', 'resp'), 'head'), parts along dimension 0, may hold values from -4 to 4
- resp_q: bfloat16 [64, 64, 8192], P(('batch', 'resp'), None, 'head'), parts along dimension 0, may hold values from -40 to 40
- resp_kv: bfloat16 [64, 64, 2048], P(('batch', 'resp'), None, 'head'), parts along dimension 0, may hold values from -4 to 4
- prompt_grad: bfloat16 [4096, 8192], P(('batch', 'resp'), 'head'), parts along dimension 0, may hold values from -6 to 6
- resp_grad: bfloat16 [64, 64, 8192], P(('batch', 'resp'), None, 'head'), parts along dimension 0, may hold values from -6 to 6
- resp_len: int32 [64], P(('batch', 'resp')), parts along dimension 0, may hold values from 1 to 64, 1536 in all
- logratio: float32 [64], P(('batch', 'resp')), parts along dimension 0, may hold values from -60 to 60
- partner: int32 [64], P(('batch', 'resp')), parts along dimension 0, may hold values from 0 to 31, as said below
- chosen: int32 [64], P(('batch', 'resp')), parts along dimension 0, may hold values from 0 to 1, as said below
Outputs:
- prompt_out: bfloat16 [4096, 8192], P(('batch', 'resp'), 'head'), parts along dimension 0
- resp_out: bfloat16 [64, 64, 8192], P(('batch', 'resp'), None, 'head'), parts along dimension 0
- prompt_dq: bfloat16 [4096, 8192], P(('batch', 'resp'), 'head'), parts along dimension 0
- resp_dq: bfloat16 [64, 64, 8192], P(('batch', 'resp'), None, 'head'), parts along dimension 0
- prompt_dkv: bfloat16 [4096, 2048], P(('batch', 'resp'), 'head'), parts along dimension 0
- resp_dkv: bfloat16 [64, 64, 2048], P(('batch', 'resp'), None, 'head'), parts along dimension 0
The draws below stay inside these ranges and needn't reach their ends.
There are 2 independent parts, one for each index of `batch`. The reference program is written for one: setup_inputs(seed, part) draws one part's arguments, and reference() takes and returns one part's arrays. A program takes and returns all parts, laid end to end along the dimension named above; each array names one. Nothing has to cross between parts.
Inputs may be any that keep to these rules, and one draw needn't show every extreme that they name: The responses of one prompt form pairs: partner[partner[j]] = j and partner[j] != j. `chosen`: exactly one response of each pair has 1.
All inputs are finite; a program needn't handle non-finite values. No bound on the sum of `resp_len` on one device may be relied on, other than what follows from the above.
Results may differ from the reference program's by a relative error of at most 0.035.
Values may be sent and summed in bfloat16 or wider, within the bound.
No kernel may reach another device: no remote copies, remote signals or barrier semaphores. Data moves between devices by JAX's collectives and lax.ppermute only.
A program may use at most 128 MiB of HBM per device.

```python
import math
import jax
import jax.numpy as jnp
import numpy as np
from jax import lax

HEADS_Q = 64
HEADS_KV = 8
HEAD_DIM = 128
RESP_LEN = 64
PROMPT_LEN = 2048
RESPONSES = 32


def shared_keys(key, blend):
    normal = jax.random.truncated_normal(jax.random.fold_in(key, 100), -4.0, 4.0, (PROMPT_LEN, HEADS_KV, HEAD_DIM), jnp.float32)
    base = normal
    row_ids = jnp.arange(PROMPT_LEN)[:, None, None]
    pair_rows = jnp.logical_and(row_ids < 6, row_ids % 2 == 1).astype(jnp.float32) * blend
    return (1.0 - pair_rows) * base


def drawn(plain, row_ids, blend):
    hot_rows = (row_ids % 17 == 16).astype(jnp.float32)[..., None] * blend
    return (1.0 - hot_rows) * plain


def query_base(key, shape):
    normal = 2.0 * jax.random.truncated_normal(jax.random.fold_in(key, 1), -4.0, 4.0, shape, jnp.float32)
    return normal


def pairing(key):
    order = jax.random.permutation(jax.random.fold_in(key, 300), RESPONSES)
    place = jnp.argsort(order, stable=True)
    mate_place = place + 1 - 2 * (place % 2)
    mates = jnp.take(order, mate_place)
    coins = jax.random.randint(jax.random.fold_in(key, 301), (RESPONSES // 2,), 0, 2)
    coin = jnp.take(coins, place // 2)
    picked = jnp.where(place % 2 == 0, coin, 1 - coin)
    return (mates.astype(jnp.int32), picked.astype(jnp.int32))


def draw_prompt_kv(key, part):
    blend = 0.0
    key_rows = shared_keys(key, blend)
    key = jax.random.fold_in(key, 3)
    normal = jax.random.truncated_normal(jax.random.fold_in(key, 1), -4.0, 4.0, (PROMPT_LEN, HEADS_KV, HEAD_DIM), jnp.float32)
    value_rows = normal
    return jnp.stack([key_rows, value_rows], axis=2).reshape(PROMPT_LEN, 2 * HEADS_KV * HEAD_DIM).astype(jnp.bfloat16)


def draw_prompt_q(key, part):
    blend = 0.0
    key = jax.random.fold_in(key, 4)
    plain = query_base(key, (PROMPT_LEN, HEADS_Q * HEAD_DIM))
    return drawn(plain, jnp.arange(PROMPT_LEN), blend).astype(jnp.bfloat16)


def draw_resp_q(key, part):
    blend = 0.0
    key = jax.random.fold_in(key, 5)
    plain = query_base(key, (RESPONSES, RESP_LEN, HEADS_Q * HEAD_DIM))
    row_ids = jnp.broadcast_to(jnp.arange(RESP_LEN)[None, :], (RESPONSES, RESP_LEN))
    return drawn(plain, row_ids, blend).astype(jnp.bfloat16)


def draw_partner(key, part):
    mates, picked = pairing(key)
    return mates


def draw_chosen(key, part):
    mates, picked = pairing(key)
    return picked


def levels(key, shape, split, low, high):
    gain, own = 1.0, jax.random.fold_in(key, 6)
    for dim, blocks in split:
        steps = jnp.exp(jax.random.uniform(jax.random.fold_in(own, dim), (blocks,), jnp.float32, low / len(split), high / len(split)))
        gain = gain * jnp.repeat(steps, shape[dim] // blocks).reshape([-1 if axis == dim else 1 for axis in range(len(shape))])
    return gain


def length_profile(amount, total, reach, slope):
    weights = [(1 << 20) // math.isqrt(grade ** slope) + 1 for grade in range(2, amount + 1)]
    spare, given = total - reach - (amount - 1), [1] * (amount - 1)
    while spare > 0:
        candidates = [i for i in range(amount - 1) if given[i] < reach]
        pool, left = sum([weights[i] for i in candidates]), spare
        for i in candidates:
            addition = min(reach - given[i], max(1, left * weights[i] // pool), spare)
            given[i] = given[i] + addition
            spare = spare - addition
    return np.array([reach] + given)


def ragged_sizes(rng, number_of, total, most, skew):
    if number_of == 2:
        one = jax.random.randint(rng, (), max(1, total - most), min(most, total - 1) + 1)
        return jnp.stack([one, total - one])
    lengths = jnp.asarray(length_profile(number_of, total, most, skew), jnp.int32)
    pairs = (number_of - 1) // 2
    giver, taker = lengths[1:1 + 2 * pairs:2], lengths[2:2 + 2 * pairs:2]
    slack = jnp.minimum(giver - 1, most - taker)
    passed = jax.random.randint(jax.random.fold_in(rng, 1), (pairs,), 0, 1 << 20) % (slack + 1)
    lengths = lengths.at[1:1 + 2 * pairs:2].set(giver - passed).at[2:2 + 2 * pairs:2].set(taker + passed)
    return lengths[jax.random.permutation(jax.random.fold_in(rng, 2), number_of)]


def noise(own_key, shape, width, bound, shards=(), kind=jnp.bfloat16):
    gain = levels(own_key, shape, shards, -0.22, 0.18) if shards else 1.0
    array = jax.random.normal(own_key, shape, jnp.float32) * width * gain
    return jnp.minimum(jnp.maximum(array, -bound), bound).astype(kind)


def setup_inputs(seed: int = 0, part: int = 0) -> dict:
    key_of = jax.random.split(jax.random.key(seed), 11)
    own_keys = jax.random.split(jax.random.fold_in(key_of[10], part), 11)
    return {
        "prompt_q": draw_prompt_q(jax.random.fold_in(jax.random.fold_in(key_of[10], part), 71), part),
        "prompt_kv": draw_prompt_kv(jax.random.fold_in(jax.random.fold_in(key_of[10], part), 71), part),
        "resp_q": draw_resp_q(jax.random.fold_in(jax.random.fold_in(key_of[10], part), 71), part),
        "resp_kv": noise(own_keys[3], (RESPONSES, RESP_LEN, 2 * HEADS_KV * HEAD_DIM), 1.0, 4.0, ((0, 32), (2, 4))),
        "prompt_grad": noise(own_keys[4], (PROMPT_LEN, HEADS_Q * HEAD_DIM), 1.0, 6.0, ((0, 32), (1, 4))),
        "resp_grad": noise(own_keys[5], (RESPONSES, RESP_LEN, HEADS_Q * HEAD_DIM), 1.0, 6.0, ((0, 32), (2, 4))),
        "resp_len": ragged_sizes(own_keys[6], RESPONSES, (3 * RESPONSES * RESP_LEN) // 4, RESP_LEN, 0).astype(jnp.int32),
        "logratio": noise(own_keys[7], (RESPONSES,), 15.0, 60.0, ((0, 32),), jnp.float32),
        "partner": draw_partner(jax.random.fold_in(jax.random.fold_in(key_of[10], part), 71), part),
        "chosen": draw_chosen(jax.random.fold_in(jax.random.fold_in(key_of[10], part), 71), part),
    }


pair_beta = 0.1
masked_score = -1e30


def head_pass(queries, key_rows, value_rows, cotangent, allowed):
    score_scale = HEAD_DIM ** -0.5
    scores = jnp.einsum("ngd,md->gnm", queries.astype(jnp.float32), key_rows.astype(jnp.float32)) * score_scale
    scores = jnp.where(allowed[None], scores, masked_score)
    row_max = jnp.max(scores, axis=-1, keepdims=True)
    raised = jnp.exp(scores - row_max)
    normed = raised / jnp.sum(raised, axis=-1, keepdims=True)
    weights = normed.astype(jnp.bfloat16)
    output = jnp.einsum("gnm,md->ngd", weights.astype(jnp.float32), value_rows.astype(jnp.float32)).astype(jnp.bfloat16)
    row_dot = jnp.sum(cotangent.astype(jnp.float32) * output.astype(jnp.float32), axis=-1)
    dweights = jnp.einsum("ngd,md->gnm", cotangent.astype(jnp.float32), value_rows.astype(jnp.float32))
    dscores = (score_scale * normed * (dweights - jnp.transpose(row_dot)[:, :, None])).astype(jnp.bfloat16)
    dqueries = jnp.einsum("gnm,md->ngd", dscores.astype(jnp.float32), key_rows.astype(jnp.float32)).astype(jnp.bfloat16)
    return output, dqueries, dscores, weights


def contract(left, right):
    return jnp.einsum("gnm,ngd->md", left.astype(jnp.float32), right.astype(jnp.float32))


def block_contract(left, right, block_count):
    groups, rows, keys = left.shape
    left_blocks = left.astype(jnp.float32).reshape(groups, block_count, rows // block_count, keys)
    right_blocks = right.astype(jnp.float32).reshape(block_count, rows // block_count, groups, right.shape[-1])
    return jnp.einsum("gbnm,bngd->bmd", left_blocks, right_blocks)


def reference(prompt_q, prompt_kv, resp_q, resp_kv, prompt_grad, resp_grad, resp_len, logratio, partner, chosen):
    prompt_len = prompt_q.shape[0]
    resp_count = resp_q.shape[0]
    length = resp_q.shape[1]
    head_pairs = prompt_kv.shape[1] // (2 * HEAD_DIM)
    group_size = prompt_q.shape[1] // (head_pairs * HEAD_DIM)
    mate_ratio = jnp.take(logratio, partner)
    pair_sign = 2.0 * chosen.astype(jnp.float32) - 1.0
    margin = pair_sign * (logratio - mate_ratio)
    pair_weight = pair_sign * jax.nn.sigmoid(-pair_beta * margin)
    positions = jnp.arange(length, dtype=jnp.int32)
    live_rows = (positions[None, :] < resp_len[:, None]).astype(jnp.float32)
    resp_cot = (pair_weight[:, None, None] * live_rows[:, :, None] * resp_grad.astype(jnp.float32)).astype(jnp.bfloat16)
    columns = jnp.arange(prompt_len, dtype=jnp.int32)
    prompt_allowed = columns[None, :] <= columns[:, None]
    resp_allowed = jnp.concatenate([jnp.ones((length, prompt_len), bool), positions[None, :] <= positions[:, None]], axis=1)
    prompt_query = jnp.moveaxis(prompt_q.reshape(prompt_len, head_pairs, group_size, HEAD_DIM), 1, 0)
    prompt_cot = jnp.moveaxis(prompt_grad.reshape(prompt_len, head_pairs, group_size, HEAD_DIM), 1, 0)
    shared_rows = jnp.moveaxis(prompt_kv.reshape(prompt_len, head_pairs, 2, HEAD_DIM), 1, 0)
    resp_query = jnp.moveaxis(resp_q.reshape(resp_count, length, head_pairs, group_size, HEAD_DIM), 2, 1)
    resp_cots = jnp.moveaxis(resp_cot.reshape(resp_count, length, head_pairs, group_size, HEAD_DIM), 2, 1)
    own_rows = jnp.moveaxis(resp_kv.reshape(resp_count, length, head_pairs, 2, HEAD_DIM), 2, 1)

    def prompt_head(operands):
        queries, cotangent, rows = operands
        output, dqueries, dscores, weights = head_pass(queries, rows[:, 0], rows[:, 1], cotangent, prompt_allowed)
        return output, dqueries, block_contract(dscores, queries, resp_count), block_contract(weights, cotangent, resp_count)

    prompt_parts = lax.map(prompt_head, (prompt_query, prompt_cot, shared_rows))
    prompt_key_blocks = jnp.moveaxis(prompt_parts[2], 1, 0)
    prompt_value_blocks = jnp.moveaxis(prompt_parts[3], 1, 0)

    def resp_head(operands):
        queries, cotangent, rows, own = operands
        key_rows = jnp.concatenate([rows[:, 0], own[:, 0]], axis=0)
        value_rows = jnp.concatenate([rows[:, 1], own[:, 1]], axis=0)
        output, dqueries, dscores, weights = head_pass(queries, key_rows, value_rows, cotangent, resp_allowed)
        key_grad = contract(dscores, queries)
        value_grad = contract(weights, cotangent)
        return output, dqueries, key_grad[:prompt_len], value_grad[:prompt_len], key_grad[prompt_len:], value_grad[prompt_len:]

    def one_response(carry, operands):
        queries, cotangent, own, key_block, value_block = operands
        parts = lax.map(resp_head, (queries, cotangent, shared_rows, own))
        key_part = lax.optimization_barrier((key_block + parts[2]).astype(jnp.bfloat16)).astype(jnp.float32)
        value_part = lax.optimization_barrier((value_block + parts[3]).astype(jnp.bfloat16)).astype(jnp.float32)
        return (carry[0] + key_part, carry[1] + value_part), (parts[0], parts[1], parts[4], parts[5])

    start = jnp.zeros((head_pairs, prompt_len, HEAD_DIM), jnp.float32)
    sums, resp_parts = lax.scan(one_response, (start, start), (resp_query, resp_cots, own_rows, prompt_key_blocks, prompt_value_blocks))
    prompt_out = jnp.moveaxis(prompt_parts[0], 0, 1).reshape(prompt_len, -1)
    prompt_dq = jnp.moveaxis(prompt_parts[1], 0, 1).reshape(prompt_len, -1)
    resp_out = jnp.moveaxis(resp_parts[0], 1, 2).reshape(resp_count, length, -1)
    resp_dq = jnp.moveaxis(resp_parts[1], 1, 2).reshape(resp_count, length, -1)
    prompt_dkv = jnp.moveaxis(jnp.stack([sums[0], sums[1]], axis=2), 0, 1).reshape(prompt_len, -1).astype(jnp.bfloat16)
    resp_dkv = jnp.moveaxis(jnp.stack([resp_parts[2], resp_parts[3]], axis=3), 1, 2).reshape(resp_count, length, -1).astype(jnp.bfloat16)
    return prompt_out, resp_out, prompt_dq, resp_dq, prompt_dkv, resp_dkv
```

```python
import functools

import jax
import jax.numpy as jnp
from jax import lax
from jax.experimental import pallas as pl
from jax.experimental.pallas import tpu as pltpu
from jax.sharding import PartitionSpec as P

HEAD_DIM = 128
GROUP = 8
TOKENS = 64
KV_COLS = 2 * HEAD_DIM
Q_COLS = GROUP * HEAD_DIM
BLOCK = 2 * TOKENS
CHUNK = 4 * BLOCK
TILE = GROUP * TOKENS
LANES = 4 * TILE
SUB = 256

score_scale = HEAD_DIM ** (-0.5)
exp2_scale = score_scale * 1.4426950408889634
pair_beta = 0.1
blocked_score = -(2.0**30)
no_max = -(2.0**31)

bf16 = jnp.bfloat16
f32 = jnp.float32


def params(**kw):
    return pltpu.CompilerParams(vmem_limit_bytes=40 * 2**20, **kw)


def dot(left, right, left_dim=1, right_dim=0):
    return lax.dot_general(
        left, right, (((left_dim,), (right_dim,)), ((), ())), preferred_element_type=f32
    )


def iota(shape, dim):
    return lax.broadcasted_iota(jnp.int32, shape, dim)


def swap_core(value):
    return lax.ppermute(value, "resp", [(r, r ^ 1) for r in range(32)])


def shift_z(value, step):
    pairs = [(r, ((r // 8 + step) % 4) * 8 + r % 8) for r in range(32)]
    return lax.ppermute(value, "resp", pairs)


def shift_x(value, step):
    pairs = [(r, (r // 8) * 8 + (r % 8 // 2 + step) % 4 * 2 + r % 2) for r in range(32)]
    return lax.ppermute(value, "resp", pairs)


def pack_kv_kernel(info, p_own, r_own, p_sib, r_sib, own, send):
    own[:TOKENS] = p_own[...]
    own[TOKENS:] = r_own[0]
    send[:TOKENS] = p_sib[...]
    send[TOKENS:] = r_sib[0]


def pack_kv(info, prompt_kv, resp_kv):
    two = (TOKENS, KV_COLS)
    three = (1, TOKENS, KV_COLS)
    return pl.pallas_call(
        pack_kv_kernel,
        grid_spec=pltpu.PrefetchScalarGridSpec(
            num_scalar_prefetch=1,
            grid=(1,),
            in_specs=[
                pl.BlockSpec(two, lambda i, s: (0, s[0])),
                pl.BlockSpec(three, lambda i, s: (0, 0, s[0])),
                pl.BlockSpec(two, lambda i, s: (0, 1 - s[0])),
                pl.BlockSpec(three, lambda i, s: (0, 0, 1 - s[0])),
            ],
            out_specs=[pl.BlockSpec((BLOCK, KV_COLS), lambda i, s: (0, 0))] * 2,
        ),
        out_shape=[jax.ShapeDtypeStruct((BLOCK, KV_COLS), bf16)] * 2,
        compiler_params=params(),
        name="pack_kv",
    )(info, prompt_kv, resp_kv, prompt_kv, resp_kv)


def pack_q_kernel(info, pq, rq, pg, rg, send):
    send[0] = pq[...]
    send[1] = rq[0]
    send[2] = pg[...]
    send[3] = rg[0]


def pack_q(info, prompt_q, resp_q, prompt_grad, resp_grad):
    two = pl.BlockSpec((TOKENS, Q_COLS), lambda i, s: (0, 1 - s[0]))
    three = pl.BlockSpec((1, TOKENS, Q_COLS), lambda i, s: (0, 0, 1 - s[0]))
    return pl.pallas_call(
        pack_q_kernel,
        grid_spec=pltpu.PrefetchScalarGridSpec(
            num_scalar_prefetch=1,
            grid=(1,),
            in_specs=[two, three, two, three],
            out_specs=pl.BlockSpec((4, TOKENS, Q_COLS), lambda i, s: (0, 0, 0)),
        ),
        out_shape=jax.ShapeDtypeStruct((4, TOKENS, Q_COLS), bf16),
        compiler_params=params(),
        name="pack_q",
    )(info, prompt_q, resp_q, prompt_grad, resp_grad)


def turned(block):
    rows = jnp.concatenate(
        [block[:, g * HEAD_DIM : (g + 1) * HEAD_DIM] for g in range(GROUP)], axis=0
    )
    return rows.T


def softmax_part(scores, value_rows):
    top = jnp.max(scores, axis=0, keepdims=True)
    raised = jnp.exp2((scores - top) * exp2_scale).astype(bf16)
    total = dot(value_rows, raised)
    packed = jnp.concatenate(
        [total[: HEAD_DIM + 8], jnp.broadcast_to(top, (8, top.shape[1]))], axis=0
    )
    return raised, packed


def with_ones(value_rows):
    return jnp.concatenate([value_rows.T, jnp.ones((16, value_rows.shape[0]), bf16)], axis=0)


def prep_kernel(info, pq, rq, pg, rg, recv, kv_own, kv_recv, q_aug, grads, raised, packed):
    core = info[0]
    none = jnp.concatenate(
        [jnp.zeros((HEAD_DIM + 8, TILE), f32), jnp.full((8, TILE), no_max, f32)], axis=0
    )
    for j in range(4):
        lanes = slice(j * TILE, (j + 1) * TILE)
        sib, resp = j // 2, j % 2
        if sib:
            block, grad = recv[resp], recv[2 + resp]
        else:
            block, grad = (rq[0], rg[0]) if resp else (pq[...], pg[...])
        turned_q = turned(block)
        q_aug[:HEAD_DIM, lanes] = turned_q
        grads[:, lanes] = turned(grad)
        if resp:
            q_aug[HEAD_DIM:, lanes] = jnp.zeros((HEAD_DIM, TILE), bf16)
            rows = (kv_recv if sib else kv_own)[TOKENS:]
            scores = dot(rows[:, :HEAD_DIM], turned_q)
            token = iota(scores.shape, 1) % TOKENS
            scores = jnp.where(iota(scores.shape, 0) <= token, scores, blocked_score)
            part, info_rows = softmax_part(scores, with_ones(rows[:, HEAD_DIM:]))
            raised[:, sib * TILE : (sib + 1) * TILE] = part
            packed[:, lanes] = info_rows
        else:
            own_core = 1 - core if sib else core
            token = iota((HEAD_DIM, TILE), 1) % TOKENS + own_core * TOKENS
            row = iota((HEAD_DIM, TILE), 0)
            hidden = jnp.logical_or(row == 0, row > token)
            q_aug[HEAD_DIM:, lanes] = jnp.where(hidden, blocked_score, 0.0).astype(bf16)
            packed[:, lanes] = none


def prep(info, prompt_q, resp_q, prompt_grad, resp_grad, recv, kv_own, kv_recv):
    two = pl.BlockSpec((TOKENS, Q_COLS), lambda i, s: (0, s[0]))
    three = pl.BlockSpec((1, TOKENS, Q_COLS), lambda i, s: (0, 0, s[0]))

    def whole(*shape):
        return pl.BlockSpec(shape, lambda i, s: (0,) * len(shape))

    return pl.pallas_call(
        prep_kernel,
        grid_spec=pltpu.PrefetchScalarGridSpec(
            num_scalar_prefetch=1,
            grid=(1,),
            in_specs=[
                two,
                three,
                two,
                three,
                whole(4, TOKENS, Q_COLS),
                whole(BLOCK, KV_COLS),
                whole(BLOCK, KV_COLS),
            ],
            out_specs=[
                whole(2 * HEAD_DIM, LANES),
                whole(HEAD_DIM, LANES),
                whole(TOKENS, 2 * TILE),
                whole(HEAD_DIM + 16, LANES),
            ],
        ),
        out_shape=[
            jax.ShapeDtypeStruct((2 * HEAD_DIM, LANES), bf16),
            jax.ShapeDtypeStruct((HEAD_DIM, LANES), bf16),
            jax.ShapeDtypeStruct((TOKENS, 2 * TILE), bf16),
            jax.ShapeDtypeStruct((HEAD_DIM + 16, LANES), f32),
        ],
        compiler_params=params(),
        name="prep",
    )(info, prompt_q, resp_q, prompt_grad, resp_grad, recv, kv_own, kv_recv)


def forward_kernel(offset, info, kv, q_aug, raised, packed, key_aug, value_rows):
    @pl.when(pl.program_id(0) == 0)
    def _():
        core, z_own, x_own = info[0], info[1], info[2]
        x_here = (x_own + offset) % 4
        row = iota((BLOCK, HEAD_DIM), 1)
        token = (iota((BLOCK, HEAD_DIM), 0) + core * TOKENS) % BLOCK
        first = (row == 0).astype(f32)
        same = jnp.logical_and(row == token, row > 0).astype(f32)
        for p in range(4):
            rows = slice(p * BLOCK, (p + 1) * BLOCK)
            z_here = (z_own + 4 - p) % 4
            later = jnp.logical_or(
                z_here > z_own, jnp.logical_and(z_here == z_own, x_here > x_own)
            )
            diagonal = jnp.logical_and(z_here == z_own, x_here == x_own)
            key_aug[rows, :HEAD_DIM] = kv[rows, :HEAD_DIM]
            key_aug[rows, HEAD_DIM:] = (
                first * later.astype(f32) + same * diagonal.astype(f32)
            ).astype(bf16)
        value_rows[...] = with_ones(kv[:, HEAD_DIM:])

    for s in range(TILE // SUB):
        lanes = slice(s * SUB, (s + 1) * SUB)
        part, info_rows = softmax_part(dot(key_aug[...], q_aug[:, lanes]), value_rows[...])
        raised[:, lanes] = part
        packed[:, lanes] = info_rows


def forward(info, kv, q_aug, offset):
    return pl.pallas_call(
        functools.partial(forward_kernel, offset),
        grid_spec=pltpu.PrefetchScalarGridSpec(
            num_scalar_prefetch=1,
            grid=(4,),
            in_specs=[
                pl.BlockSpec((CHUNK, KV_COLS), lambda j, s: (0, 0)),
                pl.BlockSpec((2 * HEAD_DIM, TILE), lambda j, s: (0, j)),
            ],
            out_specs=[
                pl.BlockSpec((CHUNK, TILE), lambda j, s: (0, j)),
                pl.BlockSpec((HEAD_DIM + 16, TILE), lambda j, s: (0, j)),
            ],
            scratch_shapes=[
                pltpu.VMEM((CHUNK, 2 * HEAD_DIM), bf16),
                pltpu.VMEM((HEAD_DIM + 16, CHUNK), bf16),
            ],
        ),
        out_shape=[
            jax.ShapeDtypeStruct((CHUNK, LANES), bf16),
            jax.ShapeDtypeStruct((HEAD_DIM + 16, LANES), f32),
        ],
        compiler_params=params(),
        cost_estimate=pl.CostEstimate(
            flops=4 * CHUNK * LANES * HEAD_DIM, bytes_accessed=5 * 2**20, transcendentals=0
        ),
        name="forward",
    )(info, kv, q_aug)


def combine_kernel(info, table, grads, part_0, part_1, part_2, part_3, part_own, out, cot_aug, gains):
    j = pl.program_id(0)
    parts = (part_0, part_1, part_2, part_3, part_own)
    tops = [part[HEAD_DIM + 8 : HEAD_DIM + 9, :] for part in parts]
    top = functools.reduce(jnp.maximum, tops)
    factors = [jnp.exp2((one - top) * exp2_scale) for one in tops]
    length = sum(f * part[HEAD_DIM : HEAD_DIM + 1, :] for f, part in zip(factors, parts))
    total = sum(f * part[:HEAD_DIM, :] for f, part in zip(factors, parts))
    inverse = 1.0 / length
    rounded = (total * inverse).astype(bf16)
    out[...] = rounded
    gains[...] = jnp.concatenate(
        [f * inverse for f in factors] + [jnp.zeros((3, TILE), f32)], axis=0
    )
    own = info[1] * 8 + info[2] * 2 + jnp.where(j < 2, info[0], 1 - info[0])
    ids = iota((32, 1), 0)
    here = ids == own

    def pick(column, mask):
        return jnp.sum(
            jnp.where(mask, table[:, column : column + 1], 0.0), axis=0, keepdims=True
        )

    ratio, partner, chosen, count = [pick(column, here) for column in range(4)]
    mate = pick(0, ids.astype(f32) == partner)
    sign = 2.0 * chosen - 1.0
    pair_weight = sign * jax.nn.sigmoid(-pair_beta * (sign * (ratio - mate)))
    token = (iota((1, TILE), 1) % TOKENS).astype(f32)
    weight = jnp.where(token < count, pair_weight, 0.0)
    weight = jnp.where(j % 2 == 1, weight, 1.0)
    cot = (weight * grads[...].astype(f32)).astype(bf16)
    cot_aug[:HEAD_DIM] = cot
    row_dot = -jnp.sum(cot.astype(f32) * rounded.astype(f32), axis=0, keepdims=True)
    high = row_dot.astype(bf16).astype(f32)
    middle = (row_dot - high).astype(bf16).astype(f32)
    low = row_dot - high - middle
    row = iota((HEAD_DIM, TILE), 0)
    cot_aug[HEAD_DIM:] = jnp.where(
        row == 0, high, jnp.where(row == 1, middle, jnp.where(row == 2, low, 0.0))
    ).astype(bf16)


def combine(info, table, grads, parts):
    def tile(rows):
        return pl.BlockSpec((rows, TILE), lambda j, s: (0, j))

    return pl.pallas_call(
        combine_kernel,
        grid_spec=pltpu.PrefetchScalarGridSpec(
            num_scalar_prefetch=1,
            grid=(4,),
            in_specs=[pl.BlockSpec((32, 128), lambda j, s: (0, 0)), tile(HEAD_DIM)]
            + [tile(HEAD_DIM + 16)] * 5,
            out_specs=[tile(HEAD_DIM), tile(2 * HEAD_DIM), tile(8)],
        ),
        out_shape=[
            jax.ShapeDtypeStruct((HEAD_DIM, LANES), bf16),
            jax.ShapeDtypeStruct((2 * HEAD_DIM, LANES), bf16),
            jax.ShapeDtypeStruct((8, LANES), f32),
        ],
        compiler_params=params(),
        name="combine",
    )(info, table, grads, *parts)


def value_aug_of(value_rows):
    column = iota(value_rows.shape, 1)
    return jnp.concatenate([value_rows, (column < 3).astype(f32).astype(bf16)], axis=1)


def backward_kernel(chunk, kv, raised, q_aug, cot_aug, gains, slopes, grad, value_aug, dkey, dvalue):
    j = pl.program_id(0)

    @pl.when(j == 0)
    def _():
        value_aug[...] = value_aug_of(kv[:, HEAD_DIM:])
        dkey[...] = jnp.zeros_like(dkey)
        dvalue[...] = jnp.zeros_like(dvalue)

    gain = gains[chunk : chunk + 1, :]
    scaled_q = (q_aug[...].astype(f32) * (gain * score_scale)).astype(bf16)
    scaled_cot = (cot_aug[:HEAD_DIM].astype(f32) * gain).astype(bf16)
    for s in range(TILE // SUB):
        lanes = slice(s * SUB, (s + 1) * SUB)
        moved = dot(value_aug[...], cot_aug[:, lanes])
        slopes[:, lanes] = (raised[:, lanes].astype(f32) * moved).astype(bf16)
    dkey[...] += dot(slopes[...], scaled_q, 1, 1)
    dvalue[...] += dot(raised[...], scaled_cot, 1, 1)

    @pl.when(j == 3)
    def _():
        grad[:, :HEAD_DIM] = dkey[...].astype(grad.dtype)
        grad[:, HEAD_DIM:] = dvalue[...].astype(grad.dtype)


def backward(kv, raised, q_aug, cot_aug, gains, chunk, kind):
    def tile(rows):
        return pl.BlockSpec((rows, TILE), lambda j: (0, j))

    return pl.pallas_call(
        functools.partial(backward_kernel, chunk),
        grid=(4,),
        in_specs=[
            pl.BlockSpec((CHUNK, KV_COLS), lambda j: (0, 0)),
            tile(CHUNK),
            tile(HEAD_DIM),
            tile(2 * HEAD_DIM),
            tile(8),
        ],
        out_specs=[tile(CHUNK), pl.BlockSpec((CHUNK, KV_COLS), lambda j: (0, 0))],
        scratch_shapes=[
            pltpu.VMEM((CHUNK, 2 * HEAD_DIM), bf16),
            pltpu.VMEM((CHUNK, HEAD_DIM), f32),
            pltpu.VMEM((CHUNK, HEAD_DIM), f32),
        ],
        out_shape=[
            jax.ShapeDtypeStruct((CHUNK, LANES), bf16),
            jax.ShapeDtypeStruct((CHUNK, KV_COLS), kind),
        ],
        compiler_params=params(),
        cost_estimate=pl.CostEstimate(
            flops=6 * CHUNK * LANES * HEAD_DIM, bytes_accessed=6 * 2**20, transcendentals=0
        ),
        name="backward",
    )(kv, raised, q_aug, cot_aug, gains)


def rows_of(turned_rows):
    rows = turned_rows.T
    return jnp.concatenate(
        [rows[g * TOKENS : (g + 1) * TOKENS] for g in range(GROUP)], axis=1
    )


def finish_kernel(
    kv_0, kv_1, kv_2, kv_3, slopes_0, slopes_1, slopes_2, slopes_3,
    kv_own, raised, q_aug, cot_aug, gains, out, result, own_grad, keys, total,
):
    j = pl.program_id(0)

    @pl.when(j == 0)
    def _():
        for chunk, kv in enumerate((kv_0, kv_1, kv_2, kv_3)):
            keys[:, chunk * CHUNK : (chunk + 1) * CHUNK] = kv[:, :HEAD_DIM].T

    acc = None
    for chunk, slopes in enumerate((slopes_0, slopes_1, slopes_2, slopes_3)):
        part = dot(keys[:, chunk * CHUNK : (chunk + 1) * CHUNK], slopes[...])
        part = part * (gains[chunk : chunk + 1, :] * score_scale)
        acc = part if acc is None else acc + part
    total[...] = acc

    @pl.when(j == 1)
    def _():
        gain = gains[4:5, :]
        rows = kv_own[TOKENS:]
        moved = dot(value_aug_of(rows[:, HEAD_DIM:]), cot_aug[...])
        slopes = (raised[...].astype(f32) * moved).astype(bf16)
        total[...] += dot(rows[:, :HEAD_DIM].T, slopes) * (gain * score_scale)
        scaled_q = (q_aug[...].astype(f32) * (gain * score_scale)).astype(bf16)
        scaled_cot = (cot_aug[:HEAD_DIM].astype(f32) * gain).astype(bf16)
        own_grad[:, :HEAD_DIM] = dot(slopes, scaled_q, 1, 1).astype(bf16)
        own_grad[:, HEAD_DIM:] = dot(raised[...], scaled_cot, 1, 1).astype(bf16)

    result[0, 0] = rows_of(out[...].astype(f32)).astype(bf16)
    result[0, 1] = rows_of(total[...]).astype(bf16)


def finish(kvs, slopes, kv_own, raised, q_aug, cot_aug, gains, out, sib):
    def whole(*shape):
        return pl.BlockSpec(shape, lambda j: (0,) * len(shape))

    def tile(rows):
        return pl.BlockSpec((rows, TILE), lambda j: (0, 2 * sib + j))

    return pl.pallas_call(
        finish_kernel,
        grid=(2,),
        in_specs=[whole(CHUNK, KV_COLS)] * 4
        + [tile(CHUNK)] * 4
        + [
            whole(BLOCK, KV_COLS),
            pl.BlockSpec((TOKENS, TILE), lambda j: (0, sib)),
            tile(HEAD_DIM),
            tile(2 * HEAD_DIM),
            tile(8),
            tile(HEAD_DIM),
        ],
        out_specs=[
            pl.BlockSpec((1, 2, TOKENS, Q_COLS), lambda j: (j, 0, 0, 0)),
            whole(TOKENS, KV_COLS),
        ],
        scratch_shapes=[
            pltpu.VMEM((HEAD_DIM, 4 * CHUNK), bf16),
            pltpu.VMEM((HEAD_DIM, TILE), f32),
        ],
        out_shape=[
            jax.ShapeDtypeStruct((2, 2, TOKENS, Q_COLS), bf16),
            jax.ShapeDtypeStruct((TOKENS, KV_COLS), bf16),
        ],
        compiler_params=params(),
        cost_estimate=pl.CostEstimate(
            flops=4 * CHUNK * LANES * HEAD_DIM, bytes_accessed=5 * 2**20, transcendentals=0
        ),
        name="finish",
    )(*kvs, *slopes, kv_own, raised, q_aug, cot_aug, gains, out)


def place_kernel(info, own, recv, own_dkv, recv_dkv, prompt_out, resp_out, prompt_dq, resp_dq, resp_dkv):
    def write(source, dkv):
        prompt_out[...] = source[0, 0]
        prompt_dq[...] = source[0, 1]
        resp_out[0] = source[1, 0]
        resp_dq[0] = source[1, 1]
        resp_dkv[0] = dkv[...]

    @pl.when(pl.program_id(0) == 0)
    def _():
        write(own, own_dkv)

    @pl.when(pl.program_id(0) == 1)
    def _():
        write(recv, recv_dkv)


def place(info, own, recv, own_dkv, recv_dkv):
    def whole(*shape):
        return pl.BlockSpec(shape, lambda i, s: (0,) * len(shape))

    def column(i, s):
        return s[0] + i - 2 * s[0] * i

    two = pl.BlockSpec((TOKENS, Q_COLS), lambda i, s: (0, column(i, s)))
    three = pl.BlockSpec((1, TOKENS, Q_COLS), lambda i, s: (0, 0, column(i, s)))
    prompt = jax.ShapeDtypeStruct((TOKENS, 2 * Q_COLS), bf16)
    resp = jax.ShapeDtypeStruct((1, TOKENS, 2 * Q_COLS), bf16)
    return pl.pallas_call(
        place_kernel,
        grid_spec=pltpu.PrefetchScalarGridSpec(
            num_scalar_prefetch=1,
            grid=(2,),
            in_specs=[whole(2, 2, TOKENS, Q_COLS)] * 2 + [whole(TOKENS, KV_COLS)] * 2,
            out_specs=[
                two,
                three,
                two,
                three,
                pl.BlockSpec((1, TOKENS, KV_COLS), lambda i, s: (0, 0, column(i, s))),
            ],
        ),
        out_shape=[
            prompt,
            resp,
            prompt,
            resp,
            jax.ShapeDtypeStruct((1, TOKENS, 2 * KV_COLS), bf16),
        ],
        compiler_params=params(),
        name="place",
    )(info, own, recv, own_dkv, recv_dkv)


def sum_x_kernel(own, recv_1, recv_2, recv_3, first, second, third, fourth):
    for p, out in enumerate((first, second, third, fourth)):
        rows = slice(p * BLOCK, (p + 1) * BLOCK)
        total = own[rows]
        for recv in (recv_1, recv_2, recv_3):
            total = total + recv[rows].astype(f32)
        out[...] = total.astype(out.dtype)


def sum_x(own, recvs):
    return pl.pallas_call(
        sum_x_kernel,
        out_shape=[
            jax.ShapeDtypeStruct((BLOCK, KV_COLS), f32 if p == 0 else bf16) for p in range(4)
        ],
        compiler_params=params(),
        name="sum_x",
    )(own, *recvs)


def sum_z_kernel(own, recv_1, recv_2, recv_3, kept, sent):
    total = own[...]
    for recv in (recv_1, recv_2, recv_3):
        total = total + recv[...].astype(f32)
    kept[...] = total[:TOKENS].astype(bf16)
    sent[...] = total[TOKENS:].astype(bf16)


def sum_z(own, recvs):
    return pl.pallas_call(
        sum_z_kernel,
        out_shape=[jax.ShapeDtypeStruct((TOKENS, KV_COLS), bf16)] * 2,
        compiler_params=params(),
        name="sum_z",
    )(own, *recvs)


def shards(
    prompt_q,
    prompt_kv,
    resp_q,
    resp_kv,
    prompt_grad,
    resp_grad,
    resp_len,
    logratio,
    partner,
    chosen,
):
    own_index = lax.axis_index("resp")
    core = own_index % 2
    info = jnp.stack([core, own_index // 8, own_index // 2 % 4]).astype(jnp.int32)

    kv_own, kv_send = pack_kv(info, prompt_kv, resp_kv)
    kv_recv = swap_core(kv_send)
    q_send = pack_q(info, prompt_q, resp_q, prompt_grad, resp_grad)
    q_recv = swap_core(q_send)

    scalars = jnp.concatenate(
        [
            logratio,
            partner.astype(f32),
            chosen.astype(f32),
            resp_len.astype(f32),
            jnp.zeros((124,), f32),
        ]
    )
    table = lax.all_to_all(
        jnp.broadcast_to(scalars[None, :], (32, 128)), "resp", split_axis=0, concat_axis=0, tiled=True
    )

    block = jnp.concatenate([kv_own[:TOKENS], kv_recv[:TOKENS]], axis=0)
    chunk_own = jnp.concatenate([block] + [shift_z(block, step) for step in (1, 2, 3)], axis=0)
    offsets = (0, 3, 1, 2)
    kvs = [chunk_own] + [shift_x(chunk_own, 4 - offset) for offset in offsets[1:]]

    q_aug, grads, raised_own, part_own = prep(
        info, prompt_q, resp_q, prompt_grad, resp_grad, q_recv, kv_own, kv_recv
    )
    raised, parts = [], []
    for kv, offset in zip(kvs, offsets):
        one, part = forward(info, kv, q_aug, offset)
        raised.append(one)
        parts.append(part)
    out, cot_aug, gains = combine(info, table, grads, parts + [part_own])

    slopes = [None] * 4
    returned = []
    for chunk in (3, 2, 1, 0):
        kind = bf16 if chunk else f32
        slopes[chunk], grad = backward(
            kvs[chunk], raised[chunk], q_aug, cot_aug, gains, chunk, kind
        )
        returned.append(shift_x(grad, offsets[chunk]) if chunk else grad)

    blocks = sum_x(returned[3], returned[:3])
    recvs = [shift_z(blocks[p], 4 - p) for p in (1, 2, 3)]

    sib_result, sib_dkv = finish(
        kvs, slopes, kv_recv, raised_own, q_aug, cot_aug, gains, out, 1
    )
    recv_result = swap_core(sib_result)
    recv_dkv = swap_core(sib_dkv)
    own_result, own_dkv = finish(
        kvs, slopes, kv_own, raised_own, q_aug, cot_aug, gains, out, 0
    )
    prompt_out, resp_out, prompt_dq, resp_dq, resp_dkv = place(
        info, own_result, recv_result, own_dkv, recv_dkv
    )

    kept, sent = sum_z(blocks[0], recvs)
    other = swap_core(sent)
    prompt_dkv = jnp.where(
        core == 0,
        jnp.concatenate([kept, other], axis=1),
        jnp.concatenate([other, kept], axis=1),
    )
    return (prompt_out, resp_out, prompt_dq, resp_dq, prompt_dkv, resp_dkv)


def solution(mesh):
    return jax.shard_map(
        shards,
        mesh=mesh,
        in_specs=(
            P(("batch", "resp"), "head"),
            P(("batch", "resp"), "head"),
            P(("batch", "resp"), None, "head"),
            P(("batch", "resp"), None, "head"),
            P(("batch", "resp"), "head"),
            P(("batch", "resp"), None, "head"),
            P(("batch", "resp")),
            P(("batch", "resp")),
            P(("batch", "resp")),
            P(("batch", "resp")),
        ),
        out_specs=(
            P(("batch", "resp"), "head"),
            P(("batch", "resp"), None, "head"),
            P(("batch", "resp"), "head"),
            P(("batch", "resp"), None, "head"),
            P(("batch", "resp"), "head"),
            P(("batch", "resp"), None, "head"),
        ),
        check_vma=False,
    )
```

```python
import functools

import jax
import jax.numpy as jnp
from jax import lax
from jax.experimental import pallas as pl
from jax.experimental.pallas import tpu as pltpu
from jax.sharding import PartitionSpec as P

HEAD_DIM = 128
GROUP = 8
TOKENS = 64
KV_COLS = 2 * HEAD_DIM
Q_COLS = GROUP * HEAD_DIM
BLOCK = 2 * TOKENS
NOTE = 16
PIECE = BLOCK + NOTE
CHUNK = 4 * BLOCK
TILE = GROUP * TOKENS
LANES = 4 * TILE
SUB = 256

score_scale = HEAD_DIM ** (-0.5)
exp2_scale = score_scale * 1.4426950408889634
pair_beta = 0.1
blocked_score = -(2.0**30)
no_max = -(2.0**31)

bf16 = jnp.bfloat16
f32 = jnp.float32


def params(**kw):
    return pltpu.CompilerParams(vmem_limit_bytes=16 * 2**20, **kw)


def dot(left, right, left_dim=1, right_dim=0):
    return lax.dot_general(
        left, right, (((left_dim,), (right_dim,)), ((), ())), preferred_element_type=f32
    )


def iota(shape, dim):
    return lax.broadcasted_iota(jnp.int32, shape, dim)


def swap_core(value):
    return lax.ppermute(value, "resp", [(r, r ^ 1) for r in range(32)])


def shift_z(value, step):
    pairs = [(r, ((r // 8 + step) % 4) * 8 + r % 8) for r in range(32)]
    return lax.ppermute(value, "resp", pairs)


def shift_x(value, step):
    pairs = [(r, (r // 8) * 8 + (r % 8 // 2 + step) % 4 * 2 + r % 2) for r in range(32)]
    return lax.ppermute(value, "resp", pairs)


def columns(core, width):
    return pl.ds(pl.multiple_of(core * width, width), width)


def run_copies(pairs, sems):
    copies = [pltpu.make_async_copy(a, b, sems.at[i]) for i, (a, b) in enumerate(pairs)]
    for copy in copies:
        copy.start()
    for copy in copies:
        copy.wait()


def pack_kv_kernel(info, facts, prompt_kv, resp_kv, own, send, sems):
    core = info[0]
    pairs = []
    for side, out in ((core, own), (1 - core, send)):
        cols = columns(side, KV_COLS)
        pairs.append((prompt_kv.at[:, cols], out.at[pl.ds(0, TOKENS)]))
        pairs.append((resp_kv.at[0, :, cols], out.at[pl.ds(TOKENS, TOKENS)]))
    copies = [pltpu.make_async_copy(a, b, sems.at[i]) for i, (a, b) in enumerate(pairs)]
    for copy in copies:
        copy.start()
    row, lane = iota((NOTE, KV_COLS), 0), iota((NOTE, KV_COLS), 1)
    ratio = jnp.full((NOTE, KV_COLS), facts[0], f32)
    high = ratio.astype(bf16).astype(f32)
    middle = (ratio - high).astype(bf16).astype(f32)
    low = ratio - high - middle
    note = jnp.zeros((NOTE, KV_COLS), f32)
    for field, value in enumerate((high, middle, low, facts[1], facts[2], facts[3])):
        note = jnp.where(lane == core * 8 + field, value, note)
    note = jnp.where(row == 0, note, 0.0).astype(bf16)
    own[BLOCK:] = note
    send[BLOCK:] = note
    for copy in copies:
        copy.wait()


def pack_kv(info, facts, prompt_kv, resp_kv):
    return pl.pallas_call(
        pack_kv_kernel,
        in_specs=[pl.BlockSpec(memory_space=pltpu.SMEM)] * 2
        + [pl.BlockSpec(memory_space=pltpu.HBM)] * 2,
        out_shape=[jax.ShapeDtypeStruct((PIECE, KV_COLS), bf16)] * 2,
        scratch_shapes=[pltpu.SemaphoreType.DMA((4,))],
        compiler_params=params(),
        name="pack_kv",
    )(info, facts, prompt_kv, resp_kv)


def pack_q_kernel(info, pq, rq, pg, rg, send, sems):
    cols = columns(1 - info[0], Q_COLS)
    run_copies(
        [
            (pq.at[:, cols], send.at[0]),
            (rq.at[0, :, cols], send.at[1]),
            (pg.at[:, cols], send.at[2]),
            (rg.at[0, :, cols], send.at[3]),
        ],
        sems,
    )


def pack_q(info, prompt_q, resp_q, prompt_grad, resp_grad):
    return pl.pallas_call(
        pack_q_kernel,
        in_specs=[pl.BlockSpec(memory_space=pltpu.SMEM)]
        + [pl.BlockSpec(memory_space=pltpu.HBM)] * 4,
        out_shape=jax.ShapeDtypeStruct((4, TOKENS, Q_COLS), bf16),
        scratch_shapes=[pltpu.SemaphoreType.DMA((4,))],
        compiler_params=params(),
        name="pack_q",
    )(info, prompt_q, resp_q, prompt_grad, resp_grad)


def turned(block):
    rows = jnp.concatenate(
        [block[:, g * HEAD_DIM : (g + 1) * HEAD_DIM] for g in range(GROUP)], axis=0
    )
    return rows.T


def softmax_part(scores, value_rows):
    top = jnp.max(scores, axis=0, keepdims=True)
    raised = jnp.exp2((scores - top) * exp2_scale).astype(bf16)
    total = dot(value_rows, raised)
    packed = jnp.concatenate(
        [total[: HEAD_DIM + 8], jnp.broadcast_to(top, (8, top.shape[1]))], axis=0
    )
    return raised, packed


def with_ones(value_rows):
    return jnp.concatenate([value_rows.T, jnp.ones((16, value_rows.shape[0]), bf16)], axis=0)


def prep_kernel(
    info, pq, rq, pg, rg, recv, kv_own, kv_recv, q_aug, grads, raised, packed, local, sems
):
    core = info[0]
    cols = columns(core, Q_COLS)
    run_copies(
        [
            (pq.at[:, cols], local.at[0]),
            (rq.at[0, :, cols], local.at[1]),
            (pg.at[:, cols], local.at[2]),
            (rg.at[0, :, cols], local.at[3]),
        ],
        sems,
    )
    none = jnp.concatenate(
        [jnp.zeros((HEAD_DIM + 8, TILE), f32), jnp.full((8, TILE), no_max, f32)], axis=0
    )
    for j in range(4):
        lanes = slice(j * TILE, (j + 1) * TILE)
        sib, resp = j // 2, j % 2
        source = recv if sib else local
        turned_q = turned(source[resp])
        q_aug[:HEAD_DIM, lanes] = turned_q
        grads[:, lanes] = turned(source[2 + resp])
        if resp:
            q_aug[HEAD_DIM:, lanes] = jnp.zeros((HEAD_DIM, TILE), bf16)
            rows = (kv_recv if sib else kv_own)[TOKENS:BLOCK]
            scores = dot(rows[:, :HEAD_DIM], turned_q)
            token = iota(scores.shape, 1) % TOKENS
            scores = jnp.where(iota(scores.shape, 0) <= token, scores, blocked_score)
            part, info_rows = softmax_part(scores, with_ones(rows[:, HEAD_DIM:]))
            raised[:, sib * TILE : (sib + 1) * TILE] = part
            packed[:, lanes] = info_rows
        else:
            own_core = 1 - core if sib else core
            token = iota((HEAD_DIM, TILE), 1) % TOKENS + own_core * TOKENS
            row = iota((HEAD_DIM, TILE), 0)
            hidden = jnp.logical_or(row == 0, row > token)
            q_aug[HEAD_DIM:, lanes] = jnp.where(hidden, blocked_score, 0.0).astype(bf16)
            packed[:, lanes] = none


def prep(info, prompt_q, resp_q, prompt_grad, resp_grad, recv, kv_own, kv_recv):
    return pl.pallas_call(
        prep_kernel,
        in_specs=[pl.BlockSpec(memory_space=pltpu.SMEM)]
        + [pl.BlockSpec(memory_space=pltpu.HBM)] * 4
        + [pl.BlockSpec(memory_space=pltpu.VMEM)] * 3,
        out_shape=[
            jax.ShapeDtypeStruct((2 * HEAD_DIM, LANES), bf16),
            jax.ShapeDtypeStruct((HEAD_DIM, LANES), bf16),
            jax.ShapeDtypeStruct((TOKENS, 2 * TILE), bf16),
            jax.ShapeDtypeStruct((HEAD_DIM + 16, LANES), f32),
        ],
        scratch_shapes=[
            pltpu.VMEM((4, TOKENS, Q_COLS), bf16),
            pltpu.SemaphoreType.DMA((4,)),
        ],
        compiler_params=params(),
        name="prep",
    )(info, prompt_q, resp_q, prompt_grad, resp_grad, recv, kv_own, kv_recv)


def chunk_rows(kv, cols):
    return jnp.concatenate([kv[p * PIECE : p * PIECE + BLOCK, cols] for p in range(4)], axis=0)


key_cols = slice(0, HEAD_DIM)
value_cols = slice(HEAD_DIM, KV_COLS)


def forward_kernel(offset, info, kv, q_aug, raised, packed, notes, key_aug, value_rows):
    @pl.when(pl.program_id(0) == 0)
    def _():
        core, z_own, x_own = info[0], info[1], info[2]
        x_here = (x_own + offset) % 4
        row = iota((BLOCK, HEAD_DIM), 1)
        token = (iota((BLOCK, HEAD_DIM), 0) + core * TOKENS) % BLOCK
        first = (row == 0).astype(f32)
        same = jnp.logical_and(row == token, row > 0).astype(f32)
        for p in range(4):
            rows = slice(p * BLOCK, (p + 1) * BLOCK)
            z_here = (z_own + 4 - p) % 4
            later = jnp.logical_or(
                z_here > z_own, jnp.logical_and(z_here == z_own, x_here > x_own)
            )
            diagonal = jnp.logical_and(z_here == z_own, x_here == x_own)
            key_aug[rows, :HEAD_DIM] = kv[p * PIECE : p * PIECE + BLOCK, key_cols]
            notes[p * NOTE : (p + 1) * NOTE] = kv[p * PIECE + BLOCK : (p + 1) * PIECE]
            key_aug[rows, HEAD_DIM:] = (
                first * later.astype(f32) + same * diagonal.astype(f32)
            ).astype(bf16)
        value_rows[...] = with_ones(chunk_rows(kv, value_cols))

    for s in range(TILE // SUB):
        lanes = slice(s * SUB, (s + 1) * SUB)
        part, info_rows = softmax_part(dot(key_aug[...], q_aug[:, lanes]), value_rows[...])
        raised[:, lanes] = part
        packed[:, lanes] = info_rows


def forward(info, kv, q_aug, offset):
    return pl.pallas_call(
        functools.partial(forward_kernel, offset),
        grid_spec=pltpu.PrefetchScalarGridSpec(
            num_scalar_prefetch=1,
            grid=(4,),
            in_specs=[
                pl.BlockSpec((4 * PIECE, KV_COLS), lambda j, s: (0, 0)),
                pl.BlockSpec((2 * HEAD_DIM, TILE), lambda j, s: (0, j)),
            ],
            out_specs=[
                pl.BlockSpec((CHUNK, TILE), lambda j, s: (0, j)),
                pl.BlockSpec((HEAD_DIM + 16, TILE), lambda j, s: (0, j)),
                pl.BlockSpec((4 * NOTE, KV_COLS), lambda j, s: (0, 0)),
            ],
            scratch_shapes=[
                pltpu.VMEM((CHUNK, 2 * HEAD_DIM), bf16),
                pltpu.VMEM((HEAD_DIM + 16, CHUNK), bf16),
            ],
        ),
        out_shape=[
            jax.ShapeDtypeStruct((CHUNK, LANES), bf16),
            jax.ShapeDtypeStruct((HEAD_DIM + 16, LANES), f32),
            jax.ShapeDtypeStruct((4 * NOTE, KV_COLS), bf16),
        ],
        compiler_params=params(),
        cost_estimate=pl.CostEstimate(
            flops=4 * CHUNK * LANES * HEAD_DIM, bytes_accessed=5 * 2**20, transcendentals=0
        ),
        name="forward",
    )(info, kv, q_aug)


def combine_kernel(info, note_0, note_1, note_2, note_3, grads, part_0, part_1, part_2, part_3, part_own, out, cot_aug, gains):
    j = pl.program_id(0)
    parts = (part_0, part_1, part_2, part_3, part_own)
    tops = [part[HEAD_DIM + 8 : HEAD_DIM + 9, :] for part in parts]
    top = functools.reduce(jnp.maximum, tops)
    factors = [jnp.exp2((one - top) * exp2_scale) for one in tops]
    length = sum(f * part[HEAD_DIM : HEAD_DIM + 1, :] for f, part in zip(factors, parts))
    total = sum(f * part[:HEAD_DIM, :] for f, part in zip(factors, parts))
    inverse = 1.0 / length
    rounded = (total * inverse).astype(bf16)
    out[...] = rounded
    gains[...] = jnp.concatenate(
        [f * inverse for f in factors] + [jnp.zeros((3, TILE), f32)], axis=0
    )
    own_core = jnp.where(j < 2, info[0], 1 - info[0])
    own_row = note_0[0:1, :].astype(f32)
    lane = iota(own_row.shape, 1)

    def field(number):
        mask = lane == own_core * 8 + number
        return jnp.sum(jnp.where(mask, own_row, 0.0), axis=1, keepdims=True)

    ratio = field(0) + field(1) + field(2)
    partner, chosen, count = field(3), field(4), field(5)
    mate = jnp.zeros((1, 1), f32)
    row = iota((4 * NOTE, 1), 0)
    z_here = (info[1] + 4 - row // NOTE) % 4
    for offset, note in zip(offsets, (note_0, note_1, note_2, note_3)):
        seat = z_here * 8 + (info[2] + offset) % 4 * 2
        for side in range(2):
            lanes = [note[:, side * 8 + k : side * 8 + k + 1].astype(f32) for k in range(3)]
            found = jnp.logical_and(
                row % NOTE == 0, (seat + side).astype(f32) == partner
            )
            ratios = lanes[0] + lanes[1] + lanes[2]
            mate = mate + jnp.sum(jnp.where(found, ratios, 0.0), axis=0, keepdims=True)
    sign = 2.0 * chosen - 1.0
    pair_weight = sign * jax.nn.sigmoid(-pair_beta * (sign * (ratio - mate)))
    token = (iota((1, TILE), 1) % TOKENS).astype(f32)
    weight = jnp.where(token < count, pair_weight, 0.0)
    weight = jnp.where(j % 2 == 1, weight, 1.0)
    cot = (weight * grads[...].astype(f32)).astype(bf16)
    cot_aug[:HEAD_DIM] = cot
    row_dot = -jnp.sum(cot.astype(f32) * rounded.astype(f32), axis=0, keepdims=True)
    high = row_dot.astype(bf16).astype(f32)
    middle = (row_dot - high).astype(bf16).astype(f32)
    low = row_dot - high - middle
    row = iota((HEAD_DIM, TILE), 0)
    cot_aug[HEAD_DIM:] = jnp.where(
        row == 0, high, jnp.where(row == 1, middle, jnp.where(row == 2, low, 0.0))
    ).astype(bf16)


def combine(info, notes, grads, parts):
    def tile(rows):
        return pl.BlockSpec((rows, TILE), lambda j, s: (0, j))

    return pl.pallas_call(
        combine_kernel,
        grid_spec=pltpu.PrefetchScalarGridSpec(
            num_scalar_prefetch=1,
            grid=(4,),
            in_specs=[pl.BlockSpec((4 * NOTE, KV_COLS), lambda j, s: (0, 0))] * 4
            + [tile(HEAD_DIM)]
            + [tile(HEAD_DIM + 16)] * 5,
            out_specs=[tile(HEAD_DIM), tile(2 * HEAD_DIM), tile(8)],
        ),
        out_shape=[
            jax.ShapeDtypeStruct((HEAD_DIM, LANES), bf16),
            jax.ShapeDtypeStruct((2 * HEAD_DIM, LANES), bf16),
            jax.ShapeDtypeStruct((8, LANES), f32),
        ],
        compiler_params=params(),
        name="combine",
    )(info, *notes, grads, *parts)


offsets = (0, 3, 1, 2)


def value_aug_of(value_rows):
    column = iota(value_rows.shape, 1)
    return jnp.concatenate([value_rows, (column < 3).astype(f32).astype(bf16)], axis=1)


def backward_kernel(chunk, kv, raised, q_aug, cot_aug, gains, slopes, grad, value_aug, dkey, dvalue):
    j = pl.program_id(0)

    @pl.when(j == 0)
    def _():
        value_aug[...] = value_aug_of(chunk_rows(kv, value_cols))
        dkey[...] = jnp.zeros_like(dkey)
        dvalue[...] = jnp.zeros_like(dvalue)

    gain = gains[chunk : chunk + 1, :]
    scaled_q = (q_aug[...].astype(f32) * (gain * score_scale)).astype(bf16)
    scaled_cot = (cot_aug[:HEAD_DIM].astype(f32) * gain).astype(bf16)
    for s in range(TILE // SUB):
        lanes = slice(s * SUB, (s + 1) * SUB)
        moved = dot(value_aug[...], cot_aug[:, lanes])
        slopes[:, lanes] = (raised[:, lanes].astype(f32) * moved).astype(bf16)
    dkey[...] += dot(slopes[...], scaled_q, 1, 1)
    dvalue[...] += dot(raised[...], scaled_cot, 1, 1)

    @pl.when(j == 3)
    def _():
        grad[:, :HEAD_DIM] = dkey[...].astype(grad.dtype)
        grad[:, HEAD_DIM:] = dvalue[...].astype(grad.dtype)


def backward(kv, raised, q_aug, cot_aug, gains, chunk, kind):
    def tile(rows):
        return pl.BlockSpec((rows, TILE), lambda j: (0, j))

    return pl.pallas_call(
        functools.partial(backward_kernel, chunk),
        grid=(4,),
        in_specs=[
            pl.BlockSpec((4 * PIECE, KV_COLS), lambda j: (0, 0)),
            tile(CHUNK),
            tile(HEAD_DIM),
            tile(2 * HEAD_DIM),
            tile(8),
        ],
        out_specs=[tile(CHUNK), pl.BlockSpec((CHUNK, KV_COLS), lambda j: (0, 0))],
        scratch_shapes=[
            pltpu.VMEM((CHUNK, 2 * HEAD_DIM), bf16),
            pltpu.VMEM((CHUNK, HEAD_DIM), f32),
            pltpu.VMEM((CHUNK, HEAD_DIM), f32),
        ],
        out_shape=[
            jax.ShapeDtypeStruct((CHUNK, LANES), bf16),
            jax.ShapeDtypeStruct((CHUNK, KV_COLS), kind),
        ],
        compiler_params=params(),
        cost_estimate=pl.CostEstimate(
            flops=6 * CHUNK * LANES * HEAD_DIM, bytes_accessed=6 * 2**20, transcendentals=0
        ),
        name="backward",
    )(kv, raised, q_aug, cot_aug, gains)


def rows_of(turned_rows):
    rows = turned_rows.T
    return jnp.concatenate(
        [rows[g * TOKENS : (g + 1) * TOKENS] for g in range(GROUP)], axis=1
    )


def finish_kernel(
    kv_0, kv_1, kv_2, kv_3, slopes_0, slopes_1, slopes_2, slopes_3,
    kv_own, raised, q_aug, cot_aug, gains, out, after, result, own_grad, keys, total,
):
    j = pl.program_id(0)

    @pl.when(j == 0)
    def _():
        for chunk, kv in enumerate((kv_0, kv_1, kv_2, kv_3)):
            keys[:, chunk * CHUNK : (chunk + 1) * CHUNK] = chunk_rows(kv, key_cols).T

    acc = None
    for chunk, slopes in enumerate((slopes_0, slopes_1, slopes_2, slopes_3)):
        part = dot(keys[:, chunk * CHUNK : (chunk + 1) * CHUNK], slopes[...])
        part = part * (gains[chunk : chunk + 1, :] * score_scale)
        acc = part if acc is None else acc + part
    total[...] = acc

    @pl.when(j == 1)
    def _():
        gain = gains[4:5, :]
        rows = kv_own[TOKENS:BLOCK]
        moved = dot(value_aug_of(rows[:, HEAD_DIM:]), cot_aug[...])
        slopes = (raised[...].astype(f32) * moved).astype(bf16)
        total[...] += dot(rows[:, :HEAD_DIM].T, slopes) * (gain * score_scale)
        scaled_q = (q_aug[...].astype(f32) * (gain * score_scale)).astype(bf16)
        scaled_cot = (cot_aug[:HEAD_DIM].astype(f32) * gain).astype(bf16)
        own_grad[:, :HEAD_DIM] = dot(slopes, scaled_q, 1, 1).astype(bf16)
        own_grad[:, HEAD_DIM:] = dot(raised[...], scaled_cot, 1, 1).astype(bf16)

    result[0, 0] = rows_of(out[...].astype(f32)).astype(bf16)
    result[0, 1] = rows_of(total[...]).astype(bf16)


def finish(kvs, slopes, kv_own, raised, q_aug, cot_aug, gains, out, after, sib):
    def whole(*shape):
        return pl.BlockSpec(shape, lambda j: (0,) * len(shape))

    def tile(rows):
        return pl.BlockSpec((rows, TILE), lambda j: (0, 2 * sib + j))

    return pl.pallas_call(
        finish_kernel,
        grid=(2,),
        in_specs=[whole(4 * PIECE, KV_COLS)] * 4
        + [tile(CHUNK)] * 4
        + [
            whole(PIECE, KV_COLS),
            pl.BlockSpec((TOKENS, TILE), lambda j: (0, sib)),
            tile(HEAD_DIM),
            tile(2 * HEAD_DIM),
            tile(8),
            tile(HEAD_DIM),
            pl.BlockSpec(memory_space=pl.ANY),
        ],
        out_specs=[
            pl.BlockSpec((1, 2, TOKENS, Q_COLS), lambda j: (j, 0, 0, 0)),
            whole(TOKENS, KV_COLS),
        ],
        scratch_shapes=[
            pltpu.VMEM((HEAD_DIM, 4 * CHUNK), bf16),
            pltpu.VMEM((HEAD_DIM, TILE), f32),
        ],
        out_shape=[
            jax.ShapeDtypeStruct((2, 2, TOKENS, Q_COLS), bf16),
            jax.ShapeDtypeStruct((TOKENS, KV_COLS), bf16),
        ],
        compiler_params=params(),
        cost_estimate=pl.CostEstimate(
            flops=4 * CHUNK * LANES * HEAD_DIM, bytes_accessed=5 * 2**20, transcendentals=0
        ),
        name="finish",
    )(*kvs, *slopes, kv_own, raised, q_aug, cot_aug, gains, out, after)


def place_kernel(info, own, recv, own_dkv, recv_dkv, prompt_out, resp_out, prompt_dq, resp_dq, resp_dkv):
    def write(source, dkv):
        prompt_out[...] = source[0, 0]
        prompt_dq[...] = source[0, 1]
        resp_out[0] = source[1, 0]
        resp_dq[0] = source[1, 1]
        resp_dkv[0] = dkv[...]

    @pl.when(pl.program_id(0) == 0)
    def _():
        write(own, own_dkv)

    @pl.when(pl.program_id(0) == 1)
    def _():
        write(recv, recv_dkv)


def place(info, own, recv, own_dkv, recv_dkv):
    def whole(*shape):
        return pl.BlockSpec(shape, lambda i, s: (0,) * len(shape))

    def column(i, s):
        return s[0] + i - 2 * s[0] * i

    two = pl.BlockSpec((TOKENS, Q_COLS), lambda i, s: (0, column(i, s)))
    three = pl.BlockSpec((1, TOKENS, Q_COLS), lambda i, s: (0, 0, column(i, s)))
    prompt = jax.ShapeDtypeStruct((TOKENS, 2 * Q_COLS), bf16)
    resp = jax.ShapeDtypeStruct((1, TOKENS, 2 * Q_COLS), bf16)
    return pl.pallas_call(
        place_kernel,
        grid_spec=pltpu.PrefetchScalarGridSpec(
            num_scalar_prefetch=1,
            grid=(2,),
            in_specs=[whole(2, 2, TOKENS, Q_COLS)] * 2 + [whole(TOKENS, KV_COLS)] * 2,
            out_specs=[
                two,
                three,
                two,
                three,
                pl.BlockSpec((1, TOKENS, KV_COLS), lambda i, s: (0, 0, column(i, s))),
            ],
        ),
        out_shape=[
            prompt,
            resp,
            prompt,
            resp,
            jax.ShapeDtypeStruct((1, TOKENS, 2 * KV_COLS), bf16),
        ],
        compiler_params=params(),
        name="place",
    )(info, own, recv, own_dkv, recv_dkv)


def sum_x_kernel(own, recv_1, recv_2, recv_3, first, second, third, fourth):
    for p, out in enumerate((first, second, third, fourth)):
        rows = slice(p * BLOCK, (p + 1) * BLOCK)
        total = own[rows]
        for recv in (recv_1, recv_2, recv_3):
            total = total + recv[rows].astype(f32)
        out[...] = total.astype(out.dtype)


def sum_x(own, recvs):
    return pl.pallas_call(
        sum_x_kernel,
        out_shape=[
            jax.ShapeDtypeStruct((BLOCK, KV_COLS), f32 if p == 0 else bf16) for p in range(4)
        ],
        compiler_params=params(),
        name="sum_x",
    )(own, *recvs)


def sum_z_kernel(own, recv_1, recv_2, recv_3, after, kept, sent):
    total = own[...]
    for recv in (recv_1, recv_2, recv_3):
        total = total + recv[...].astype(f32)
    kept[...] = total[:TOKENS].astype(bf16)
    sent[...] = total[TOKENS:].astype(bf16)


def sum_z(own, recvs, after):
    return pl.pallas_call(
        sum_z_kernel,
        in_specs=[pl.BlockSpec(memory_space=pltpu.VMEM)] * 4
        + [pl.BlockSpec(memory_space=pl.ANY)],
        out_shape=[jax.ShapeDtypeStruct((TOKENS, KV_COLS), bf16)] * 2,
        compiler_params=params(),
        name="sum_z",
    )(own, *recvs, after)


def shards(
    prompt_q,
    prompt_kv,
    resp_q,
    resp_kv,
    prompt_grad,
    resp_grad,
    resp_len,
    logratio,
    partner,
    chosen,
):
    own_index = lax.axis_index("resp")
    core = own_index % 2
    info = jnp.stack([core, own_index // 8, own_index // 2 % 4]).astype(jnp.int32)

    prompt_q, prompt_kv, resp_q, resp_kv, prompt_grad, resp_grad = [
        pltpu.with_memory_space_constraint(array, pltpu.HBM)
        for array in (prompt_q, prompt_kv, resp_q, resp_kv, prompt_grad, resp_grad)
    ]
    facts = jnp.concatenate(
        [logratio, partner.astype(f32), chosen.astype(f32), resp_len.astype(f32)]
    )

    kv_own, kv_send = pack_kv(info, facts, prompt_kv, resp_kv)
    kv_recv = swap_core(kv_send)
    q_recv = swap_core(pack_q(info, prompt_q, resp_q, prompt_grad, resp_grad))

    block = jnp.concatenate(
        [kv_own[:TOKENS], kv_recv[:TOKENS], kv_own[BLOCK:] + kv_recv[BLOCK:]], axis=0
    )
    chunk_own = jnp.concatenate([block] + [shift_z(block, step) for step in (1, 2, 3)], axis=0)
    kvs = [chunk_own] + [shift_x(chunk_own, 4 - offset) for offset in offsets[1:]]

    q_aug, grads, raised_own, part_own = prep(
        info, prompt_q, resp_q, prompt_grad, resp_grad, q_recv, kv_own, kv_recv
    )
    raised, parts, notes = [], [], []
    for kv, offset in zip(kvs, offsets):
        one, part, note = forward(info, kv, q_aug, offset)
        raised.append(one)
        parts.append(part)
        notes.append(note)
    out, cot_aug, gains = combine(info, notes, grads, parts + [part_own])

    slopes = [None] * 4
    returned = []
    for chunk in (3, 2, 1, 0):
        kind = bf16 if chunk else f32
        slopes[chunk], grad = backward(
            kvs[chunk], raised[chunk], q_aug, cot_aug, gains, chunk, kind
        )
        returned.append(shift_x(grad, offsets[chunk]) if chunk else grad)

    blocks = sum_x(returned[3], returned[:3])
    recvs = [shift_z(blocks[p], 4 - p) for p in (1, 2, 3)]

    sib_result, sib_dkv = finish(
        kvs, slopes, kv_recv, raised_own, q_aug, cot_aug, gains, out, blocks[3], 1
    )
    recv_result = swap_core(sib_result)
    recv_dkv = swap_core(sib_dkv)
    own_result, own_dkv = finish(
        kvs, slopes, kv_own, raised_own, q_aug, cot_aug, gains, out, sib_dkv, 0
    )
    prompt_out, resp_out, prompt_dq, resp_dq, resp_dkv = place(
        info, own_result, recv_result, own_dkv, recv_dkv
    )

    kept, sent = sum_z(blocks[0], recvs, own_dkv)
    other = swap_core(sent)
    prompt_dkv = jnp.where(
        core == 0,
        jnp.concatenate([kept, other], axis=1),
        jnp.concatenate([other, kept], axis=1),
    )
    return (prompt_out, resp_out, prompt_dq, resp_dq, prompt_dkv, resp_dkv)


def solution(mesh):
    return jax.shard_map(
        shards,
        mesh=mesh,
        in_specs=(
            P(("batch", "resp"), "head"),
            P(("batch", "resp"), "head"),
            P(("batch", "resp"), None, "head"),
            P(("batch", "resp"), None, "head"),
            P(("batch", "resp"), "head"),
            P(("batch", "resp"), None, "head"),
            P(("batch", "resp")),
            P(("batch", "resp")),
            P(("batch", "resp")),
            P(("batch", "resp")),
        ),
        out_specs=(
            P(("batch", "resp"), "head"),
            P(("batch", "resp"), None, "head"),
            P(("batch", "resp"), "head"),
            P(("batch", "resp"), None, "head"),
            P(("batch", "resp"), "head"),
            P(("batch", "resp"), None, "head"),
        ),
        check_vma=False,
    )
```

```python
import functools

import jax
import jax.numpy as jnp
from jax import lax
from jax.experimental import pallas as pl
from jax.experimental.pallas import tpu as pltpu
from jax.sharding import PartitionSpec as P

HEAD_DIM = 128
GROUP = 8
TOKENS = 64
KV_COLS = 2 * HEAD_DIM
Q_COLS = GROUP * HEAD_DIM
BLOCK = 2 * TOKENS
NOTE = 16
PIECE = BLOCK + NOTE
CHUNK = 4 * BLOCK
TILE = GROUP * TOKENS
LANES = 4 * TILE
SUBS = LANES // TILE

score_scale = HEAD_DIM ** (-0.5)
exp2_scale = score_scale * 1.4426950408889634
pair_beta = 0.1
blocked_score = -(2.0**30)
no_max = -(2.0**31)

bf16 = jnp.bfloat16
f32 = jnp.float32


def params(**kw):
    return pltpu.CompilerParams(vmem_limit_bytes=16 * 2**20, **kw)


def dot(left, right, left_dim=1, right_dim=0):
    return lax.dot_general(
        left, right, (((left_dim,), (right_dim,)), ((), ())), preferred_element_type=f32
    )


def iota(shape, dim):
    return lax.broadcasted_iota(jnp.int32, shape, dim)


VMEM = pl.BlockSpec(memory_space=pltpu.VMEM)
SMEM = pl.BlockSpec(memory_space=pltpu.SMEM)
HBM = pl.BlockSpec(memory_space=pltpu.HBM)
AFTER = pl.BlockSpec(memory_space=pl.ANY)


def shape(*dims, dtype=bf16):
    return jax.ShapeDtypeStruct(dims, dtype)


def call(kernel, name, in_specs, out_shape, scratch=(), out_specs=None, flops=0):
    extra = {} if out_specs is None else {"out_specs": out_specs}
    cost = pl.CostEstimate(flops=flops, bytes_accessed=2**20, transcendentals=0)
    return pl.pallas_call(
        kernel,
        in_specs=in_specs,
        out_shape=out_shape,
        scratch_shapes=list(scratch),
        compiler_params=params(),
        cost_estimate=cost,
        name=name,
        **extra,
    )


def lanes_of(j):
    return slice(j * TILE, (j + 1) * TILE)


def swap_core(value):
    return lax.ppermute(value, "resp", [(r, r ^ 1) for r in range(32)])


def shift_z(value, step):
    pairs = [(r, ((r // 8 + step) % 4) * 8 + r % 8) for r in range(32)]
    return lax.ppermute(value, "resp", pairs)


def shift_x(value, step):
    pairs = [(r, (r // 8) * 8 + (r % 8 // 2 + step) % 4 * 2 + r % 2) for r in range(32)]
    return lax.ppermute(value, "resp", pairs)


def columns(core, width):
    return pl.ds(pl.multiple_of(core * width, width), width)


def run_copies(pairs, sems):
    copies = [pltpu.make_async_copy(a, b, sems.at[i]) for i, (a, b) in enumerate(pairs)]
    for copy in copies:
        copy.start()
    for copy in copies:
        copy.wait()


def columns(core, width):
    return pl.ds(pl.multiple_of(core * width, width), width)


def started(pairs, sems):
    copies = [pltpu.make_async_copy(a, b, sems.at[i]) for i, (a, b) in enumerate(pairs)]
    for copy in copies:
        copy.start()
    return copies


def waited(copies):
    for copy in copies:
        copy.wait()


def half_copies(side, pq, rq, pg, rg, target):
    cols = columns(side, Q_COLS)
    return [
        (pq.at[:, cols], target.at[0]),
        (rq.at[0, :, cols], target.at[1]),
        (pg.at[:, cols], target.at[2]),
        (rg.at[0, :, cols], target.at[3]),
    ]


def pack_kernel(
    info, logratio, partner, chosen, resp_len, prompt_kv, resp_kv, pq, rq, pg, rg,
    own, send, send_q, sems,
):
    core = info[0]
    pairs = []
    for side, out in ((core, own), (1 - core, send)):
        cols = columns(side, KV_COLS)
        pairs.append((prompt_kv.at[:, cols], out.at[pl.ds(0, TOKENS)]))
        pairs.append((resp_kv.at[0, :, cols], out.at[pl.ds(TOKENS, TOKENS)]))
    pairs += half_copies(1 - core, pq, rq, pg, rg, send_q)
    copies = started(pairs, sems)
    row, lane = iota((NOTE, KV_COLS), 0), iota((NOTE, KV_COLS), 1)
    ratio = jnp.full((NOTE, KV_COLS), logratio[0], f32)
    high = ratio.astype(bf16).astype(f32)
    middle = (ratio - high).astype(bf16).astype(f32)
    low = ratio - high - middle
    note = jnp.zeros((NOTE, KV_COLS), f32)
    fields = (
        high,
        middle,
        low,
        partner[0].astype(f32),
        chosen[0].astype(f32),
        resp_len[0].astype(f32),
    )
    for number, value in enumerate(fields):
        note = jnp.where(lane == core * 8 + number, value, note)
    note = jnp.where(row == 0, note, 0.0).astype(bf16)
    own[BLOCK:] = note
    send[BLOCK:] = note
    waited(copies)


def pack(*operands):
    return call(
        pack_kernel,
        "pack",
        [SMEM] * 5 + [HBM] * 6,
        [shape(PIECE, KV_COLS)] * 2 + [shape(4, TOKENS, Q_COLS)],
        [pltpu.SemaphoreType.DMA((8,))],
    )(*operands)


def join_cores_kernel(own, recv, block):
    block[:TOKENS] = own[:TOKENS]
    block[TOKENS:BLOCK] = recv[:TOKENS]
    block[BLOCK:] = own[BLOCK:] + recv[BLOCK:]


def join_cores(own, recv):
    return call(join_cores_kernel, "join_cores", [VMEM] * 2, shape(PIECE, KV_COLS))(own, recv)


def join_z_kernel(piece_0, piece_1, piece_2, piece_3, after, chunk):
    for p, piece in enumerate((piece_0, piece_1, piece_2, piece_3)):
        chunk[p * PIECE : (p + 1) * PIECE] = piece[...]


def join_z(pieces, after):
    return call(join_z_kernel, "join_z", [VMEM] * 4 + [AFTER], shape(4 * PIECE, KV_COLS))(
        *pieces, after
    )


def turned(block):
    rows = jnp.concatenate(
        [block[:, g * HEAD_DIM : (g + 1) * HEAD_DIM] for g in range(GROUP)], axis=0
    )
    return rows.T


def softmax_part(scores, value_rows):
    top = jnp.max(scores, axis=0, keepdims=True)
    raised = jnp.exp2((scores - top) * exp2_scale).astype(bf16)
    total = dot(value_rows, raised)
    packed = jnp.concatenate(
        [total[: HEAD_DIM + 8], jnp.broadcast_to(top, (8, top.shape[1]))], axis=0
    )
    return raised, packed


def with_ones(value_rows):
    return jnp.concatenate([value_rows.T, jnp.ones((16, value_rows.shape[0]), bf16)], axis=0)


def prep_kernel(
    info, pq, rq, pg, rg, recv, kv_own, kv_recv, q_aug, grads, raised, packed, local, sems
):
    core = info[0]
    copies = started(half_copies(core, pq, rq, pg, rg, local), sems)
    none = jnp.concatenate(
        [jnp.zeros((HEAD_DIM + 8, TILE), f32), jnp.full((8, TILE), no_max, f32)], axis=0
    )
    for j in (2, 3, 0, 1):
        lanes = lanes_of(j)
        sib, resp = j // 2, j % 2
        if j == 0:
            waited(copies)
        source = recv if sib else local
        turned_q = turned(source[resp])
        q_aug[:HEAD_DIM, lanes] = turned_q
        grads[:, lanes] = turned(source[2 + resp])
        if resp:
            q_aug[HEAD_DIM:, lanes] = jnp.zeros((HEAD_DIM, TILE), bf16)
            rows = (kv_recv if sib else kv_own)[TOKENS:BLOCK]
            scores = dot(rows[:, :HEAD_DIM], turned_q)
            token = iota(scores.shape, 1) % TOKENS
            scores = jnp.where(iota(scores.shape, 0) <= token, scores, blocked_score)
            part, info_rows = softmax_part(scores, with_ones(rows[:, HEAD_DIM:]))
            raised[:, lanes_of(sib)] = part
            packed[:, lanes] = info_rows
        else:
            own_core = 1 - core if sib else core
            token = iota((HEAD_DIM, TILE), 1) % TOKENS + own_core * TOKENS
            row = iota((HEAD_DIM, TILE), 0)
            hidden = jnp.logical_or(row == 0, row > token)
            q_aug[HEAD_DIM:, lanes] = jnp.where(hidden, blocked_score, 0.0).astype(bf16)
            packed[:, lanes] = none


def prep(info, prompt_q, resp_q, prompt_grad, resp_grad, recv, kv_own, kv_recv):
    return call(
        prep_kernel,
        "prep",
        [SMEM] + [HBM] * 4 + [VMEM] * 3,
        [
            shape(2 * HEAD_DIM, LANES),
            shape(HEAD_DIM, LANES),
            shape(TOKENS, 2 * TILE),
            shape(HEAD_DIM + 16, LANES, dtype=f32),
        ],
        [pltpu.VMEM((4, TOKENS, Q_COLS), bf16), pltpu.SemaphoreType.DMA((4,))],
    )(info, prompt_q, resp_q, prompt_grad, resp_grad, recv, kv_own, kv_recv)


offsets = (0, 3, 1, 2)
key_cols = slice(0, HEAD_DIM)
value_cols = slice(HEAD_DIM, KV_COLS)


def chunk_rows(kv, cols):
    return jnp.concatenate([kv[p * PIECE : p * PIECE + BLOCK, cols] for p in range(4)], axis=0)


def forward_kernel(offset, info, kv, q_aug, raised, packed, notes, key_aug, value_rows, scores):
    core, z_own, x_own = info[0], info[1], info[2]
    x_here = (x_own + offset) % 4
    row = iota((BLOCK, HEAD_DIM), 1)
    token = (iota((BLOCK, HEAD_DIM), 0) + core * TOKENS) % BLOCK
    first = (row == 0).astype(f32)
    same = jnp.logical_and(row == token, row > 0).astype(f32)
    for p in range(4):
        rows = slice(p * BLOCK, (p + 1) * BLOCK)
        z_here = (z_own + 4 - p) % 4
        later = jnp.logical_or(
            z_here > z_own, jnp.logical_and(z_here == z_own, x_here > x_own)
        )
        diagonal = jnp.logical_and(z_here == z_own, x_here == x_own)
        key_aug[rows, :HEAD_DIM] = kv[p * PIECE : p * PIECE + BLOCK, key_cols]
        notes[p * NOTE : (p + 1) * NOTE] = kv[p * PIECE + BLOCK : (p + 1) * PIECE]
        key_aug[rows, HEAD_DIM:] = (
            first * later.astype(f32) + same * diagonal.astype(f32)
        ).astype(bf16)
    value_rows[...] = with_ones(chunk_rows(kv, value_cols))
    scores[0] = dot(key_aug[...], q_aug[:, lanes_of(0)])
    for j in range(SUBS):
        if j + 1 < SUBS:
            scores[(j + 1) % 2] = dot(key_aug[...], q_aug[:, lanes_of(j + 1)])
        part, info_rows = softmax_part(scores[j % 2], value_rows[...])
        raised[:, lanes_of(j)] = part
        packed[:, lanes_of(j)] = info_rows


def forward(info, kv, q_aug, offset):
    return call(
        functools.partial(forward_kernel, offset),
        "forward",
        [SMEM] + [VMEM] * 2,
        [
            shape(CHUNK, LANES),
            shape(HEAD_DIM + 16, LANES, dtype=f32),
            shape(4 * NOTE, KV_COLS),
        ],
        [
            pltpu.VMEM((CHUNK, 2 * HEAD_DIM), bf16),
            pltpu.VMEM((HEAD_DIM + 16, CHUNK), bf16),
            pltpu.VMEM((2, CHUNK, TILE), f32),
        ],
        flops=4 * CHUNK * LANES * HEAD_DIM,
    )(info, kv, q_aug)


def combine_kernel(
    info, note_0, note_1, note_2, note_3, grads, part_0, part_1, part_2, part_3, part_own,
    out, cot_aug, gains,
):
    notes = (note_0, note_1, note_2, note_3)
    weights = []
    for sib in range(2):
        own_core = 1 - info[0] if sib else info[0]
        own_row = note_0[0:1, :].astype(f32)
        lane = iota(own_row.shape, 1)

        def field(number):
            mask = lane == own_core * 8 + number
            return jnp.sum(jnp.where(mask, own_row, 0.0), axis=1, keepdims=True)

        ratio = field(0) + field(1) + field(2)
        partner, chosen, count = field(3), field(4), field(5)
        mate = jnp.zeros((1, 1), f32)
        row = iota((4 * NOTE, 1), 0)
        z_here = (info[1] + 4 - row // NOTE) % 4
        for offset, note in zip(offsets, notes):
            seat = z_here * 8 + (info[2] + offset) % 4 * 2
            for side in range(2):
                lanes = [note[:, side * 8 + k : side * 8 + k + 1].astype(f32) for k in range(3)]
                found = jnp.logical_and(
                    row % NOTE == 0, (seat + side).astype(f32) == partner
                )
                ratios = lanes[0] + lanes[1] + lanes[2]
                mate = mate + jnp.sum(jnp.where(found, ratios, 0.0), axis=0, keepdims=True)
        sign = 2.0 * chosen - 1.0
        pair_weight = sign * jax.nn.sigmoid(-pair_beta * (sign * (ratio - mate)))
        token = (iota((1, TILE), 1) % TOKENS).astype(f32)
        weights.append(jnp.where(token < count, pair_weight, 0.0))

    for j in range(SUBS):
        lanes = lanes_of(j)
        parts = (part_0, part_1, part_2, part_3) + ((part_own,) if j % 2 else ())
        tops = [part[HEAD_DIM + 8 : HEAD_DIM + 9, lanes] for part in parts]
        top = functools.reduce(jnp.maximum, tops)
        factors = [jnp.exp2((one - top) * exp2_scale) for one in tops]
        length = sum(f * part[HEAD_DIM : HEAD_DIM + 1, lanes] for f, part in zip(factors, parts))
        inverse = 1.0 / length
        factors = [f * inverse for f in factors]
        rounded = sum(f * part[:HEAD_DIM, lanes] for f, part in zip(factors, parts)).astype(bf16)
        out[:, lanes] = rounded
        gains[:, lanes] = jnp.concatenate(
            factors + [jnp.zeros((8 - len(factors), TILE), f32)], axis=0
        )
        if j % 2:
            cot = (weights[j // 2] * grads[:, lanes].astype(f32)).astype(bf16)
        else:
            cot = grads[:, lanes]
        cot_aug[:HEAD_DIM, lanes] = cot
        row_dot = -jnp.sum(cot.astype(f32) * rounded.astype(f32), axis=0, keepdims=True)
        high = row_dot.astype(bf16).astype(f32)
        middle = (row_dot - high).astype(bf16).astype(f32)
        low = row_dot - high - middle
        row = iota((16, TILE), 0)
        split = jnp.where(
            row == 0, high, jnp.where(row == 1, middle, jnp.where(row == 2, low, 0.0))
        )
        cot_aug[HEAD_DIM : HEAD_DIM + 16, lanes] = split.astype(bf16)
        cot_aug[HEAD_DIM + 16 :, lanes] = jnp.zeros((HEAD_DIM - 16, TILE), bf16)


def combine(info, notes, grads, parts):
    return call(
        combine_kernel,
        "combine",
        [SMEM] + [VMEM] * 10,
        [shape(HEAD_DIM, LANES), shape(2 * HEAD_DIM, LANES), shape(8, LANES, dtype=f32)],
    )(info, *notes, grads, *parts)


def value_aug_of(value_rows):
    column = iota(value_rows.shape, 1)
    return jnp.concatenate([value_rows, (column < 3).astype(f32).astype(bf16)], axis=1)


def backward_kernel(
    chunk, kv, raised, q_aug, cot_aug, gains, slopes, grad, value_aug, moved, scaled_q, scaled_cot
):
    value_aug[...] = value_aug_of(chunk_rows(kv, value_cols))
    moved[0] = dot(value_aug[...], cot_aug[:, lanes_of(0)])
    for j in range(SUBS):
        lanes = lanes_of(j)
        if j + 1 < SUBS:
            moved[(j + 1) % 2] = dot(value_aug[...], cot_aug[:, lanes_of(j + 1)])
        gain = gains[chunk : chunk + 1, lanes]
        scaled_cot[:, lanes] = (cot_aug[:HEAD_DIM, lanes].astype(f32) * gain).astype(bf16)
        scaled_q[:, lanes] = (
            q_aug[:HEAD_DIM, lanes].astype(f32) * (gain * score_scale)
        ).astype(bf16)
        slopes[:, lanes] = (raised[:, lanes].astype(f32) * moved[j % 2]).astype(bf16)
    grad[:, HEAD_DIM:] = dot(raised[...], scaled_cot[...], 1, 1).astype(grad.dtype)
    grad[:, :HEAD_DIM] = dot(slopes[...], scaled_q[...], 1, 1).astype(grad.dtype)


def backward(kv, raised, q_aug, cot_aug, gains, chunk, kind):
    return call(
        functools.partial(backward_kernel, chunk),
        "backward",
        [VMEM] * 5,
        [shape(CHUNK, LANES), shape(CHUNK, KV_COLS, dtype=kind)],
        [
            pltpu.VMEM((CHUNK, 2 * HEAD_DIM), bf16),
            pltpu.VMEM((2, CHUNK, TILE), f32),
            pltpu.VMEM((HEAD_DIM, LANES), bf16),
            pltpu.VMEM((HEAD_DIM, LANES), bf16),
        ],
        flops=6 * CHUNK * LANES * HEAD_DIM,
    )(kv, raised, q_aug, cot_aug, gains)


def rows_of(turned_rows):
    rows = turned_rows.T
    return jnp.concatenate(
        [rows[g * TOKENS : (g + 1) * TOKENS] for g in range(GROUP)], axis=1
    )


def finish_kernel(
    kv_0, kv_1, kv_2, kv_3, slopes_0, slopes_1, slopes_2, slopes_3,
    kv_own, kv_recv, raised, q_aug, cot_aug, gains, out,
    own_result, sib_result, own_grad, sib_grad, keys,
):
    for chunk, kv in enumerate((kv_0, kv_1, kv_2, kv_3)):
        keys[:, chunk * CHUNK : (chunk + 1) * CHUNK] = chunk_rows(kv, key_cols).T
    for j in (2, 3, 0, 1):
        lanes = lanes_of(j)
        sib, resp = j // 2, j % 2
        result = sib_result if sib else own_result
        total = None
        for chunk, slopes in enumerate((slopes_0, slopes_1, slopes_2, slopes_3)):
            part = dot(keys[:, chunk * CHUNK : (chunk + 1) * CHUNK], slopes[:, lanes])
            part = part * (gains[chunk : chunk + 1, lanes] * score_scale)
            total = part if total is None else total + part
        if resp:
            gain = gains[4:5, lanes]
            rows = (kv_recv if sib else kv_own)[TOKENS:BLOCK]
            own_raised = raised[:, lanes_of(sib)]
            grad = sib_grad if sib else own_grad
            moved = dot(value_aug_of(rows[:, HEAD_DIM:]), cot_aug[:, lanes])
            own_slopes = (own_raised.astype(f32) * moved).astype(bf16)
            total = total + dot(rows[:, :HEAD_DIM].T, own_slopes) * (gain * score_scale)
            scaled_q = (q_aug[:HEAD_DIM, lanes].astype(f32) * (gain * score_scale)).astype(bf16)
            scaled_cot = (cot_aug[:HEAD_DIM, lanes].astype(f32) * gain).astype(bf16)
            grad[:, :HEAD_DIM] = dot(own_slopes, scaled_q, 1, 1).astype(bf16)
            grad[:, HEAD_DIM:] = dot(own_raised, scaled_cot, 1, 1).astype(bf16)
        result[resp] = rows_of(out[:, lanes].astype(f32)).astype(bf16)
        result[2 + resp] = rows_of(total).astype(bf16)


def finish(kvs, slopes, kv_own, kv_recv, raised, q_aug, cot_aug, gains, out):
    return call(
        finish_kernel,
        "finish",
        [VMEM] * 15,
        [shape(4, TOKENS, Q_COLS)] * 2 + [shape(TOKENS, KV_COLS)] * 2,
        [pltpu.VMEM((HEAD_DIM, 4 * CHUNK), bf16)],
        flops=6 * CHUNK * LANES * HEAD_DIM,
    )(*kvs, *slopes, kv_own, kv_recv, raised, q_aug, cot_aug, gains, out)


def gate_kernel(result, grad, after, result_out, grad_out):
    result_out[...] = result[...]
    grad_out[...] = grad[...]


def gate(result, grad, after):
    return call(
        gate_kernel,
        "gate",
        [VMEM] * 2 + [AFTER],
        [shape(4, TOKENS, Q_COLS), shape(TOKENS, KV_COLS)],
    )(result, grad, after)


def place_kernel(
    info, own, recv, own_grad, recv_grad, prompt_out, resp_out, prompt_dq, resp_dq, resp_dkv, done, sems
):
    pairs = []
    for side, source, grad in ((info[0], own, own_grad), (1 - info[0], recv, recv_grad)):
        pairs += [
            (b, a) for a, b in half_copies(side, prompt_out, resp_out, prompt_dq, resp_dq, source)
        ]
        pairs.append((grad, resp_dkv.at[0, :, columns(side, KV_COLS)]))
    copies = started(pairs, sems)
    done[...] = jnp.zeros_like(done)
    waited(copies)


def place(info, own, recv, own_grad, recv_grad):
    prompt = shape(TOKENS, 2 * Q_COLS)
    resp = shape(1, TOKENS, 2 * Q_COLS)
    return call(
        place_kernel,
        "place",
        [SMEM] + [VMEM] * 4,
        [prompt, resp, prompt, resp, shape(1, TOKENS, 2 * KV_COLS), shape(8, 128, dtype=f32)],
        [pltpu.SemaphoreType.DMA((10,))],
        out_specs=[HBM] * 5 + [VMEM],
    )(info, own, recv, own_grad, recv_grad)


def sum_x_kernel(own, recv_1, recv_2, recv_3, after, kept, sent):
    for p in range(4):
        rows = slice(p * BLOCK, (p + 1) * BLOCK)
        total = own[rows]
        for recv in (recv_1, recv_2, recv_3):
            total = total + recv[rows].astype(f32)
        kept[p * TOKENS : (p + 1) * TOKENS] = total[:TOKENS]
        sent[p * TOKENS : (p + 1) * TOKENS] = total[TOKENS:].astype(bf16)


def sum_x(own, recvs, after):
    return call(
        sum_x_kernel,
        "sum_x",
        [VMEM] * 4 + [AFTER],
        [shape(4 * TOKENS, KV_COLS, dtype=f32), shape(4 * TOKENS, KV_COLS)],
    )(own, *recvs, after)


def mix_kernel(kept, recv, first, second, third, fourth):
    for p, out in enumerate((first, second, third, fourth)):
        rows = slice(p * TOKENS, (p + 1) * TOKENS)
        out[:, :KV_COLS] = kept[rows].astype(out.dtype)
        out[:, KV_COLS:] = recv[rows].astype(out.dtype)


def mix(kept, recv):
    return call(
        mix_kernel,
        "mix",
        [VMEM] * 2,
        [shape(TOKENS, 2 * KV_COLS, dtype=bf16 if p else f32) for p in range(4)],
    )(kept, recv)


def sum_z_kernel(info, own, recv_1, recv_2, recv_3, after, out):
    total = own[...]
    for recv in (recv_1, recv_2, recv_3):
        total = total + recv[...].astype(f32)
    total = total.astype(bf16)
    core = info[0]

    @pl.when(core == 0)
    def _():
        out[...] = total

    @pl.when(core == 1)
    def _():
        out[:, :KV_COLS] = total[:, KV_COLS:]
        out[:, KV_COLS:] = total[:, :KV_COLS]


def sum_z(info, own, recvs, after):
    return call(
        sum_z_kernel,
        "sum_z",
        [SMEM] + [VMEM] * 4 + [AFTER],
        shape(TOKENS, 2 * KV_COLS),
    )(info, own, *recvs, after)


def shards(
    prompt_q,
    prompt_kv,
    resp_q,
    resp_kv,
    prompt_grad,
    resp_grad,
    resp_len,
    logratio,
    partner,
    chosen,
):
    own_index = lax.axis_index("resp")
    core = own_index % 2
    info = jnp.stack([core, own_index // 8, own_index // 2 % 4]).astype(jnp.int32)
    prompt_q, prompt_kv, resp_q, resp_kv, prompt_grad, resp_grad = [
        pltpu.with_memory_space_constraint(array, pltpu.HBM)
        for array in (prompt_q, prompt_kv, resp_q, resp_kv, prompt_grad, resp_grad)
    ]

    kv_own, kv_send, q_send = pack(
        info,
        logratio,
        partner,
        chosen,
        resp_len,
        prompt_kv,
        resp_kv,
        prompt_q,
        resp_q,
        prompt_grad,
        resp_grad,
    )
    kv_recv = swap_core(kv_send)
    q_recv = swap_core(q_send)
    block = join_cores(kv_own, kv_recv)
    pieces = [block] + [shift_z(block, step) for step in (1, 2, 3)]
    q_aug, grads, raised_own, part_own = prep(
        info, prompt_q, resp_q, prompt_grad, resp_grad, q_recv, kv_own, kv_recv
    )
    chunk_own = join_z(pieces, part_own)
    kvs = [chunk_own] + [shift_x(chunk_own, 4 - offset) for offset in offsets[1:]]

    raised, parts, notes = [], [], []
    for kv, offset in zip(kvs, offsets):
        one, part, note = forward(info, kv, q_aug, offset)
        raised.append(one)
        parts.append(part)
        notes.append(note)
    out, cot_aug, gains = combine(info, notes, grads, parts + [part_own])

    slopes = [None] * 4
    returned = []
    for chunk in (3, 2, 1, 0):
        kind = bf16 if chunk else f32
        slopes[chunk], grad = backward(
            kvs[chunk], raised[chunk], q_aug, cot_aug, gains, chunk, kind
        )
        returned.append(shift_x(grad, offsets[chunk]) if chunk else grad)

    own_result, sib_result, own_grad, sib_grad = finish(
        kvs, slopes, kv_own, kv_recv, raised_own, q_aug, cot_aug, gains, out
    )
    kept, sent = sum_x(returned[3], returned[:3], own_grad)
    recv_sent = swap_core(sent)
    blocks = mix(kept, recv_sent)
    sib_result, sib_grad = gate(sib_result, sib_grad, blocks[3])
    recv_result = swap_core(sib_result)
    recv_grad = swap_core(sib_grad)
    recvs = [shift_z(blocks[p], 4 - p) for p in (1, 2, 3)]
    prompt_out, resp_out, prompt_dq, resp_dq, resp_dkv, placed = place(
        info, own_result, recv_result, own_grad, recv_grad
    )
    prompt_dkv = sum_z(info, blocks[0], recvs, placed)
    return (prompt_out, resp_out, prompt_dq, resp_dq, prompt_dkv, resp_dkv)


def solution(mesh):
    return jax.shard_map(
        shards,
        mesh=mesh,
        in_specs=(
            P(("batch", "resp"), "head"),
            P(("batch", "resp"), "head"),
            P(("batch", "resp"), None, "head"),
            P(("batch", "resp"), None, "head"),
            P(("batch", "resp"), "head"),
            P(("batch", "resp"), None, "head"),
            P(("batch", "resp")),
            P(("batch", "resp")),
            P(("batch", "resp")),
            P(("batch", "resp")),
        ),
        out_specs=(
            P(("batch", "resp"), "head"),
            P(("batch", "resp"), None, "head"),
            P(("batch", "resp"), "head"),
            P(("batch", "resp"), None, "head"),
            P(("batch", "resp"), "head"),
            P(("batch", "resp"), None, "head"),
        ),
        check_vma=False,
    )
```

```python
import functools

import jax
import jax.numpy as jnp
from jax import lax
from jax.experimental import pallas as pl
from jax.experimental.pallas import tpu as pltpu
from jax.sharding import PartitionSpec as P

HEAD_DIM = 128
GROUP = 8
TOKENS = 64
KV_COLS = 2 * HEAD_DIM
Q_COLS = GROUP * HEAD_DIM
BLOCK = 2 * TOKENS
NOTE = 16
PIECE = BLOCK + NOTE
TILE = GROUP * TOKENS
LANES = 4 * TILE
SUBS = LANES // TILE

score_scale = HEAD_DIM ** (-0.5)
exp2_scale = score_scale * 1.4426950408889634
pair_beta = 0.1
blocked_score = -(2.0**30)
no_max = -(2.0**31)

bf16 = jnp.bfloat16
f32 = jnp.float32


def params(**kw):
    return pltpu.CompilerParams(vmem_limit_bytes=16 * 2**20, **kw)


def dot(left, right, left_dim=1, right_dim=0):
    return lax.dot_general(
        left, right, (((left_dim,), (right_dim,)), ((), ())), preferred_element_type=f32
    )


def iota(shape, dim):
    return lax.broadcasted_iota(jnp.int32, shape, dim)


VMEM = pl.BlockSpec(memory_space=pltpu.VMEM)
SMEM = pl.BlockSpec(memory_space=pltpu.SMEM)
HBM = pl.BlockSpec(memory_space=pltpu.HBM)
AFTER = pl.BlockSpec(memory_space=pl.ANY)


def shape(*dims, dtype=bf16):
    return jax.ShapeDtypeStruct(dims, dtype)


def call(kernel, name, in_specs, out_shape, scratch=(), out_specs=None, flops=0):
    extra = {} if out_specs is None else {"out_specs": out_specs}
    cost = pl.CostEstimate(flops=flops, bytes_accessed=2**20, transcendentals=0)
    return pl.pallas_call(
        kernel,
        in_specs=in_specs,
        out_shape=out_shape,
        scratch_shapes=list(scratch),
        compiler_params=params(),
        cost_estimate=cost,
        name=name,
        **extra,
    )


def lanes_of(j):
    return slice(j * TILE, (j + 1) * TILE)


def swap_core(value):
    return lax.ppermute(value, "resp", [(r, r ^ 1) for r in range(32)])


def shift_z(value, step):
    pairs = [(r, ((r // 8 + step) % 4) * 8 + r % 8) for r in range(32)]
    return lax.ppermute(value, "resp", pairs)


def shift_x(value, step):
    pairs = [(r, (r // 8) * 8 + (r % 8 // 2 + step) % 4 * 2 + r % 2) for r in range(32)]
    return lax.ppermute(value, "resp", pairs)


def here():
    index = lax.axis_index("resp")
    return lax.rem(index, 2), lax.div(index, 8), lax.rem(lax.div(index, 2), 4)


def columns(core, width):
    return pl.ds(pl.multiple_of(core * width, width), width)


def run_copies(pairs, sems):
    copies = [pltpu.make_async_copy(a, b, sems.at[i]) for i, (a, b) in enumerate(pairs)]
    for copy in copies:
        copy.start()
    for copy in copies:
        copy.wait()


def columns(core, width):
    return pl.ds(pl.multiple_of(core * width, width), width)


def started(pairs, sems):
    copies = [pltpu.make_async_copy(a, b, sems.at[i]) for i, (a, b) in enumerate(pairs)]
    for copy in copies:
        copy.start()
    return copies


def waited(copies):
    for copy in copies:
        copy.wait()


def half_copies(side, pq, rq, pg, rg, target):
    cols = columns(side, Q_COLS)
    return [
        (pq.at[:, cols], target.at[0]),
        (rq.at[0, :, cols], target.at[1]),
        (pg.at[:, cols], target.at[2]),
        (rg.at[0, :, cols], target.at[3]),
    ]


def pack_kernel(prompt_kv, resp_kv, pq, rq, pg, rg, own, send, send_q, sems):
    core = here()[0]
    pairs = []
    for side, out in ((core, own), (1 - core, send)):
        cols = columns(side, KV_COLS)
        pairs.append((prompt_kv.at[:, cols], out.at[pl.ds(0, TOKENS)]))
        pairs.append((resp_kv.at[0, :, cols], out.at[pl.ds(TOKENS, TOKENS)]))
    pairs += half_copies(1 - core, pq, rq, pg, rg, send_q)
    waited(started(pairs, sems))


def pack(*operands):
    return call(
        pack_kernel,
        "pack",
        [HBM] * 6,
        [shape(BLOCK, KV_COLS)] * 2 + [shape(4, TOKENS, Q_COLS)],
        [pltpu.SemaphoreType.DMA((8,))],
    )(*operands)


def note_of(core, first, values):
    row, lane = iota((NOTE, KV_COLS), 0), iota((NOTE, KV_COLS), 1)
    note = jnp.zeros((NOTE, KV_COLS), f32)
    for number, value in enumerate(values):
        note = jnp.where(lane == core * 8 + first + number, value, note)
    return jnp.where(row == 0, note, 0.0).astype(bf16)


def join_cores_kernel(logratio, own, recv, after, block):
    block[:TOKENS] = own[:TOKENS]
    block[TOKENS:BLOCK] = recv[:TOKENS]
    ratio = jnp.full((NOTE, KV_COLS), logratio[0], f32)
    high = ratio.astype(bf16).astype(f32)
    middle = (ratio - high).astype(bf16).astype(f32)
    block[BLOCK:] = note_of(here()[0], 0, (high, middle, ratio - high - middle))


def join_cores(logratio, own, recv, after):
    return call(
        join_cores_kernel,
        "join_cores",
        [SMEM] + [VMEM] * 2 + [AFTER],
        shape(PIECE, KV_COLS),
    )(logratio, own, recv, after)


def facts_kernel(partner, chosen, resp_len, after, note):
    values = [ref[0].astype(f32) for ref in (partner, chosen, resp_len)]
    note[...] = note_of(here()[0], 3, values)


def facts(partner, chosen, resp_len, after):
    return call(facts_kernel, "facts", [SMEM] * 3 + [AFTER], shape(NOTE, KV_COLS))(
        partner, chosen, resp_len, after
    )


def join_kernel(*refs):
    pieces, chunk = refs[:-2], refs[-1]
    for p, piece in enumerate(pieces):
        chunk[p * PIECE : (p + 1) * PIECE] = piece[...]


def join(pieces, after):
    return call(
        join_kernel,
        "join",
        [VMEM] * len(pieces) + [AFTER],
        shape(len(pieces) * PIECE, KV_COLS),
    )(*pieces, after)


def turned(block):
    rows = jnp.concatenate(
        [block[:, g * HEAD_DIM : (g + 1) * HEAD_DIM] for g in range(GROUP)], axis=0
    )
    return rows.T


def softmax_part(scores, value_rows):
    top = jnp.max(scores, axis=0, keepdims=True)
    raised = jnp.exp2((scores - top) * exp2_scale).astype(bf16)
    total = dot(value_rows, raised)
    packed = jnp.concatenate(
        [total[: HEAD_DIM + 8], jnp.broadcast_to(top, (8, top.shape[1]))], axis=0
    )
    return raised, packed


def with_ones(value_rows):
    return jnp.concatenate([value_rows.T, jnp.ones((16, value_rows.shape[0]), bf16)], axis=0)


def prep_kernel(
    pq, rq, pg, rg, recv, kv_own, kv_recv, q_aug, grads, raised, packed, local, sems
):
    core = here()[0]
    copies = started(half_copies(core, pq, rq, pg, rg, local), sems)
    none = jnp.concatenate(
        [jnp.zeros((HEAD_DIM + 8, TILE), f32), jnp.full((8, TILE), no_max, f32)], axis=0
    )
    for j in (2, 3, 0, 1):
        lanes = lanes_of(j)
        sib, resp = j // 2, j % 2
        if j == 0:
            waited(copies)
        source = recv if sib else local
        turned_q = turned(source[resp])
        q_aug[:HEAD_DIM, lanes] = turned_q
        grads[:, lanes] = turned(source[2 + resp])
        if resp:
            q_aug[HEAD_DIM:, lanes] = jnp.zeros((HEAD_DIM, TILE), bf16)
            rows = (kv_recv if sib else kv_own)[TOKENS:BLOCK]
            scores = dot(rows[:, :HEAD_DIM], turned_q)
            token = iota(scores.shape, 1) % TOKENS
            scores = jnp.where(iota(scores.shape, 0) <= token, scores, blocked_score)
            part, info_rows = softmax_part(scores, with_ones(rows[:, HEAD_DIM:]))
            raised[:, lanes_of(sib)] = part
            packed[:, lanes] = info_rows
        else:
            own_core = 1 - core if sib else core
            token = iota((HEAD_DIM, TILE), 1) % TOKENS + own_core * TOKENS
            row = iota((HEAD_DIM, TILE), 0)
            hidden = jnp.logical_or(row == 0, row > token)
            q_aug[HEAD_DIM:, lanes] = jnp.where(hidden, blocked_score, 0.0).astype(bf16)
            packed[:, lanes] = none


def prep(prompt_q, resp_q, prompt_grad, resp_grad, recv, kv_own, kv_recv):
    return call(
        prep_kernel,
        "prep",
        [HBM] * 4 + [VMEM] * 3,
        [
            shape(2 * HEAD_DIM, LANES),
            shape(HEAD_DIM, LANES),
            shape(TOKENS, 2 * TILE),
            shape(HEAD_DIM + 16, LANES, dtype=f32),
        ],
        [pltpu.VMEM((4, TOKENS, Q_COLS), bf16), pltpu.SemaphoreType.DMA((4,))],
    )(prompt_q, resp_q, prompt_grad, resp_grad, recv, kv_own, kv_recv)


offsets = (0, 3, 1, 2)
early_part = (((0, 0),), ((1, 0),), ((2, 0),), ((3, 0),), ((0, 1), (0, 2)))
side_part = (((1, 1), (1, 2)), ((2, 1), (3, 1)), ((2, 2), (3, 2)))
far_part = (((0, 3), (1, 3), (2, 3), (3, 3)),)
all_parts = (early_part, side_part, far_part)
key_cols = slice(0, HEAD_DIM)
value_cols = slice(HEAD_DIM, KV_COLS)


def blocks_of(part):
    return [block for array in part for block in array]


def keys_in(part):
    return BLOCK * len(blocks_of(part))


def part_rows(kvs, part, cols):
    return jnp.concatenate(
        [
            kv[n * PIECE : n * PIECE + BLOCK, cols]
            for kv, array in zip(kvs, part)
            for n in range(len(array))
        ],
        axis=0,
    )


def place_of(info, block):
    p, i = block
    return (info[1] + 4 - p) % 4, (info[2] + offsets[i]) % 4


def forward_kernel(part, *refs):
    kvs = refs[: len(part)]
    q_aug, after, raised, packed, key_aug, value_rows, scores = refs[len(part) :]
    info = here()
    core, z_own, x_own = info
    row = iota((BLOCK, HEAD_DIM), 1)
    token = (iota((BLOCK, HEAD_DIM), 0) + core * TOKENS) % BLOCK
    first = (row == 0).astype(f32)
    same = jnp.logical_and(row == token, row > 0).astype(f32)
    number = 0
    for kv, array in zip(kvs, part):
        for n, block in enumerate(array):
            rows = slice(number * BLOCK, (number + 1) * BLOCK)
            z_here, x_here = place_of(info, block)
            later = jnp.logical_or(
                z_here > z_own, jnp.logical_and(z_here == z_own, x_here > x_own)
            )
            hidden = first * later.astype(f32)
            if block == (0, 0):
                hidden = same
            key_aug[rows, :HEAD_DIM] = kv[n * PIECE : n * PIECE + BLOCK, key_cols]
            key_aug[rows, HEAD_DIM:] = hidden.astype(bf16)
            number += 1
    value_rows[...] = with_ones(part_rows(kvs, part, value_cols))
    scores[0] = dot(key_aug[...], q_aug[:, lanes_of(0)])
    for j in range(SUBS):
        if j + 1 < SUBS:
            scores[(j + 1) % 2] = dot(key_aug[...], q_aug[:, lanes_of(j + 1)])
        one, info_rows = softmax_part(scores[j % 2], value_rows[...])
        raised[:, lanes_of(j)] = one
        packed[:, lanes_of(j)] = info_rows


def forward(kvs, q_aug, after, part):
    keys = keys_in(part)
    return call(
        functools.partial(forward_kernel, part),
        "forward",
        [VMEM] * (len(part) + 1) + [AFTER],
        [
            shape(keys, LANES),
            shape(HEAD_DIM + 16, LANES, dtype=f32),
        ],
        [
            pltpu.VMEM((keys, 2 * HEAD_DIM), bf16),
            pltpu.VMEM((HEAD_DIM + 16, keys), bf16),
            pltpu.VMEM((2, keys, TILE), f32),
        ],
        flops=4 * keys * LANES * HEAD_DIM,
    )(*kvs, q_aug, after)


def collect_kernel(*refs):
    note, *refs = refs
    refs, notes = list(refs[:-1]), refs[-1]
    rows = []
    for part in all_parts:
        for array in part:
            kv = refs.pop(0)
            for n in range(len(array)):
                rows.append(kv[n * PIECE + BLOCK : (n + 1) * PIECE].astype(f32)[0:1])
    notes[...] = (jnp.concatenate(rows, axis=0) + note[...].astype(f32)).astype(bf16)


def collect(note, kv_lists):
    flat = [kv for kvs in kv_lists for kv in kvs]
    return call(collect_kernel, "collect", [VMEM] * (len(flat) + 1), shape(16, KV_COLS))(
        note, *flat
    )


def combine_kernel(
    own_notes, sib_notes, grads, part_0, part_1, part_2, part_own, out, cot_aug, gains
):
    info = here()
    notes = own_notes[...].astype(f32) + sib_notes[...].astype(f32)
    row = iota((16, 1), 0)
    seat = jnp.zeros_like(row)
    for number, block in enumerate(block for part in all_parts for block in blocks_of(part)):
        z_here, x_here = place_of(info, block)
        seat = jnp.where(row == number, z_here * 8 + x_here * 2, seat)
    ratios = [
        notes[:, side * 8 : side * 8 + 1]
        + notes[:, side * 8 + 1 : side * 8 + 2]
        + notes[:, side * 8 + 2 : side * 8 + 3]
        for side in range(2)
    ]
    weights = []
    for sib in range(2):
        own_core = 1 - info[0] if sib else info[0]
        own_row = notes[0:1, :]
        lane = iota(own_row.shape, 1)

        def field(number):
            mask = lane == own_core * 8 + number
            return jnp.sum(jnp.where(mask, own_row, 0.0), axis=1, keepdims=True)

        ratio = field(0) + field(1) + field(2)
        partner, chosen, count = field(3), field(4), field(5)
        mate = jnp.zeros((1, 1), f32)
        for side in range(2):
            found = (seat + side).astype(f32) == partner
            mate = mate + jnp.sum(jnp.where(found, ratios[side], 0.0), axis=0, keepdims=True)
        sign = 2.0 * chosen - 1.0
        pair_weight = sign * jax.nn.sigmoid(-pair_beta * (sign * (ratio - mate)))
        token = (iota((1, TILE), 1) % TOKENS).astype(f32)
        weights.append(jnp.where(token < count, pair_weight, 0.0))

    for j in range(SUBS):
        lanes = lanes_of(j)
        parts = (part_0, part_1, part_2) + ((part_own,) if j % 2 else ())
        tops = [part[HEAD_DIM + 8 : HEAD_DIM + 9, lanes] for part in parts]
        top = functools.reduce(jnp.maximum, tops)
        factors = [jnp.exp2((one - top) * exp2_scale) for one in tops]
        length = sum(f * part[HEAD_DIM : HEAD_DIM + 1, lanes] for f, part in zip(factors, parts))
        inverse = 1.0 / length
        factors = [f * inverse for f in factors]
        rounded = sum(f * part[:HEAD_DIM, lanes] for f, part in zip(factors, parts)).astype(bf16)
        out[:, lanes] = rounded
        gains[:, lanes] = jnp.concatenate(
            factors + [jnp.zeros((8 - len(factors), TILE), f32)], axis=0
        )
        if j % 2:
            cot = (weights[j // 2] * grads[:, lanes].astype(f32)).astype(bf16)
        else:
            cot = grads[:, lanes]
        cot_aug[:HEAD_DIM, lanes] = cot
        row_dot = -jnp.sum(cot.astype(f32) * rounded.astype(f32), axis=0, keepdims=True)
        high = row_dot.astype(bf16).astype(f32)
        middle = (row_dot - high).astype(bf16).astype(f32)
        low = row_dot - high - middle
        row = iota((16, TILE), 0)
        split = jnp.where(
            row == 0, high, jnp.where(row == 1, middle, jnp.where(row == 2, low, 0.0))
        )
        cot_aug[HEAD_DIM : HEAD_DIM + 16, lanes] = split.astype(bf16)
        cot_aug[HEAD_DIM + 16 :, lanes] = jnp.zeros((HEAD_DIM - 16, TILE), bf16)


def combine(own_notes, sib_notes, grads, parts):
    return call(
        combine_kernel,
        "combine",
        [VMEM] * (3 + len(parts)),
        [shape(HEAD_DIM, LANES), shape(2 * HEAD_DIM, LANES), shape(8, LANES, dtype=f32)],
    )(own_notes, sib_notes, grads, *parts)


def value_aug_of(value_rows):
    column = iota(value_rows.shape, 1)
    return jnp.concatenate([value_rows, (column < 3).astype(f32).astype(bf16)], axis=1)


def backward_kernel(part, splits, chunk, *refs):
    kvs = refs[: len(part)]
    raised, q_aug, cot_aug, gains, after, slopes = refs[len(part) : len(part) + 6]
    grads = refs[len(part) + 6 : len(part) + 6 + len(splits)]
    value_aug, moved, scaled_q, scaled_cot = refs[len(part) + 6 + len(splits) :]
    value_aug[...] = value_aug_of(part_rows(kvs, part, value_cols))
    moved[0] = dot(value_aug[...], cot_aug[:, lanes_of(0)])
    for j in range(SUBS):
        lanes = lanes_of(j)
        if j + 1 < SUBS:
            moved[(j + 1) % 2] = dot(value_aug[...], cot_aug[:, lanes_of(j + 1)])
        gain = gains[chunk : chunk + 1, lanes]
        scaled_cot[:, lanes] = (cot_aug[:HEAD_DIM, lanes].astype(f32) * gain).astype(bf16)
        scaled_q[:, lanes] = (
            q_aug[:HEAD_DIM, lanes].astype(f32) * (gain * score_scale)
        ).astype(bf16)
        slopes[:, lanes] = (raised[:, lanes].astype(f32) * moved[j % 2]).astype(bf16)
    for columns_here, left, right in (
        (value_cols, raised, scaled_cot),
        (key_cols, slopes, scaled_q),
    ):
        total = dot(left[...], right[...], 1, 1)
        for grad, (numbers, _) in zip(grads, splits):
            for n, number in enumerate(numbers):
                grad[n * BLOCK : (n + 1) * BLOCK, columns_here] = total[
                    number * BLOCK : (number + 1) * BLOCK
                ].astype(grad.dtype)


def backward(kvs, raised, q_aug, cot_aug, gains, after, part, chunk, splits):
    keys = keys_in(part)
    return call(
        functools.partial(backward_kernel, part, splits, chunk),
        "backward",
        [VMEM] * (len(part) + 4) + [AFTER],
        [shape(keys, LANES)]
        + [shape(len(numbers) * BLOCK, KV_COLS, dtype=kind) for numbers, kind in splits],
        [
            pltpu.VMEM((keys, 2 * HEAD_DIM), bf16),
            pltpu.VMEM((2, keys, TILE), f32),
            pltpu.VMEM((HEAD_DIM, LANES), bf16),
            pltpu.VMEM((HEAD_DIM, LANES), bf16),
        ],
        flops=6 * keys * LANES * HEAD_DIM,
    )(*kvs, raised, q_aug, cot_aug, gains, after)


def rows_of(turned_rows):
    rows = turned_rows.T
    return jnp.concatenate(
        [rows[g * TOKENS : (g + 1) * TOKENS] for g in range(GROUP)], axis=1
    )


def finish_kernel(*refs):
    refs = list(refs)
    kv_lists = [[refs.pop(0) for _ in part] for part in all_parts]
    all_slopes = [refs.pop(0) for _ in all_parts]
    (kv_own, kv_recv, raised, q_aug, cot_aug, gains, out, after) = refs[:8]
    (own_result, sib_result, keys) = refs[8:]
    spans, start = [], 0
    for kvs, part in zip(kv_lists, all_parts):
        span = slice(start, start + keys_in(part))
        keys[:, span] = part_rows(kvs, part, key_cols).T
        spans.append(span)
        start = span.stop
    for j in (2, 3, 0, 1):
        lanes = lanes_of(j)
        sib, resp = j // 2, j % 2
        result = sib_result if sib else own_result
        total = None
        for chunk, slopes in enumerate(all_slopes):
            part = dot(keys[:, spans[chunk]], slopes[:, lanes])
            part = part * (gains[chunk : chunk + 1, lanes] * score_scale)
            total = part if total is None else total + part
        if resp:
            gain = gains[3:4, lanes]
            rows = (kv_recv if sib else kv_own)[TOKENS:BLOCK]
            own_raised = raised[:, lanes_of(sib)]
            moved = dot(value_aug_of(rows[:, HEAD_DIM:]), cot_aug[:, lanes])
            own_slopes = (own_raised.astype(f32) * moved).astype(bf16)
            total = total + dot(rows[:, :HEAD_DIM].T, own_slopes) * (gain * score_scale)
            scaled_q = (q_aug[:HEAD_DIM, lanes].astype(f32) * (gain * score_scale)).astype(bf16)
            scaled_cot = (cot_aug[:HEAD_DIM, lanes].astype(f32) * gain).astype(bf16)
            key_grad = dot(own_slopes, scaled_q, 1, 1)
            value_grad = dot(own_raised, scaled_cot, 1, 1)
            result[:, 4 * Q_COLS :] = jnp.concatenate([key_grad, value_grad], axis=1).astype(bf16)
        result[:, resp * Q_COLS : (resp + 1) * Q_COLS] = rows_of(
            out[:, lanes].astype(f32)
        ).astype(bf16)
        result[:, (2 + resp) * Q_COLS : (3 + resp) * Q_COLS] = rows_of(total).astype(bf16)


def finish(kv_lists, slopes, kv_own, kv_recv, raised, q_aug, cot_aug, gains, out, after):
    flat = [kv for kvs in kv_lists for kv in kvs]
    return call(
        finish_kernel,
        "finish",
        [VMEM] * (len(flat) + len(slopes) + 7) + [AFTER],
        [shape(TOKENS, 4 * Q_COLS + KV_COLS)] * 2,
        [pltpu.VMEM((HEAD_DIM, 16 * BLOCK), bf16)],
        flops=6 * 4 * BLOCK * LANES * HEAD_DIM,
    )(*flat, *slopes, kv_own, kv_recv, raised, q_aug, cot_aug, gains, out, after)


def place_kernel(own, recv, prompt_out, resp_out, prompt_dq, resp_dq, resp_dkv, done, sems):
    pairs = []
    core = here()[0]
    for side, source in ((core, own), (1 - core, recv)):
        cols = columns(side, Q_COLS)
        targets = (
            prompt_out.at[:, cols],
            resp_out.at[0, :, cols],
            prompt_dq.at[:, cols],
            resp_dq.at[0, :, cols],
        )
        pairs += [
            (source.at[:, pl.ds(n * Q_COLS, Q_COLS)], target) for n, target in enumerate(targets)
        ]
        pairs.append(
            (source.at[:, pl.ds(4 * Q_COLS, KV_COLS)], resp_dkv.at[0, :, columns(side, KV_COLS)])
        )
    copies = started(pairs, sems)
    done[...] = jnp.zeros_like(done)
    waited(copies)


def place(own, recv):
    prompt = shape(TOKENS, 2 * Q_COLS)
    resp = shape(1, TOKENS, 2 * Q_COLS)
    return call(
        place_kernel,
        "place",
        [VMEM] * 2,
        [prompt, resp, prompt, resp, shape(1, TOKENS, 2 * KV_COLS), shape(8, 128, dtype=f32)],
        [pltpu.SemaphoreType.DMA((10,))],
        out_specs=[HBM] * 5 + [VMEM],
    )(own, recv)


def add_split_kernel(count, *refs):
    terms, outs = refs[:count], refs[count + 1 :]
    start = 0
    for out in outs:
        rows = slice(start, start + out.shape[0])
        total = terms[0][rows].astype(f32)
        for term in terms[1:]:
            total = total + term[rows].astype(f32)
        out[...] = total.astype(out.dtype)
        start += out.shape[0]


def add_split(terms, outs, rows, after, flops=0):
    return call(
        functools.partial(add_split_kernel, len(terms)),
        "add_split",
        [VMEM] * len(terms) + [AFTER],
        [shape(rows, KV_COLS)] * outs,
        flops=flops,
    )(*terms, after)


def sum_column_kernel(own, grad_z, back_far, back_1, back_2, own_sum, to_1, to_2, to_3):
    own_sum[...] = own[...] + back_far[:BLOCK].astype(f32)
    for p, out in ((1, to_1), (2, to_2), (3, to_3)):
        rows = slice((p - 1) * BLOCK, p * BLOCK)
        total = grad_z[rows] + back_far[p * BLOCK : (p + 1) * BLOCK].astype(f32)
        total = total + back_1[rows].astype(f32) + back_2[rows].astype(f32)
        out[...] = total.astype(bf16)


def sum_column(own, grad_z, back_far, back_1, back_2):
    own_sum, *to_z = call(
        sum_column_kernel,
        "sum_column",
        [VMEM] * 5,
        [shape(BLOCK, KV_COLS, dtype=f32)] + [shape(BLOCK, KV_COLS)] * 3,
    )(own, grad_z, back_far, back_1, back_2)
    return own_sum, to_z


def last_kernel(kept, recv, after, out):
    core = here()[0]

    @pl.when(core == 0)
    def _():
        out[:, :KV_COLS] = kept[...]
        out[:, KV_COLS:] = recv[...]

    @pl.when(core == 1)
    def _():
        out[:, :KV_COLS] = recv[...]
        out[:, KV_COLS:] = kept[...]


def last(kept, recv, after):
    return call(
        last_kernel, "last", [VMEM] * 2 + [AFTER], shape(TOKENS, 2 * KV_COLS)
    )(kept, recv, after)


def shards(
    prompt_q,
    prompt_kv,
    resp_q,
    resp_kv,
    prompt_grad,
    resp_grad,
    resp_len,
    logratio,
    partner,
    chosen,
):
    prompt_q, prompt_kv, resp_q, resp_kv, prompt_grad, resp_grad = [
        pltpu.with_memory_space_constraint(array, pltpu.HBM)
        for array in (prompt_q, prompt_kv, resp_q, resp_kv, prompt_grad, resp_grad)
    ]
    kv_own, kv_send, q_send = pack(
        prompt_kv, resp_kv, prompt_q, resp_q, prompt_grad, resp_grad
    )
    kv_recv = swap_core(kv_send)
    q_recv = swap_core(q_send)
    block = join_cores(logratio, kv_own, kv_recv, q_recv)

    from_z = [shift_z(block, p) for p in (1, 2, 3)]
    from_x = [shift_x(block, 4 - offset) for offset in offsets[1:3]]
    q_aug, grads, raised_own, part_own = prep(
        prompt_q, resp_q, prompt_grad, resp_grad, q_recv, kv_own, kv_recv
    )
    note = facts(partner, chosen, resp_len, part_own)
    far = join(from_z[1:], note)
    near = join(from_x, note)
    column = join([block] + from_z, near)
    early_kvs = [block] + from_z + [near]
    side_kvs = [shift_z(near, 1)] + [shift_x(far, 4 - offset) for offset in offsets[1:3]]
    far_kvs = [shift_x(column, 2)]
    kv_lists = [early_kvs, side_kvs, far_kvs]

    raised, packs = [], []
    for kvs, part in zip(kv_lists, all_parts):
        one, pack_rows = forward(kvs, q_aug, note, part)
        raised.append(one)
        packs.append(pack_rows)
    own_notes = collect(note, kv_lists)
    out, cot_aug, gains = combine(
        own_notes, swap_core(own_notes), grads, packs + [part_own]
    )

    def backward_of(chunk, splits, after):
        return backward(
            kv_lists[chunk],
            raised[chunk],
            q_aug,
            cot_aug,
            gains,
            after,
            all_parts[chunk],
            chunk,
            splits,
        )

    slopes_far, grad_far = backward_of(2, (((0, 1, 2, 3), bf16),), gains)
    back_far = shift_x(grad_far, 2)
    slopes_side, grad_1, grad_2 = backward_of(
        1, (((0, 2, 3), bf16), ((1, 4, 5), bf16)), grad_far
    )
    back_1, back_2 = shift_x(grad_1, offsets[1]), shift_x(grad_2, offsets[2])
    slopes_early, grad_own, grad_z, *to_x = backward_of(
        0, (((0,), f32), ((1, 2, 3), f32), ((4,), bf16), ((5,), bf16)), grad_1
    )
    slopes = [slopes_early, slopes_side, slopes_far]

    back_x = [shift_x(term, offset) for term, offset in zip(to_x, offsets[1:3])]
    own_sum, to_z = sum_column(grad_own, grad_z, back_far, back_1, back_2)
    back_z = [shift_z(term, 4 - p) for p, term in zip((1, 2, 3), to_z)]
    own_result, sib_result = finish(
        kv_lists, slopes, kv_own, kv_recv, raised_own, q_aug, cot_aug, gains, out, grad_own
    )
    prompt_out, resp_out, prompt_dq, resp_dq, resp_dkv, placed = place(
        own_result, swap_core(sib_result)
    )
    kept, sent = add_split([own_sum] + back_z + back_x, 2, TOKENS, own_sum, 2 * 10**10)
    prompt_dkv = last(kept, swap_core(sent), placed)
    return (prompt_out, resp_out, prompt_dq, resp_dq, prompt_dkv, resp_dkv)


def solution(mesh):
    return jax.shard_map(
        shards,
        mesh=mesh,
        in_specs=(
            P(("batch", "resp"), "head"),
            P(("batch", "resp"), "head"),
            P(("batch", "resp"), None, "head"),
            P(("batch", "resp"), None, "head"),
            P(("batch", "resp"), "head"),
            P(("batch", "resp"), None, "head"),
            P(("batch", "resp")),
            P(("batch", "resp")),
            P(("batch", "resp")),
            P(("batch", "resp")),
        ),
        out_specs=(
            P(("batch", "resp"), "head"),
            P(("batch", "resp"), None, "head"),
            P(("batch", "resp"), "head"),
            P(("batch", "resp"), None, "head"),
            P(("batch", "resp"), "head"),
            P(("batch", "resp"), None, "head"),
        ),
        check_vma=False,
    )
```

```python
import functools

import jax
import jax.numpy as jnp
from jax import lax
from jax.experimental import pallas as pl
from jax.experimental.pallas import tpu as pltpu
from jax.sharding import PartitionSpec as P

HEAD_DIM = 128
GROUP = 8
TOKENS = 64
KV_COLS = 2 * HEAD_DIM
Q_COLS = GROUP * HEAD_DIM
BLOCK = 2 * TOKENS
NOTE = 16
PIECE = BLOCK + NOTE
TILE = GROUP * TOKENS
LANES = 4 * TILE
SUBS = LANES // TILE

score_scale = HEAD_DIM ** (-0.5)
exp2_scale = score_scale * 1.4426950408889634
pair_beta = 0.1
blocked_score = -(2.0**30)
no_max = -(2.0**31)

bf16 = jnp.bfloat16
f32 = jnp.float32


def params(**kw):
    return pltpu.CompilerParams(vmem_limit_bytes=16 * 2**20, **kw)


def dot(left, right, left_dim=1, right_dim=0):
    return lax.dot_general(
        left, right, (((left_dim,), (right_dim,)), ((), ())), preferred_element_type=f32
    )


def iota(shape, dim):
    return lax.broadcasted_iota(jnp.int32, shape, dim)


VMEM = pl.BlockSpec(memory_space=pltpu.VMEM)
SMEM = pl.BlockSpec(memory_space=pltpu.SMEM)
HBM = pl.BlockSpec(memory_space=pltpu.HBM)
AFTER = pl.BlockSpec(memory_space=pl.ANY)


def shape(*dims, dtype=bf16):
    return jax.ShapeDtypeStruct(dims, dtype)


def call(kernel, name, in_specs, out_shape, scratch=(), out_specs=None, flops=0):
    extra = {} if out_specs is None else {"out_specs": out_specs}
    cost = pl.CostEstimate(flops=flops, bytes_accessed=2**20, transcendentals=0)
    return pl.pallas_call(
        kernel,
        in_specs=in_specs,
        out_shape=out_shape,
        scratch_shapes=list(scratch),
        compiler_params=params(),
        cost_estimate=cost,
        name=name,
        **extra,
    )


def lanes_of(j):
    return slice(j * TILE, (j + 1) * TILE)


def swap_core(value):
    return lax.ppermute(value, "resp", [(r, r ^ 1) for r in range(32)])


def shift_z(value, step):
    pairs = [(r, ((r // 8 + step) % 4) * 8 + r % 8) for r in range(32)]
    return lax.ppermute(value, "resp", pairs)


def shift_x(value, step):
    pairs = [(r, (r // 8) * 8 + (r % 8 // 2 + step) % 4 * 2 + r % 2) for r in range(32)]
    return lax.ppermute(value, "resp", pairs)


def here():
    index = lax.axis_index("resp")
    return lax.rem(index, 2), lax.div(index, 8), lax.rem(lax.div(index, 2), 4)


def columns(core, width):
    return pl.ds(pl.multiple_of(core * width, width), width)


def run_copies(pairs, sems):
    copies = [pltpu.make_async_copy(a, b, sems.at[i]) for i, (a, b) in enumerate(pairs)]
    for copy in copies:
        copy.start()
    for copy in copies:
        copy.wait()


def columns(core, width):
    return pl.ds(pl.multiple_of(core * width, width), width)


def started(pairs, sems):
    copies = [pltpu.make_async_copy(a, b, sems.at[i]) for i, (a, b) in enumerate(pairs)]
    for copy in copies:
        copy.start()
    return copies


def waited(copies):
    for copy in copies:
        copy.wait()


def half_copies(side, pq, rq, pg, rg, target):
    cols = columns(side, Q_COLS)
    return [
        (pq.at[:, cols], target.at[0]),
        (rq.at[0, :, cols], target.at[1]),
        (pg.at[:, cols], target.at[2]),
        (rg.at[0, :, cols], target.at[3]),
    ]


def pack_kernel(prompt_kv, resp_kv, pq, rq, pg, rg, own, send, send_q, sems):
    core = here()[0]
    pairs = []
    for side, out in ((core, own), (1 - core, send)):
        cols = columns(side, KV_COLS)
        pairs.append((prompt_kv.at[:, cols], out.at[pl.ds(0, TOKENS)]))
        pairs.append((resp_kv.at[0, :, cols], out.at[pl.ds(TOKENS, TOKENS)]))
    pairs += half_copies(1 - core, pq, rq, pg, rg, send_q)
    waited(started(pairs, sems))


def pack(*operands):
    return call(
        pack_kernel,
        "pack",
        [HBM] * 6,
        [shape(BLOCK, KV_COLS)] * 2 + [shape(4, TOKENS, Q_COLS)],
        [pltpu.SemaphoreType.DMA((8,))],
    )(*operands)


def note_of(core, first, values):
    row, lane = iota((NOTE, KV_COLS), 0), iota((NOTE, KV_COLS), 1)
    note = jnp.zeros((NOTE, KV_COLS), f32)
    for number, value in enumerate(values):
        note = jnp.where(lane == core * 8 + first + number, value, note)
    return jnp.where(row == 0, note, 0.0).astype(bf16)


def join_cores_kernel(logratio, own, recv, after, block):
    block[:TOKENS] = own[:TOKENS]
    block[TOKENS:BLOCK] = recv[:TOKENS]
    ratio = jnp.full((NOTE, KV_COLS), logratio[0], f32)
    high = ratio.astype(bf16).astype(f32)
    middle = (ratio - high).astype(bf16).astype(f32)
    block[BLOCK:] = note_of(here()[0], 0, (high, middle, ratio - high - middle))


def join_cores(logratio, own, recv, after):
    return call(
        join_cores_kernel,
        "join_cores",
        [SMEM] + [VMEM] * 2 + [AFTER],
        shape(PIECE, KV_COLS),
    )(logratio, own, recv, after)


def facts_kernel(partner, chosen, resp_len, after, note):
    values = [ref[0].astype(f32) for ref in (partner, chosen, resp_len)]
    note[...] = note_of(here()[0], 3, values)


def facts(partner, chosen, resp_len, after):
    return call(facts_kernel, "facts", [SMEM] * 3 + [AFTER], shape(NOTE, KV_COLS))(
        partner, chosen, resp_len, after
    )


def join_kernel(count, *refs):
    pieces, chunk = refs[:count], refs[-1]
    for p, piece in enumerate(pieces):
        chunk[p * PIECE : (p + 1) * PIECE] = piece[...]


def join(pieces, *afters):
    return call(
        functools.partial(join_kernel, len(pieces)),
        "join",
        [VMEM] * len(pieces) + [AFTER] * len(afters),
        shape(len(pieces) * PIECE, KV_COLS),
    )(*pieces, *afters)


def turned(block):
    rows = jnp.concatenate(
        [block[:, g * HEAD_DIM : (g + 1) * HEAD_DIM] for g in range(GROUP)], axis=0
    )
    return rows.T


def softmax_part(scores, value_rows):
    top = jnp.max(scores, axis=0, keepdims=True)
    raised = jnp.exp2((scores - top) * exp2_scale).astype(bf16)
    total = dot(value_rows, raised)
    packed = jnp.concatenate(
        [total[: HEAD_DIM + 8], jnp.broadcast_to(top, (8, top.shape[1]))], axis=0
    )
    return raised, packed


def with_ones(value_rows):
    return jnp.concatenate([value_rows.T, jnp.ones((16, value_rows.shape[0]), bf16)], axis=0)


def prep_kernel(
    pq, rq, pg, rg, recv, kv_own, kv_recv, q_aug, grads, raised, packed, local, sems
):
    core = here()[0]
    copies = started(half_copies(core, pq, rq, pg, rg, local), sems)
    none = jnp.concatenate(
        [jnp.zeros((HEAD_DIM + 8, TILE), f32), jnp.full((8, TILE), no_max, f32)], axis=0
    )
    for j in (2, 3, 0, 1):
        lanes = lanes_of(j)
        sib, resp = j // 2, j % 2
        if j == 0:
            waited(copies)
        source = recv if sib else local
        turned_q = turned(source[resp])
        q_aug[:HEAD_DIM, lanes] = turned_q
        grads[:, lanes] = turned(source[2 + resp])
        if resp:
            q_aug[HEAD_DIM:, lanes] = jnp.zeros((HEAD_DIM, TILE), bf16)
            rows = (kv_recv if sib else kv_own)[TOKENS:BLOCK]
            scores = dot(rows[:, :HEAD_DIM], turned_q)
            token = iota(scores.shape, 1) % TOKENS
            scores = jnp.where(iota(scores.shape, 0) <= token, scores, blocked_score)
            part, info_rows = softmax_part(scores, with_ones(rows[:, HEAD_DIM:]))
            raised[:, lanes_of(sib)] = part
            packed[:, lanes] = info_rows
        else:
            own_core = 1 - core if sib else core
            token = iota((HEAD_DIM, TILE), 1) % TOKENS + own_core * TOKENS
            row = iota((HEAD_DIM, TILE), 0)
            hidden = jnp.logical_or(row == 0, row > token)
            q_aug[HEAD_DIM:, lanes] = jnp.where(hidden, blocked_score, 0.0).astype(bf16)
            packed[:, lanes] = none


def prep(prompt_q, resp_q, prompt_grad, resp_grad, recv, kv_own, kv_recv):
    return call(
        prep_kernel,
        "prep",
        [HBM] * 4 + [VMEM] * 3,
        [
            shape(2 * HEAD_DIM, LANES),
            shape(HEAD_DIM, LANES),
            shape(TOKENS, 2 * TILE),
            shape(HEAD_DIM + 16, LANES, dtype=f32),
        ],
        [pltpu.VMEM((4, TOKENS, Q_COLS), bf16), pltpu.SemaphoreType.DMA((4,))],
    )(prompt_q, resp_q, prompt_grad, resp_grad, recv, kv_own, kv_recv)


offsets = (0, 3, 1, 2)
early_part = (((0, 0),), ((1, 0),), ((2, 0),), ((3, 0),), ((0, 1), (0, 2)))
side_part = (((1, 1), (1, 2)), ((2, 1), (3, 1)), ((2, 2), (3, 2)))
far_part = (((0, 3), (1, 3), (2, 3), (3, 3)),)
all_parts = (early_part, side_part, far_part)
key_cols = slice(0, HEAD_DIM)
value_cols = slice(HEAD_DIM, KV_COLS)


def blocks_of(part):
    return [block for array in part for block in array]


def keys_in(part):
    return BLOCK * len(blocks_of(part))


def part_rows(kvs, part, cols):
    return jnp.concatenate(
        [
            kv[n * PIECE : n * PIECE + BLOCK, cols]
            for kv, array in zip(kvs, part)
            for n in range(len(array))
        ],
        axis=0,
    )


def place_of(info, block):
    p, i = block
    return (info[1] + 4 - p) % 4, (info[2] + offsets[i]) % 4


def forward_kernel(part, *refs):
    kvs = refs[: len(part)]
    q_aug, after, raised, packed, key_aug, value_rows, scores = refs[len(part) :]
    info = here()
    core, z_own, x_own = info
    row = iota((BLOCK, HEAD_DIM), 1)
    token = (iota((BLOCK, HEAD_DIM), 0) + core * TOKENS) % BLOCK
    first = (row == 0).astype(f32)
    same = jnp.logical_and(row == token, row > 0).astype(f32)
    number = 0
    for kv, array in zip(kvs, part):
        for n, block in enumerate(array):
            rows = slice(number * BLOCK, (number + 1) * BLOCK)
            z_here, x_here = place_of(info, block)
            later = jnp.logical_or(
                z_here > z_own, jnp.logical_and(z_here == z_own, x_here > x_own)
            )
            hidden = first * later.astype(f32)
            if block == (0, 0):
                hidden = same
            key_aug[rows, :HEAD_DIM] = kv[n * PIECE : n * PIECE + BLOCK, key_cols]
            key_aug[rows, HEAD_DIM:] = hidden.astype(bf16)
            number += 1
    value_rows[...] = with_ones(part_rows(kvs, part, value_cols))
    scores[0] = dot(key_aug[...], q_aug[:, lanes_of(0)])
    for j in range(SUBS):
        if j + 1 < SUBS:
            scores[(j + 1) % 2] = dot(key_aug[...], q_aug[:, lanes_of(j + 1)])
        one, info_rows = softmax_part(scores[j % 2], value_rows[...])
        raised[:, lanes_of(j)] = one
        packed[:, lanes_of(j)] = info_rows


def forward(kvs, q_aug, after, part):
    keys = keys_in(part)
    return call(
        functools.partial(forward_kernel, part),
        "forward",
        [VMEM] * (len(part) + 1) + [AFTER],
        [
            shape(keys, LANES),
            shape(HEAD_DIM + 16, LANES, dtype=f32),
        ],
        [
            pltpu.VMEM((keys, 2 * HEAD_DIM), bf16),
            pltpu.VMEM((HEAD_DIM + 16, keys), bf16),
            pltpu.VMEM((2, keys, TILE), f32),
        ],
        flops=4 * keys * LANES * HEAD_DIM,
    )(*kvs, q_aug, after)


def collect_kernel(*refs):
    note, *refs = refs
    refs, notes = list(refs[:-2]), refs[-1]
    rows = []
    for part in all_parts:
        for array in part:
            kv = refs.pop(0)
            for n in range(len(array)):
                rows.append(kv[n * PIECE + BLOCK : (n + 1) * PIECE].astype(f32)[0:1])
    notes[...] = (jnp.concatenate(rows, axis=0) + note[...].astype(f32)).astype(bf16)


def collect(note, kv_lists, after):
    flat = [kv for kvs in kv_lists for kv in kvs]
    return call(
        collect_kernel, "collect", [VMEM] * (len(flat) + 1) + [AFTER], shape(16, KV_COLS)
    )(note, *flat, after)


def combine_kernel(
    own_notes, sib_notes, grads, part_0, part_1, part_2, part_own, out, cot_aug, gains
):
    info = here()
    notes = own_notes[...].astype(f32) + sib_notes[...].astype(f32)
    row = iota((16, 1), 0)
    seat = jnp.zeros_like(row)
    for number, block in enumerate(block for part in all_parts for block in blocks_of(part)):
        z_here, x_here = place_of(info, block)
        seat = jnp.where(row == number, z_here * 8 + x_here * 2, seat)
    ratios = [
        notes[:, side * 8 : side * 8 + 1]
        + notes[:, side * 8 + 1 : side * 8 + 2]
        + notes[:, side * 8 + 2 : side * 8 + 3]
        for side in range(2)
    ]
    weights = []
    for sib in range(2):
        own_core = 1 - info[0] if sib else info[0]
        own_row = notes[0:1, :]
        lane = iota(own_row.shape, 1)

        def field(number):
            mask = lane == own_core * 8 + number
            return jnp.sum(jnp.where(mask, own_row, 0.0), axis=1, keepdims=True)

        ratio = field(0) + field(1) + field(2)
        partner, chosen, count = field(3), field(4), field(5)
        mate = jnp.zeros((1, 1), f32)
        for side in range(2):
            found = (seat + side).astype(f32) == partner
            mate = mate + jnp.sum(jnp.where(found, ratios[side], 0.0), axis=0, keepdims=True)
        sign = 2.0 * chosen - 1.0
        pair_weight = sign * jax.nn.sigmoid(-pair_beta * (sign * (ratio - mate)))
        token = (iota((1, TILE), 1) % TOKENS).astype(f32)
        weights.append(jnp.where(token < count, pair_weight, 0.0))

    for j in range(SUBS):
        lanes = lanes_of(j)
        parts = (part_0, part_1, part_2) + ((part_own,) if j % 2 else ())
        tops = [part[HEAD_DIM + 8 : HEAD_DIM + 9, lanes] for part in parts]
        top = functools.reduce(jnp.maximum, tops)
        factors = [jnp.exp2((one - top) * exp2_scale) for one in tops]
        length = sum(f * part[HEAD_DIM : HEAD_DIM + 1, lanes] for f, part in zip(factors, parts))
        inverse = 1.0 / length
        factors = [f * inverse for f in factors]
        rounded = sum(f * part[:HEAD_DIM, lanes] for f, part in zip(factors, parts)).astype(bf16)
        out[:, lanes] = rounded
        gains[:, lanes] = jnp.concatenate(
            factors + [jnp.zeros((8 - len(factors), TILE), f32)], axis=0
        )
        if j % 2:
            cot = (weights[j // 2] * grads[:, lanes].astype(f32)).astype(bf16)
        else:
            cot = grads[:, lanes]
        cot_aug[:HEAD_DIM, lanes] = cot
        row_dot = -jnp.sum(cot.astype(f32) * rounded.astype(f32), axis=0, keepdims=True)
        high = row_dot.astype(bf16).astype(f32)
        middle = (row_dot - high).astype(bf16).astype(f32)
        low = row_dot - high - middle
        row = iota((16, TILE), 0)
        split = jnp.where(
            row == 0, high, jnp.where(row == 1, middle, jnp.where(row == 2, low, 0.0))
        )
        cot_aug[HEAD_DIM : HEAD_DIM + 16, lanes] = split.astype(bf16)
        cot_aug[HEAD_DIM + 16 :, lanes] = jnp.zeros((HEAD_DIM - 16, TILE), bf16)


def combine(own_notes, sib_notes, grads, parts):
    return call(
        combine_kernel,
        "combine",
        [VMEM] * (3 + len(parts)),
        [shape(HEAD_DIM, LANES), shape(2 * HEAD_DIM, LANES), shape(8, LANES, dtype=f32)],
    )(own_notes, sib_notes, grads, *parts)


def value_aug_of(value_rows):
    column = iota(value_rows.shape, 1)
    return jnp.concatenate([value_rows, (column < 3).astype(f32).astype(bf16)], axis=1)


def backward_kernel(part, splits, chunk, *refs):
    kvs = refs[: len(part)]
    raised, q_aug, cot_aug, gains, after, slopes = refs[len(part) : len(part) + 6]
    grads = refs[len(part) + 6 : len(part) + 6 + len(splits)]
    value_aug, moved, scaled_q, scaled_cot = refs[len(part) + 6 + len(splits) :]
    value_aug[...] = value_aug_of(part_rows(kvs, part, value_cols))
    moved[0] = dot(value_aug[...], cot_aug[:, lanes_of(0)])
    for j in range(SUBS):
        lanes = lanes_of(j)
        if j + 1 < SUBS:
            moved[(j + 1) % 2] = dot(value_aug[...], cot_aug[:, lanes_of(j + 1)])
        gain = gains[chunk : chunk + 1, lanes]
        scaled_cot[:, lanes] = (cot_aug[:HEAD_DIM, lanes].astype(f32) * gain).astype(bf16)
        scaled_q[:, lanes] = (
            q_aug[:HEAD_DIM, lanes].astype(f32) * (gain * score_scale)
        ).astype(bf16)
        slopes[:, lanes] = (raised[:, lanes].astype(f32) * moved[j % 2]).astype(bf16)
    for columns_here, left, right in (
        (value_cols, raised, scaled_cot),
        (key_cols, slopes, scaled_q),
    ):
        total = dot(left[...], right[...], 1, 1)
        for grad, (numbers, _) in zip(grads, splits):
            for n, number in enumerate(numbers):
                grad[n * BLOCK : (n + 1) * BLOCK, columns_here] = total[
                    number * BLOCK : (number + 1) * BLOCK
                ].astype(grad.dtype)


def backward(kvs, raised, q_aug, cot_aug, gains, after, part, chunk, splits):
    keys = keys_in(part)
    return call(
        functools.partial(backward_kernel, part, splits, chunk),
        "backward",
        [VMEM] * (len(part) + 4) + [AFTER],
        [shape(keys, LANES)]
        + [shape(len(numbers) * BLOCK, KV_COLS, dtype=kind) for numbers, kind in splits],
        [
            pltpu.VMEM((keys, 2 * HEAD_DIM), bf16),
            pltpu.VMEM((2, keys, TILE), f32),
            pltpu.VMEM((HEAD_DIM, LANES), bf16),
            pltpu.VMEM((HEAD_DIM, LANES), bf16),
        ],
        flops=6 * keys * LANES * HEAD_DIM,
    )(*kvs, raised, q_aug, cot_aug, gains, after)


def rows_of(turned_rows):
    rows = turned_rows.T
    return jnp.concatenate(
        [rows[g * TOKENS : (g + 1) * TOKENS] for g in range(GROUP)], axis=1
    )


def finish_kernel(*refs):
    refs = list(refs)
    kv_lists = [[refs.pop(0) for _ in part] for part in all_parts]
    all_slopes = [refs.pop(0) for _ in all_parts]
    (kv_own, kv_recv, raised, q_aug, cot_aug, gains, out, after) = refs[:8]
    (own_result, sib_result, keys) = refs[8:]
    spans, start = [], 0
    for kvs, part in zip(kv_lists, all_parts):
        span = slice(start, start + keys_in(part))
        keys[:, span] = part_rows(kvs, part, key_cols).T
        spans.append(span)
        start = span.stop
    for j in (2, 3, 0, 1):
        lanes = lanes_of(j)
        sib, resp = j // 2, j % 2
        result = sib_result if sib else own_result
        total = None
        for chunk, slopes in enumerate(all_slopes):
            part = dot(keys[:, spans[chunk]], slopes[:, lanes])
            part = part * (gains[chunk : chunk + 1, lanes] * score_scale)
            total = part if total is None else total + part
        if resp:
            gain = gains[3:4, lanes]
            rows = (kv_recv if sib else kv_own)[TOKENS:BLOCK]
            own_raised = raised[:, lanes_of(sib)]
            moved = dot(value_aug_of(rows[:, HEAD_DIM:]), cot_aug[:, lanes])
            own_slopes = (own_raised.astype(f32) * moved).astype(bf16)
            total = total + dot(rows[:, :HEAD_DIM].T, own_slopes) * (gain * score_scale)
            scaled_q = (q_aug[:HEAD_DIM, lanes].astype(f32) * (gain * score_scale)).astype(bf16)
            scaled_cot = (cot_aug[:HEAD_DIM, lanes].astype(f32) * gain).astype(bf16)
            key_grad = dot(own_slopes, scaled_q, 1, 1)
            value_grad = dot(own_raised, scaled_cot, 1, 1)
            result[:, 4 * Q_COLS :] = jnp.concatenate([key_grad, value_grad], axis=1).astype(bf16)
        result[:, resp * Q_COLS : (resp + 1) * Q_COLS] = rows_of(
            out[:, lanes].astype(f32)
        ).astype(bf16)
        result[:, (2 + resp) * Q_COLS : (3 + resp) * Q_COLS] = rows_of(total).astype(bf16)


def finish(kv_lists, slopes, kv_own, kv_recv, raised, q_aug, cot_aug, gains, out, after):
    flat = [kv for kvs in kv_lists for kv in kvs]
    return call(
        finish_kernel,
        "finish",
        [VMEM] * (len(flat) + len(slopes) + 7) + [AFTER],
        [shape(TOKENS, 4 * Q_COLS + KV_COLS)] * 2,
        [pltpu.VMEM((HEAD_DIM, 16 * BLOCK), bf16)],
        flops=6 * 4 * BLOCK * LANES * HEAD_DIM,
    )(*flat, *slopes, kv_own, kv_recv, raised, q_aug, cot_aug, gains, out, after)


def place_kernel(own, recv, prompt_out, resp_out, prompt_dq, resp_dq, resp_dkv, done, sems):
    pairs = []
    core = here()[0]
    for side, source in ((core, own), (1 - core, recv)):
        cols = columns(side, Q_COLS)
        targets = (
            prompt_out.at[:, cols],
            resp_out.at[0, :, cols],
            prompt_dq.at[:, cols],
            resp_dq.at[0, :, cols],
        )
        pairs += [
            (source.at[:, pl.ds(n * Q_COLS, Q_COLS)], target) for n, target in enumerate(targets)
        ]
        pairs.append(
            (source.at[:, pl.ds(4 * Q_COLS, KV_COLS)], resp_dkv.at[0, :, columns(side, KV_COLS)])
        )
    copies = started(pairs, sems)
    done[...] = jnp.zeros_like(done)
    waited(copies)


def place(own, recv):
    prompt = shape(TOKENS, 2 * Q_COLS)
    resp = shape(1, TOKENS, 2 * Q_COLS)
    return call(
        place_kernel,
        "place",
        [VMEM] * 2,
        [prompt, resp, prompt, resp, shape(1, TOKENS, 2 * KV_COLS), shape(8, 128, dtype=f32)],
        [pltpu.SemaphoreType.DMA((10,))],
        out_specs=[HBM] * 5 + [VMEM],
    )(own, recv)


def add_split_kernel(count, *refs):
    terms, outs = refs[:count], refs[count + 1 :]
    start = 0
    for out in outs:
        rows = slice(start, start + out.shape[0])
        total = terms[0][rows].astype(f32)
        for term in terms[1:]:
            total = total + term[rows].astype(f32)
        out[...] = total.astype(out.dtype)
        start += out.shape[0]


def add_split(terms, outs, rows, after, flops=0):
    return call(
        functools.partial(add_split_kernel, len(terms)),
        "add_split",
        [VMEM] * len(terms) + [AFTER],
        [shape(rows, KV_COLS)] * outs,
        flops=flops,
    )(*terms, after)


def sum_column_kernel(grad_z, back_far, back_1, back_2, after, to_1, to_2, to_3):
    for p, out in ((1, to_1), (2, to_2), (3, to_3)):
        rows = slice((p - 1) * BLOCK, p * BLOCK)
        total = grad_z[rows]
        for back in (back_far, back_1, back_2):
            total = total + back[rows].astype(f32)
        out[...] = total.astype(bf16)


def sum_column(*operands):
    return call(
        sum_column_kernel, "sum_column", [VMEM] * 4 + [AFTER], [shape(BLOCK, KV_COLS)] * 3
    )(*operands)


def gate_kernel(value, after, out):
    out[...] = value[...]


def gate(value, after):
    return call(gate_kernel, "gate", [VMEM, AFTER], shape(*value.shape))(value, after)


def last_kernel(kept, recv, after, out):
    core = here()[0]

    @pl.when(core == 0)
    def _():
        out[:, :KV_COLS] = kept[...]
        out[:, KV_COLS:] = recv[...]

    @pl.when(core == 1)
    def _():
        out[:, :KV_COLS] = recv[...]
        out[:, KV_COLS:] = kept[...]


def last(kept, recv, after):
    return call(
        last_kernel, "last", [VMEM] * 2 + [AFTER], shape(TOKENS, 2 * KV_COLS)
    )(kept, recv, after)


def shards(
    prompt_q,
    prompt_kv,
    resp_q,
    resp_kv,
    prompt_grad,
    resp_grad,
    resp_len,
    logratio,
    partner,
    chosen,
):
    prompt_q, prompt_kv, resp_q, resp_kv, prompt_grad, resp_grad = [
        pltpu.with_memory_space_constraint(array, pltpu.HBM)
        for array in (prompt_q, prompt_kv, resp_q, resp_kv, prompt_grad, resp_grad)
    ]
    kv_own, kv_send, q_send = pack(
        prompt_kv, resp_kv, prompt_q, resp_q, prompt_grad, resp_grad
    )
    kv_recv = swap_core(kv_send)
    q_recv = swap_core(q_send)
    block = join_cores(logratio, kv_own, kv_recv, q_recv)

    from_x = [shift_x(block, 4 - offset) for offset in offsets[1:3]]
    from_z = [shift_z(block, p) for p in (1, 2, 3)]
    q_aug, grads, raised_own, part_own = prep(
        prompt_q, resp_q, prompt_grad, resp_grad, q_recv, kv_own, kv_recv
    )
    note = facts(partner, chosen, resp_len, part_own)
    near = join(from_x, note, *from_z)
    far = join(from_z[1:], note, from_z[0], near)
    column = join([block] + from_z, note, near)
    early_kvs = [block] + from_z + [near]
    side_kvs = [shift_z(near, 1)] + [shift_x(far, 4 - offset) for offset in offsets[1:3]]
    far_kvs = [shift_x(column, 2)]
    kv_lists = [early_kvs, side_kvs, far_kvs]

    early = forward(early_kvs, q_aug, part_own, early_part)
    far_ones = forward(far_kvs, q_aug, early[0], far_part)
    side = forward(side_kvs, q_aug, far_ones[0], side_part)
    raised, packs = zip(early, side, far_ones)
    own_notes = collect(note, kv_lists, far_ones[0])
    out, cot_aug, gains = combine(
        own_notes, swap_core(own_notes), grads, [*packs, part_own]
    )

    def backward_of(chunk, splits, after):
        return backward(
            kv_lists[chunk],
            raised[chunk],
            q_aug,
            cot_aug,
            gains,
            after,
            all_parts[chunk],
            chunk,
            splits,
        )

    slopes_far, grad_far, grad_x3 = backward_of(
        2, (((1, 2, 3), bf16), ((0,), bf16)), gains
    )
    back_far = shift_x(grad_far, 2)
    slopes_side, grad_1, grad_2 = backward_of(
        1, (((0, 2, 3), bf16), ((1, 4, 5), bf16)), grad_far
    )
    back_1, back_2 = shift_x(grad_1, offsets[1]), shift_x(grad_2, offsets[2])
    slopes_early, grad_own, grad_z, *to_x = backward_of(
        0, (((0,), f32), ((1, 2, 3), f32), ((4,), bf16), ((5,), bf16)), grad_1
    )
    slopes = [slopes_early, slopes_side, slopes_far]

    to_x3 = gate(grad_x3, back_far)
    back_x = [
        shift_x(term, offset) for term, offset in zip((*to_x, to_x3), offsets[1:])
    ]
    to_z = sum_column(grad_z, back_far, back_1, back_2, to_x3)
    back_z = [shift_z(term, 4 - p) for p, term in zip((1, 2, 3), to_z)]
    own_result, sib_result = finish(
        kv_lists, slopes, kv_own, kv_recv, raised_own, q_aug, cot_aug, gains, out, grad_own
    )
    prompt_out, resp_out, prompt_dq, resp_dq, resp_dkv, placed = place(
        own_result, swap_core(sib_result)
    )
    kept, sent = add_split([grad_own] + back_z + back_x, 2, TOKENS, grad_own, 2 * 10**10)
    prompt_dkv = last(kept, swap_core(sent), placed)
    return (prompt_out, resp_out, prompt_dq, resp_dq, prompt_dkv, resp_dkv)


def solution(mesh):
    return jax.shard_map(
        shards,
        mesh=mesh,
        in_specs=(
            P(("batch", "resp"), "head"),
            P(("batch", "resp"), "head"),
            P(("batch", "resp"), None, "head"),
            P(("batch", "resp"), None, "head"),
            P(("batch", "resp"), "head"),
            P(("batch", "resp"), None, "head"),
            P(("batch", "resp")),
            P(("batch", "resp")),
            P(("batch", "resp")),
            P(("batch", "resp")),
        ),
        out_specs=(
            P(("batch", "resp"), "head"),
            P(("batch", "resp"), None, "head"),
            P(("batch", "resp"), "head"),
            P(("batch", "resp"), None, "head"),
            P(("batch", "resp"), "head"),
            P(("batch", "resp"), None, "head"),
        ),
        check_vma=False,
    )
```

```python
import functools

import jax
import jax.numpy as jnp
from jax import lax
from jax.experimental import pallas as pl
from jax.experimental.pallas import tpu as pltpu
from jax.sharding import PartitionSpec as P

HEAD_DIM = 128
GROUP = 8
TOKENS = 64
KV_COLS = 2 * HEAD_DIM
Q_COLS = GROUP * HEAD_DIM
BLOCK = 2 * TOKENS
NOTE = 16
PIECE = BLOCK + NOTE
TILE = GROUP * TOKENS
LANES = 4 * TILE
SUBS = LANES // TILE

score_scale = HEAD_DIM ** (-0.5)
exp2_scale = score_scale * 1.4426950408889634
pair_beta = 0.1
blocked_score = -(2.0**30)
no_max = -(2.0**31)

bf16 = jnp.bfloat16
f32 = jnp.float32


def params(**kw):
    return pltpu.CompilerParams(vmem_limit_bytes=16 * 2**20, **kw)


def dot(left, right, left_dim=1, right_dim=0):
    return lax.dot_general(
        left, right, (((left_dim,), (right_dim,)), ((), ())), preferred_element_type=f32
    )


def iota(shape, dim):
    return lax.broadcasted_iota(jnp.int32, shape, dim)


VMEM = pl.BlockSpec(memory_space=pltpu.VMEM)
SMEM = pl.BlockSpec(memory_space=pltpu.SMEM)
HBM = pl.BlockSpec(memory_space=pltpu.HBM)
AFTER = pl.BlockSpec(memory_space=pl.ANY)


def shape(*dims, dtype=bf16):
    return jax.ShapeDtypeStruct(dims, dtype)


def call(kernel, name, in_specs, out_shape, scratch=(), out_specs=None, flops=0):
    extra = {} if out_specs is None else {"out_specs": out_specs}
    cost = pl.CostEstimate(flops=flops, bytes_accessed=2**20, transcendentals=0)
    return pl.pallas_call(
        kernel,
        in_specs=in_specs,
        out_shape=out_shape,
        scratch_shapes=list(scratch),
        compiler_params=params(),
        cost_estimate=cost,
        name=name,
        **extra,
    )


def lanes_of(j):
    return slice(j * TILE, (j + 1) * TILE)


def swap_core(value):
    return lax.ppermute(value, "resp", [(r, r ^ 1) for r in range(32)])


def shift_z(value, step):
    pairs = [(r, ((r // 8 + step) % 4) * 8 + r % 8) for r in range(32)]
    return lax.ppermute(value, "resp", pairs)


def shift_x(value, step):
    pairs = [(r, (r // 8) * 8 + (r % 8 // 2 + step) % 4 * 2 + r % 2) for r in range(32)]
    return lax.ppermute(value, "resp", pairs)


def here():
    index = lax.axis_index("resp")
    return lax.rem(index, 2), lax.div(index, 8), lax.rem(lax.div(index, 2), 4)


def columns(core, width):
    return pl.ds(pl.multiple_of(core * width, width), width)


def run_copies(pairs, sems):
    copies = [pltpu.make_async_copy(a, b, sems.at[i]) for i, (a, b) in enumerate(pairs)]
    for copy in copies:
        copy.start()
    for copy in copies:
        copy.wait()


def columns(core, width):
    return pl.ds(pl.multiple_of(core * width, width), width)


def started(pairs, sems):
    copies = [pltpu.make_async_copy(a, b, sems.at[i]) for i, (a, b) in enumerate(pairs)]
    for copy in copies:
        copy.start()
    return copies


def waited(copies):
    for copy in copies:
        copy.wait()


def half_copies(side, pq, rq, pg, rg, target):
    cols = columns(side, Q_COLS)
    return [
        (pq.at[:, cols], target.at[0]),
        (rq.at[0, :, cols], target.at[1]),
        (pg.at[:, cols], target.at[2]),
        (rg.at[0, :, cols], target.at[3]),
    ]


def pack_kv_kernel(prompt_kv, resp_kv, own, send, sems):
    core = here()[0]
    pairs = []
    for side, out in ((core, own), (1 - core, send)):
        cols = columns(side, KV_COLS)
        pairs.append((prompt_kv.at[:, cols], out.at[pl.ds(0, TOKENS)]))
        pairs.append((resp_kv.at[0, :, cols], out.at[pl.ds(TOKENS, TOKENS)]))
    waited(started(pairs, sems))


def pack_kv(prompt_kv, resp_kv):
    return call(
        pack_kv_kernel,
        "pack_kv",
        [HBM] * 2,
        [shape(BLOCK, KV_COLS)] * 2,
        [pltpu.SemaphoreType.DMA((4,))],
    )(prompt_kv, resp_kv)


def pack_q_kernel(pq, rq, pg, rg, after, send, sems):
    waited(started(half_copies(1 - here()[0], pq, rq, pg, rg, send), sems))


def pack_q(prompt_q, resp_q, prompt_grad, resp_grad, after):
    return call(
        pack_q_kernel,
        "pack_q",
        [HBM] * 4 + [AFTER],
        shape(4, TOKENS, Q_COLS),
        [pltpu.SemaphoreType.DMA((4,))],
    )(prompt_q, resp_q, prompt_grad, resp_grad, after)


def note_of(core, first, values):
    row, lane = iota((NOTE, KV_COLS), 0), iota((NOTE, KV_COLS), 1)
    note = jnp.zeros((NOTE, KV_COLS), f32)
    for number, value in enumerate(values):
        note = jnp.where(lane == core * 8 + first + number, value, note)
    return jnp.where(row == 0, note, 0.0).astype(bf16)


def join_cores_kernel(logratio, own, recv, after, block):
    block[:TOKENS] = own[:TOKENS]
    block[TOKENS:BLOCK] = recv[:TOKENS]
    ratio = jnp.full((NOTE, KV_COLS), logratio[0], f32)
    high = ratio.astype(bf16).astype(f32)
    middle = (ratio - high).astype(bf16).astype(f32)
    block[BLOCK:] = note_of(here()[0], 0, (high, middle, ratio - high - middle))


def join_cores(logratio, own, recv, after):
    return call(
        join_cores_kernel,
        "join_cores",
        [SMEM] + [VMEM] * 2 + [AFTER],
        shape(PIECE, KV_COLS),
        flops=2 * 10**10,
    )(logratio, own, recv, after)


def facts_kernel(partner, chosen, resp_len, after, note):
    values = [ref[0].astype(f32) for ref in (partner, chosen, resp_len)]
    note[...] = note_of(here()[0], 3, values)


def facts(partner, chosen, resp_len, after):
    return call(facts_kernel, "facts", [SMEM] * 3 + [AFTER], shape(NOTE, KV_COLS))(
        partner, chosen, resp_len, after
    )


def join_kernel(count, *refs):
    pieces, chunk = refs[:count], refs[-1]
    for p, piece in enumerate(pieces):
        chunk[p * PIECE : (p + 1) * PIECE] = piece[...]


def join(pieces, *afters):
    return call(
        functools.partial(join_kernel, len(pieces)),
        "join",
        [VMEM] * len(pieces) + [AFTER] * len(afters),
        shape(len(pieces) * PIECE, KV_COLS),
    )(*pieces, *afters)


def turned(block):
    rows = jnp.concatenate(
        [block[:, g * HEAD_DIM : (g + 1) * HEAD_DIM] for g in range(GROUP)], axis=0
    )
    return rows.T


def softmax_part(scores, value_rows):
    top = jnp.max(scores, axis=0, keepdims=True)
    raised = jnp.exp2((scores - top) * exp2_scale).astype(bf16)
    total = dot(value_rows, raised)
    packed = jnp.concatenate(
        [total[: HEAD_DIM + 8], jnp.broadcast_to(top, (8, top.shape[1]))], axis=0
    )
    return raised, packed


def with_ones(value_rows):
    return jnp.concatenate([value_rows.T, jnp.ones((16, value_rows.shape[0]), bf16)], axis=0)


def prep_kernel(
    pq, rq, pg, rg, recv, kv_own, kv_recv, q_aug, grads, raised, packed, local, sems
):
    core = here()[0]
    copies = started(half_copies(core, pq, rq, pg, rg, local), sems)
    none = jnp.concatenate(
        [jnp.zeros((HEAD_DIM + 8, TILE), f32), jnp.full((8, TILE), no_max, f32)], axis=0
    )
    for j in (2, 3, 0, 1):
        lanes = lanes_of(j)
        sib, resp = j // 2, j % 2
        if j == 0:
            waited(copies)
        source = recv if sib else local
        turned_q = turned(source[resp])
        q_aug[:HEAD_DIM, lanes] = turned_q
        grads[:, lanes] = turned(source[2 + resp])
        if resp:
            q_aug[HEAD_DIM:, lanes] = jnp.zeros((HEAD_DIM, TILE), bf16)
            rows = (kv_recv if sib else kv_own)[TOKENS:BLOCK]
            scores = dot(rows[:, :HEAD_DIM], turned_q)
            token = iota(scores.shape, 1) % TOKENS
            scores = jnp.where(iota(scores.shape, 0) <= token, scores, blocked_score)
            part, info_rows = softmax_part(scores, with_ones(rows[:, HEAD_DIM:]))
            raised[:, lanes_of(sib)] = part
            packed[:, lanes] = info_rows
        else:
            own_core = 1 - core if sib else core
            token = iota((HEAD_DIM, TILE), 1) % TOKENS + own_core * TOKENS
            row = iota((HEAD_DIM, TILE), 0)
            hidden = jnp.logical_or(row == 0, row > token)
            q_aug[HEAD_DIM:, lanes] = jnp.where(hidden, blocked_score, 0.0).astype(bf16)
            packed[:, lanes] = none


def prep(prompt_q, resp_q, prompt_grad, resp_grad, recv, kv_own, kv_recv):
    return call(
        prep_kernel,
        "prep",
        [HBM] * 4 + [VMEM] * 3,
        [
            shape(2 * HEAD_DIM, LANES),
            shape(HEAD_DIM, LANES),
            shape(TOKENS, 2 * TILE),
            shape(HEAD_DIM + 16, LANES, dtype=f32),
        ],
        [pltpu.VMEM((4, TOKENS, Q_COLS), bf16), pltpu.SemaphoreType.DMA((4,))],
    )(prompt_q, resp_q, prompt_grad, resp_grad, recv, kv_own, kv_recv)


offsets = (0, 3, 1, 2)
early_part = (((0, 0),), ((1, 0),), ((2, 0),), ((3, 0),), ((0, 1), (0, 2)))
side_part = (((1, 1), (1, 2)), ((2, 1), (3, 1)), ((2, 2), (3, 2)))
far_part = (((0, 3), (1, 3), (2, 3), (3, 3)),)
all_parts = (early_part, side_part, far_part)
key_cols = slice(0, HEAD_DIM)
value_cols = slice(HEAD_DIM, KV_COLS)


def blocks_of(part):
    return [block for array in part for block in array]


def keys_in(part):
    return BLOCK * len(blocks_of(part))


def part_rows(kvs, part, cols):
    return jnp.concatenate(
        [
            kv[n * PIECE : n * PIECE + BLOCK, cols]
            for kv, array in zip(kvs, part)
            for n in range(len(array))
        ],
        axis=0,
    )


def place_of(info, block):
    p, i = block
    return (info[1] + 4 - p) % 4, (info[2] + offsets[i]) % 4


def forward_kernel(part, has_top, *refs):
    kvs = refs[: len(part)]
    q_aug, given, raised, packed, key_aug, value_rows, tops = refs[len(part) :]
    info = here()
    core, z_own, x_own = info
    row = iota((BLOCK, HEAD_DIM), 1)
    token = (iota((BLOCK, HEAD_DIM), 0) + core * TOKENS) % BLOCK
    first = (row == 0).astype(f32)
    same = jnp.logical_and(row == token, row > 0).astype(f32)
    number = 0
    for kv, array in zip(kvs, part):
        for n, block in enumerate(array):
            rows = slice(number * BLOCK, (number + 1) * BLOCK)
            z_here, x_here = place_of(info, block)
            later = jnp.logical_or(
                z_here > z_own, jnp.logical_and(z_here == z_own, x_here > x_own)
            )
            hidden = first * later.astype(f32)
            if block == (0, 0):
                hidden = same
            key_aug[rows, :HEAD_DIM] = kv[n * PIECE : n * PIECE + BLOCK, key_cols]
            key_aug[rows, HEAD_DIM:] = hidden.astype(bf16)
            number += 1
    value_rows[...] = with_ones(part_rows(kvs, part, value_cols))

    def find_tops():
        for j in range(SUBS):
            lanes = lanes_of(j)
            top = jnp.max(dot(key_aug[...], q_aug[:, lanes]), axis=0, keepdims=True)
            tops[:, lanes] = jnp.broadcast_to(top, (8, TILE))

    def weigh():
        for j in range(SUBS):
            lanes = lanes_of(j)
            scores = dot(key_aug[...], q_aug[:, lanes])
            raised[:, lanes] = jnp.exp2((scores - tops[0:1, lanes]) * exp2_scale).astype(bf16)
        total = dot(value_rows[...], raised[...])
        packed[: HEAD_DIM + 8] = total[: HEAD_DIM + 8]
        packed[HEAD_DIM + 8 :] = tops[...]

    if not has_top:
        find_tops()
        weigh()
        return
    tops[...] = given[HEAD_DIM + 8 :]
    weigh()
    largest = jnp.max(packed[HEAD_DIM : HEAD_DIM + 1, :])

    @pl.when(jnp.logical_not(largest < 2.0**40))
    def _():
        find_tops()
        weigh()


def forward(kvs, q_aug, given, part):
    keys = keys_in(part)
    has_top = part is not early_part
    return call(
        functools.partial(forward_kernel, part, has_top),
        "forward",
        [VMEM] * (len(part) + 1) + [VMEM if has_top else AFTER],
        [
            shape(keys, LANES),
            shape(HEAD_DIM + 16, LANES, dtype=f32),
        ],
        [
            pltpu.VMEM((keys, 2 * HEAD_DIM), bf16),
            pltpu.VMEM((HEAD_DIM + 16, keys), bf16),
            pltpu.VMEM((8, LANES), f32),
        ],
        flops=4 * keys * LANES * HEAD_DIM,
    )(*kvs, q_aug, given)


def collect_kernel(*refs):
    note, *refs = refs
    refs, notes = list(refs[:-2]), refs[-1]
    rows = []
    for part in all_parts:
        for array in part:
            kv = refs.pop(0)
            for n in range(len(array)):
                rows.append(kv[n * PIECE + BLOCK : (n + 1) * PIECE].astype(f32)[0:1])
    notes[...] = (jnp.concatenate(rows, axis=0) + note[...].astype(f32)).astype(bf16)


def collect(note, kv_lists, after):
    flat = [kv for kvs in kv_lists for kv in kvs]
    return call(
        collect_kernel, "collect", [VMEM] * (len(flat) + 1) + [AFTER], shape(16, KV_COLS)
    )(note, *flat, after)


def combine_kernel(
    own_notes, sib_notes, grads, part_0, part_1, part_2, part_own, out, cot_aug, gains
):
    info = here()
    notes = own_notes[...].astype(f32) + sib_notes[...].astype(f32)
    row = iota((16, 1), 0)
    seat = jnp.zeros_like(row)
    for number, block in enumerate(block for part in all_parts for block in blocks_of(part)):
        z_here, x_here = place_of(info, block)
        seat = jnp.where(row == number, z_here * 8 + x_here * 2, seat)
    ratios = [
        notes[:, side * 8 : side * 8 + 1]
        + notes[:, side * 8 + 1 : side * 8 + 2]
        + notes[:, side * 8 + 2 : side * 8 + 3]
        for side in range(2)
    ]
    weights = []
    for sib in range(2):
        own_core = 1 - info[0] if sib else info[0]
        own_row = notes[0:1, :]
        lane = iota(own_row.shape, 1)

        def field(number):
            mask = lane == own_core * 8 + number
            return jnp.sum(jnp.where(mask, own_row, 0.0), axis=1, keepdims=True)

        ratio = field(0) + field(1) + field(2)
        partner, chosen, count = field(3), field(4), field(5)
        mate = jnp.zeros((1, 1), f32)
        for side in range(2):
            found = (seat + side).astype(f32) == partner
            mate = mate + jnp.sum(jnp.where(found, ratios[side], 0.0), axis=0, keepdims=True)
        sign = 2.0 * chosen - 1.0
        pair_weight = sign * jax.nn.sigmoid(-pair_beta * (sign * (ratio - mate)))
        token = (iota((1, TILE), 1) % TOKENS).astype(f32)
        weights.append(jnp.where(token < count, pair_weight, 0.0))

    for j in range(SUBS):
        lanes = lanes_of(j)
        parts = (part_0, part_1, part_2) + ((part_own,) if j % 2 else ())
        tops = [part[HEAD_DIM + 8 : HEAD_DIM + 9, lanes] for part in parts]
        top = functools.reduce(jnp.maximum, tops)
        factors = [jnp.exp2((one - top) * exp2_scale) for one in tops]
        length = sum(f * part[HEAD_DIM : HEAD_DIM + 1, lanes] for f, part in zip(factors, parts))
        inverse = 1.0 / length
        factors = [f * inverse for f in factors]
        rounded = sum(f * part[:HEAD_DIM, lanes] for f, part in zip(factors, parts)).astype(bf16)
        out[:, lanes] = rounded
        gains[:, lanes] = jnp.concatenate(
            factors + [jnp.zeros((8 - len(factors), TILE), f32)], axis=0
        )
        if j % 2:
            cot = (weights[j // 2] * grads[:, lanes].astype(f32)).astype(bf16)
        else:
            cot = grads[:, lanes]
        cot_aug[:HEAD_DIM, lanes] = cot
        row_dot = -jnp.sum(cot.astype(f32) * rounded.astype(f32), axis=0, keepdims=True)
        high = row_dot.astype(bf16).astype(f32)
        middle = (row_dot - high).astype(bf16).astype(f32)
        low = row_dot - high - middle
        row = iota((16, TILE), 0)
        split = jnp.where(
            row == 0, high, jnp.where(row == 1, middle, jnp.where(row == 2, low, 0.0))
        )
        cot_aug[HEAD_DIM : HEAD_DIM + 16, lanes] = split.astype(bf16)
        cot_aug[HEAD_DIM + 16 :, lanes] = jnp.zeros((HEAD_DIM - 16, TILE), bf16)


def combine(own_notes, sib_notes, grads, parts):
    return call(
        combine_kernel,
        "combine",
        [VMEM] * (3 + len(parts)),
        [shape(HEAD_DIM, LANES), shape(2 * HEAD_DIM, LANES), shape(8, LANES, dtype=f32)],
    )(own_notes, sib_notes, grads, *parts)


def value_aug_of(value_rows):
    column = iota(value_rows.shape, 1)
    return jnp.concatenate([value_rows, (column < 3).astype(f32).astype(bf16)], axis=1)


def backward_kernel(part, splits, chunk, *refs):
    kvs = refs[: len(part)]
    raised, q_aug, cot_aug, gains, after, slopes = refs[len(part) : len(part) + 6]
    grads = refs[len(part) + 6 : len(part) + 6 + len(splits)]
    value_aug, moved, scaled_q, scaled_cot = refs[len(part) + 6 + len(splits) :]
    value_aug[...] = value_aug_of(part_rows(kvs, part, value_cols))
    moved[0] = dot(value_aug[...], cot_aug[:, lanes_of(0)])
    for j in range(SUBS):
        lanes = lanes_of(j)
        if j + 1 < SUBS:
            moved[(j + 1) % 2] = dot(value_aug[...], cot_aug[:, lanes_of(j + 1)])
        gain = gains[chunk : chunk + 1, lanes]
        scaled_cot[:, lanes] = (cot_aug[:HEAD_DIM, lanes].astype(f32) * gain).astype(bf16)
        scaled_q[:, lanes] = (
            q_aug[:HEAD_DIM, lanes].astype(f32) * (gain * score_scale)
        ).astype(bf16)
        slopes[:, lanes] = (raised[:, lanes].astype(f32) * moved[j % 2]).astype(bf16)
    for columns_here, left, right in (
        (value_cols, raised, scaled_cot),
        (key_cols, slopes, scaled_q),
    ):
        total = dot(left[...], right[...], 1, 1)
        for grad, (numbers, _) in zip(grads, splits):
            for n, number in enumerate(numbers):
                grad[n * BLOCK : (n + 1) * BLOCK, columns_here] = total[
                    number * BLOCK : (number + 1) * BLOCK
                ].astype(grad.dtype)


def backward(kvs, raised, q_aug, cot_aug, gains, after, part, chunk, splits):
    keys = keys_in(part)
    return call(
        functools.partial(backward_kernel, part, splits, chunk),
        "backward",
        [VMEM] * (len(part) + 4) + [AFTER],
        [shape(keys, LANES)]
        + [shape(len(numbers) * BLOCK, KV_COLS, dtype=kind) for numbers, kind in splits],
        [
            pltpu.VMEM((keys, 2 * HEAD_DIM), bf16),
            pltpu.VMEM((2, keys, TILE), f32),
            pltpu.VMEM((HEAD_DIM, LANES), bf16),
            pltpu.VMEM((HEAD_DIM, LANES), bf16),
        ],
        flops=6 * keys * LANES * HEAD_DIM,
    )(*kvs, raised, q_aug, cot_aug, gains, after)


def rows_of(turned_rows):
    rows = turned_rows.T
    return jnp.concatenate(
        [rows[g * TOKENS : (g + 1) * TOKENS] for g in range(GROUP)], axis=1
    )


def finish_kernel(*refs):
    refs = list(refs)
    kv_lists = [[refs.pop(0) for _ in part] for part in all_parts]
    all_slopes = [refs.pop(0) for _ in all_parts]
    (kv_own, kv_recv, raised, q_aug, cot_aug, gains, out, after) = refs[:8]
    (own_result, sib_result, keys) = refs[8:]
    spans, start = [], 0
    for kvs, part in zip(kv_lists, all_parts):
        span = slice(start, start + keys_in(part))
        keys[:, span] = part_rows(kvs, part, key_cols).T
        spans.append(span)
        start = span.stop
    for j in (2, 3, 0, 1):
        lanes = lanes_of(j)
        sib, resp = j // 2, j % 2
        result = sib_result if sib else own_result
        total = None
        for chunk, slopes in enumerate(all_slopes):
            part = dot(keys[:, spans[chunk]], slopes[:, lanes])
            part = part * (gains[chunk : chunk + 1, lanes] * score_scale)
            total = part if total is None else total + part
        if resp:
            gain = gains[3:4, lanes]
            rows = (kv_recv if sib else kv_own)[TOKENS:BLOCK]
            own_raised = raised[:, lanes_of(sib)]
            moved = dot(value_aug_of(rows[:, HEAD_DIM:]), cot_aug[:, lanes])
            own_slopes = (own_raised.astype(f32) * moved).astype(bf16)
            total = total + dot(rows[:, :HEAD_DIM].T, own_slopes) * (gain * score_scale)
            scaled_q = (q_aug[:HEAD_DIM, lanes].astype(f32) * (gain * score_scale)).astype(bf16)
            scaled_cot = (cot_aug[:HEAD_DIM, lanes].astype(f32) * gain).astype(bf16)
            key_grad = dot(own_slopes, scaled_q, 1, 1)
            value_grad = dot(own_raised, scaled_cot, 1, 1)
            result[:, 4 * Q_COLS :] = jnp.concatenate([key_grad, value_grad], axis=1).astype(bf16)
        result[:, resp * Q_COLS : (resp + 1) * Q_COLS] = rows_of(
            out[:, lanes].astype(f32)
        ).astype(bf16)
        result[:, (2 + resp) * Q_COLS : (3 + resp) * Q_COLS] = rows_of(total).astype(bf16)


def finish(kv_lists, slopes, kv_own, kv_recv, raised, q_aug, cot_aug, gains, out, after):
    flat = [kv for kvs in kv_lists for kv in kvs]
    return call(
        finish_kernel,
        "finish",
        [VMEM] * (len(flat) + len(slopes) + 7) + [AFTER],
        [shape(TOKENS, 4 * Q_COLS + KV_COLS)] * 2,
        [pltpu.VMEM((HEAD_DIM, 16 * BLOCK), bf16)],
        flops=6 * 4 * BLOCK * LANES * HEAD_DIM,
    )(*flat, *slopes, kv_own, kv_recv, raised, q_aug, cot_aug, gains, out, after)


def place_kernel(own, recv, prompt_out, resp_out, prompt_dq, resp_dq, resp_dkv, done, sems):
    pairs = []
    core = here()[0]
    for side, source in ((core, own), (1 - core, recv)):
        cols = columns(side, Q_COLS)
        targets = (
            prompt_out.at[:, cols],
            resp_out.at[0, :, cols],
            prompt_dq.at[:, cols],
            resp_dq.at[0, :, cols],
        )
        pairs += [
            (source.at[:, pl.ds(n * Q_COLS, Q_COLS)], target) for n, target in enumerate(targets)
        ]
        pairs.append(
            (source.at[:, pl.ds(4 * Q_COLS, KV_COLS)], resp_dkv.at[0, :, columns(side, KV_COLS)])
        )
    copies = started(pairs, sems)
    done[...] = jnp.zeros_like(done)
    waited(copies)


def place(own, recv):
    prompt = shape(TOKENS, 2 * Q_COLS)
    resp = shape(1, TOKENS, 2 * Q_COLS)
    return call(
        place_kernel,
        "place",
        [VMEM] * 2,
        [prompt, resp, prompt, resp, shape(1, TOKENS, 2 * KV_COLS), shape(8, 128, dtype=f32)],
        [pltpu.SemaphoreType.DMA((10,))],
        out_specs=[HBM] * 5 + [VMEM],
    )(own, recv)


def add_split_kernel(count, *refs):
    terms, outs = refs[:count], refs[count + 1 :]
    start = 0
    for out in outs:
        rows = slice(start, start + out.shape[0])
        total = terms[0][rows].astype(f32)
        for term in terms[1:]:
            total = total + term[rows].astype(f32)
        out[...] = total.astype(out.dtype)
        start += out.shape[0]


def add_split(terms, outs, rows, after, flops=0):
    return call(
        functools.partial(add_split_kernel, len(terms)),
        "add_split",
        [VMEM] * len(terms) + [AFTER],
        [shape(rows, KV_COLS)] * outs,
        flops=flops,
    )(*terms, after)


def sum_column_kernel(grad_z, back_far, back_1, back_2, after, to_1, to_2, to_3):
    for p, out in ((1, to_1), (2, to_2), (3, to_3)):
        rows = slice((p - 1) * BLOCK, p * BLOCK)
        total = grad_z[rows]
        for back in (back_far, back_1, back_2):
            total = total + back[rows].astype(f32)
        out[...] = total.astype(bf16)


def sum_column(*operands):
    return call(
        sum_column_kernel, "sum_column", [VMEM] * 4 + [AFTER], [shape(BLOCK, KV_COLS)] * 3
    )(*operands)


def gate_kernel(value, after, out):
    out[...] = value[...]


def gate(value, after):
    return call(gate_kernel, "gate", [VMEM, AFTER], shape(*value.shape))(value, after)


def last_kernel(kept, recv, after, out):
    core = here()[0]

    @pl.when(core == 0)
    def _():
        out[:, :KV_COLS] = kept[...]
        out[:, KV_COLS:] = recv[...]

    @pl.when(core == 1)
    def _():
        out[:, :KV_COLS] = recv[...]
        out[:, KV_COLS:] = kept[...]


def last(kept, recv, after):
    return call(
        last_kernel, "last", [VMEM] * 2 + [AFTER], shape(TOKENS, 2 * KV_COLS)
    )(kept, recv, after)


def shards(
    prompt_q,
    prompt_kv,
    resp_q,
    resp_kv,
    prompt_grad,
    resp_grad,
    resp_len,
    logratio,
    partner,
    chosen,
):
    prompt_q, prompt_kv, resp_q, resp_kv, prompt_grad, resp_grad = [
        pltpu.with_memory_space_constraint(array, pltpu.HBM)
        for array in (prompt_q, prompt_kv, resp_q, resp_kv, prompt_grad, resp_grad)
    ]
    kv_own, kv_send = pack_kv(prompt_kv, resp_kv)
    kv_recv = swap_core(kv_send)
    q_send = pack_q(prompt_q, resp_q, prompt_grad, resp_grad, kv_send)
    q_recv = swap_core(q_send)
    block = join_cores(logratio, kv_own, kv_recv, q_send)

    from_x = [shift_x(block, 4 - offset) for offset in offsets[1:3]]
    from_z = [shift_z(block, p) for p in (1, 2, 3)]
    q_aug, grads, raised_own, part_own = prep(
        prompt_q, resp_q, prompt_grad, resp_grad, q_recv, kv_own, kv_recv
    )
    note = facts(partner, chosen, resp_len, part_own)
    near = join(from_x, note, *from_z)
    far = join(from_z[1:], note, from_z[0], near)
    column = join([block] + from_z, note, near)
    early_kvs = [block] + from_z + [near]
    side_kvs = [shift_z(near, 1)] + [shift_x(far, 4 - offset) for offset in offsets[1:3]]
    far_kvs = [shift_x(column, 2)]
    kv_lists = [early_kvs, side_kvs, far_kvs]

    early = forward(early_kvs, q_aug, part_own, early_part)
    far_ones = forward(far_kvs, q_aug, early[1], far_part)
    side = forward(side_kvs, q_aug, far_ones[1], side_part)
    raised, packs = zip(early, side, far_ones)
    own_notes = collect(note, kv_lists, far_ones[0])
    out, cot_aug, gains = combine(
        own_notes, swap_core(own_notes), grads, [*packs, part_own]
    )

    def backward_of(chunk, splits, after):
        return backward(
            kv_lists[chunk],
            raised[chunk],
            q_aug,
            cot_aug,
            gains,
            after,
            all_parts[chunk],
            chunk,
            splits,
        )

    slopes_far, grad_far, grad_x3 = backward_of(
        2, (((1, 2, 3), bf16), ((0,), bf16)), gains
    )
    back_far = shift_x(grad_far, 2)
    slopes_side, grad_1, grad_2 = backward_of(
        1, (((0, 2, 3), bf16), ((1, 4, 5), bf16)), grad_far
    )
    back_1, back_2 = shift_x(grad_1, offsets[1]), shift_x(grad_2, offsets[2])
    slopes_early, grad_own, grad_z, *to_x = backward_of(
        0, (((0,), f32), ((1, 2, 3), f32), ((4,), bf16), ((5,), bf16)), grad_1
    )
    slopes = [slopes_early, slopes_side, slopes_far]

    to_x3 = gate(grad_x3, back_far)
    back_x = [
        shift_x(term, offset) for term, offset in zip((*to_x, to_x3), offsets[1:])
    ]
    to_z = sum_column(grad_z, back_far, back_1, back_2, to_x3)
    back_z = [shift_z(term, 4 - p) for p, term in zip((1, 2, 3), to_z)]
    own_result, sib_result = finish(
        kv_lists, slopes, kv_own, kv_recv, raised_own, q_aug, cot_aug, gains, out, grad_own
    )
    prompt_out, resp_out, prompt_dq, resp_dq, resp_dkv, placed = place(
        own_result, swap_core(sib_result)
    )
    kept, sent = add_split([grad_own] + back_z + back_x, 2, TOKENS, grad_own, 2 * 10**10)
    prompt_dkv = last(kept, swap_core(sent), placed)
    return (prompt_out, resp_out, prompt_dq, resp_dq, prompt_dkv, resp_dkv)


def solution(mesh):
    return jax.shard_map(
        shards,
        mesh=mesh,
        in_specs=(
            P(("batch", "resp"), "head"),
            P(("batch", "resp"), "head"),
            P(("batch", "resp"), None, "head"),
            P(("batch", "resp"), None, "head"),
            P(("batch", "resp"), "head"),
            P(("batch", "resp"), None, "head"),
            P(("batch", "resp")),
            P(("batch", "resp")),
            P(("batch", "resp")),
            P(("batch", "resp")),
        ),
        out_specs=(
            P(("batch", "resp"), "head"),
            P(("batch", "resp"), None, "head"),
            P(("batch", "resp"), "head"),
            P(("batch", "resp"), None, "head"),
            P(("batch", "resp"), "head"),
            P(("batch", "resp"), None, "head"),
        ),
        check_vma=False,
    )
```

```python
import functools

import jax
import jax.numpy as jnp
from jax import lax
from jax.experimental import pallas as pl
from jax.experimental.pallas import tpu as pltpu
from jax.sharding import PartitionSpec as P

HEAD_DIM = 128
GROUP = 8
TOKENS = 64
KV_COLS = 2 * HEAD_DIM
Q_COLS = GROUP * HEAD_DIM
BLOCK = 2 * TOKENS
NOTE = 16
PIECE = BLOCK + NOTE
TILE = GROUP * TOKENS
LANES = 4 * TILE
SUBS = LANES // TILE

score_scale = HEAD_DIM ** (-0.5)
exp2_scale = score_scale * 1.4426950408889634
pair_beta = 0.1
blocked_score = -(2.0**30)
no_max = -(2.0**31)

bf16 = jnp.bfloat16
f32 = jnp.float32


def params(**kw):
    return pltpu.CompilerParams(vmem_limit_bytes=16 * 2**20, **kw)


def dot(left, right, left_dim=1, right_dim=0):
    return lax.dot_general(
        left, right, (((left_dim,), (right_dim,)), ((), ())), preferred_element_type=f32
    )


def iota(shape, dim):
    return lax.broadcasted_iota(jnp.int32, shape, dim)


VMEM = pl.BlockSpec(memory_space=pltpu.VMEM)
SMEM = pl.BlockSpec(memory_space=pltpu.SMEM)
HBM = pl.BlockSpec(memory_space=pltpu.HBM)
AFTER = pl.BlockSpec(memory_space=pl.ANY)


def shape(*dims, dtype=bf16):
    return jax.ShapeDtypeStruct(dims, dtype)


def call(kernel, name, in_specs, out_shape, scratch=(), out_specs=None, flops=0):
    extra = {} if out_specs is None else {"out_specs": out_specs}
    cost = pl.CostEstimate(flops=flops, bytes_accessed=2**20, transcendentals=0)
    return pl.pallas_call(
        kernel,
        in_specs=in_specs,
        out_shape=out_shape,
        scratch_shapes=list(scratch),
        compiler_params=params(),
        cost_estimate=cost,
        name=name,
        **extra,
    )


def lanes_of(j):
    return slice(j * TILE, (j + 1) * TILE)


def swap_core(value):
    return lax.ppermute(value, "resp", [(r, r ^ 1) for r in range(32)])


def shift_z(value, step):
    pairs = [(r, ((r // 8 + step) % 4) * 8 + r % 8) for r in range(32)]
    return lax.ppermute(value, "resp", pairs)


def shift_x(value, step):
    pairs = [(r, (r // 8) * 8 + (r % 8 // 2 + step) % 4 * 2 + r % 2) for r in range(32)]
    return lax.ppermute(value, "resp", pairs)


def here():
    index = lax.axis_index("resp")
    return lax.rem(index, 2), lax.div(index, 8), lax.rem(lax.div(index, 2), 4)


def columns(core, width):
    return pl.ds(pl.multiple_of(core * width, width), width)


def run_copies(pairs, sems):
    copies = [pltpu.make_async_copy(a, b, sems.at[i]) for i, (a, b) in enumerate(pairs)]
    for copy in copies:
        copy.start()
    for copy in copies:
        copy.wait()


def columns(core, width):
    return pl.ds(pl.multiple_of(core * width, width), width)


def started(pairs, sems):
    copies = [pltpu.make_async_copy(a, b, sems.at[i]) for i, (a, b) in enumerate(pairs)]
    for copy in copies:
        copy.start()
    return copies


def waited(copies):
    for copy in copies:
        copy.wait()


def half_copies(side, pq, rq, pg, rg, target):
    cols = columns(side, Q_COLS)
    return [
        (pq.at[:, cols], target.at[0]),
        (rq.at[0, :, cols], target.at[1]),
        (pg.at[:, cols], target.at[2]),
        (rg.at[0, :, cols], target.at[3]),
    ]


def pack_kv_kernel(prompt_kv, resp_kv, own, send, sems):
    core = here()[0]
    pairs = []
    for side, out in ((core, own), (1 - core, send)):
        cols = columns(side, KV_COLS)
        pairs.append((prompt_kv.at[:, cols], out.at[pl.ds(0, TOKENS)]))
        pairs.append((resp_kv.at[0, :, cols], out.at[pl.ds(TOKENS, TOKENS)]))
    waited(started(pairs, sems))


def pack_kv(prompt_kv, resp_kv):
    return call(
        pack_kv_kernel,
        "pack_kv",
        [HBM] * 2,
        [shape(BLOCK, KV_COLS)] * 2,
        [pltpu.SemaphoreType.DMA((4,))],
    )(prompt_kv, resp_kv)


def pack_q_kernel(pq, rq, pg, rg, after, send, sems):
    waited(started(half_copies(1 - here()[0], pq, rq, pg, rg, send), sems))


def pack_q(prompt_q, resp_q, prompt_grad, resp_grad, after):
    return call(
        pack_q_kernel,
        "pack_q",
        [HBM] * 4 + [AFTER],
        shape(4, TOKENS, Q_COLS),
        [pltpu.SemaphoreType.DMA((4,))],
    )(prompt_q, resp_q, prompt_grad, resp_grad, after)


def note_of(core, first, values):
    row, lane = iota((NOTE, KV_COLS), 0), iota((NOTE, KV_COLS), 1)
    note = jnp.zeros((NOTE, KV_COLS), f32)
    for number, value in enumerate(values):
        note = jnp.where(lane == core * 8 + first + number, value, note)
    return jnp.where(row == 0, note, 0.0).astype(bf16)


def join_cores_kernel(logratio, own, recv, after, block):
    block[:TOKENS] = own[:TOKENS]
    block[TOKENS:BLOCK] = recv[:TOKENS]
    ratio = jnp.full((NOTE, KV_COLS), logratio[0], f32)
    high = ratio.astype(bf16).astype(f32)
    middle = (ratio - high).astype(bf16).astype(f32)
    block[BLOCK:] = note_of(here()[0], 0, (high, middle, ratio - high - middle))


def join_cores(logratio, own, recv, after):
    return call(
        join_cores_kernel,
        "join_cores",
        [SMEM] + [VMEM] * 2 + [AFTER],
        shape(PIECE, KV_COLS),
        flops=2 * 10**10,
    )(logratio, own, recv, after)


def facts_kernel(partner, chosen, resp_len, after, note):
    values = [ref[0].astype(f32) for ref in (partner, chosen, resp_len)]
    note[...] = note_of(here()[0], 3, values)


def facts(partner, chosen, resp_len, after):
    return call(facts_kernel, "facts", [SMEM] * 3 + [AFTER], shape(NOTE, KV_COLS))(
        partner, chosen, resp_len, after
    )


def join_kernel(count, *refs):
    pieces, chunk = refs[:count], refs[-1]
    for p, piece in enumerate(pieces):
        chunk[p * PIECE : (p + 1) * PIECE] = piece[...]


def join(pieces, *afters):
    return call(
        functools.partial(join_kernel, len(pieces)),
        "join",
        [VMEM] * len(pieces) + [AFTER] * len(afters),
        shape(len(pieces) * PIECE, KV_COLS),
    )(*pieces, *afters)


def turned(block):
    rows = jnp.concatenate(
        [block[:, g * HEAD_DIM : (g + 1) * HEAD_DIM] for g in range(GROUP)], axis=0
    )
    return rows.T


def softmax_part(scores, value_rows):
    top = jnp.max(scores, axis=0, keepdims=True)
    raised = jnp.exp2((scores - top) * exp2_scale).astype(bf16)
    total = dot(value_rows, raised)
    packed = jnp.concatenate(
        [total[: HEAD_DIM + 8], jnp.broadcast_to(top, (8, top.shape[1]))], axis=0
    )
    return raised, packed


def with_ones(value_rows):
    return jnp.concatenate([value_rows.T, jnp.ones((16, value_rows.shape[0]), bf16)], axis=0)


def prep_kernel(
    pq, rq, pg, rg, recv, kv_own, kv_recv, q_aug, grads, raised, packed, local, sems
):
    core = here()[0]
    copies = started(half_copies(core, pq, rq, pg, rg, local), sems)
    none = jnp.concatenate(
        [jnp.zeros((HEAD_DIM + 8, TILE), f32), jnp.full((8, TILE), no_max, f32)], axis=0
    )
    for j in (2, 3, 0, 1):
        lanes = lanes_of(j)
        sib, resp = j // 2, j % 2
        if j == 0:
            waited(copies)
        source = recv if sib else local
        turned_q = turned(source[resp])
        q_aug[:HEAD_DIM, lanes] = turned_q
        grads[:, lanes] = turned(source[2 + resp])
        if resp:
            q_aug[HEAD_DIM:, lanes] = jnp.zeros((HEAD_DIM, TILE), bf16)
            rows = (kv_recv if sib else kv_own)[TOKENS:BLOCK]
            scores = dot(rows[:, :HEAD_DIM], turned_q)
            token = iota(scores.shape, 1) % TOKENS
            scores = jnp.where(iota(scores.shape, 0) <= token, scores, blocked_score)
            part, info_rows = softmax_part(scores, with_ones(rows[:, HEAD_DIM:]))
            raised[:, lanes_of(sib)] = part
            packed[:, lanes] = info_rows
        else:
            own_core = 1 - core if sib else core
            token = iota((HEAD_DIM, TILE), 1) % TOKENS + own_core * TOKENS
            row = iota((HEAD_DIM, TILE), 0)
            hidden = jnp.logical_or(row == 0, row > token)
            q_aug[HEAD_DIM:, lanes] = jnp.where(hidden, blocked_score, 0.0).astype(bf16)
            packed[:, lanes] = none


def prep(prompt_q, resp_q, prompt_grad, resp_grad, recv, kv_own, kv_recv):
    return call(
        prep_kernel,
        "prep",
        [HBM] * 4 + [VMEM] * 3,
        [
            shape(2 * HEAD_DIM, LANES),
            shape(HEAD_DIM, LANES),
            shape(TOKENS, 2 * TILE),
            shape(HEAD_DIM + 16, LANES, dtype=f32),
        ],
        [pltpu.VMEM((4, TOKENS, Q_COLS), bf16), pltpu.SemaphoreType.DMA((4,))],
    )(prompt_q, resp_q, prompt_grad, resp_grad, recv, kv_own, kv_recv)


offsets = (0, 3, 1, 2)
early_part = (((0, 0),), ((1, 0),), ((2, 0),), ((3, 0),), ((0, 1), (0, 2)))
side_part = (((1, 1), (1, 2)), ((2, 1), (3, 1)), ((2, 2), (3, 2)))
far_part = (((0, 3), (1, 3), (2, 3), (3, 3)),)
all_parts = (early_part, side_part, far_part)
key_cols = slice(0, HEAD_DIM)
value_cols = slice(HEAD_DIM, KV_COLS)


def blocks_of(part):
    return [block for array in part for block in array]


def keys_in(part):
    return BLOCK * len(blocks_of(part))


def part_rows(kvs, part, cols):
    return jnp.concatenate(
        [
            kv[n * PIECE : n * PIECE + BLOCK, cols]
            for kv, array in zip(kvs, part)
            for n in range(len(array))
        ],
        axis=0,
    )


def place_of(info, block):
    p, i = block
    return (info[1] + 4 - p) % 4, (info[2] + offsets[i]) % 4


def forward_kernel(part, has_top, *refs):
    kvs = refs[: len(part)]
    q_aug, given, raised, packed, key_aug, value_rows, tops = refs[len(part) :]
    info = here()
    core, z_own, x_own = info
    row = iota((BLOCK, HEAD_DIM), 1)
    token = (iota((BLOCK, HEAD_DIM), 0) + core * TOKENS) % BLOCK
    first = (row == 0).astype(f32)
    same = jnp.logical_and(row == token, row > 0).astype(f32)
    number = 0
    for kv, array in zip(kvs, part):
        for n, block in enumerate(array):
            rows = slice(number * BLOCK, (number + 1) * BLOCK)
            z_here, x_here = place_of(info, block)
            later = jnp.logical_or(
                z_here > z_own, jnp.logical_and(z_here == z_own, x_here > x_own)
            )
            hidden = first * later.astype(f32)
            if block == (0, 0):
                hidden = same
            key_aug[rows, :HEAD_DIM] = kv[n * PIECE : n * PIECE + BLOCK, key_cols]
            key_aug[rows, HEAD_DIM:] = hidden.astype(bf16)
            number += 1
    value_rows[...] = with_ones(part_rows(kvs, part, value_cols))

    def find_tops():
        for j in range(SUBS):
            lanes = lanes_of(j)
            top = jnp.max(dot(key_aug[...], q_aug[:, lanes]), axis=0, keepdims=True)
            tops[:, lanes] = jnp.broadcast_to(top, (8, TILE))

    def weigh():
        for j in range(SUBS):
            lanes = lanes_of(j)
            scores = dot(key_aug[...], q_aug[:, lanes])
            raised[:, lanes] = jnp.exp2((scores - tops[0:1, lanes]) * exp2_scale).astype(bf16)
        total = dot(value_rows[...], raised[...])
        packed[: HEAD_DIM + 8] = total[: HEAD_DIM + 8]
        packed[HEAD_DIM + 8 :] = tops[...]

    if not has_top:
        find_tops()
        weigh()
        return
    tops[...] = given[HEAD_DIM + 8 :]
    weigh()
    largest = jnp.max(packed[HEAD_DIM : HEAD_DIM + 1, :])

    @pl.when(jnp.logical_not(largest < 2.0**40))
    def _():
        find_tops()
        weigh()


def forward(kvs, q_aug, given, part):
    keys = keys_in(part)
    has_top = part is not early_part
    return call(
        functools.partial(forward_kernel, part, has_top),
        "forward",
        [VMEM] * (len(part) + 1) + [VMEM if has_top else AFTER],
        [
            shape(keys, LANES),
            shape(HEAD_DIM + 16, LANES, dtype=f32),
        ],
        [
            pltpu.VMEM((keys, 2 * HEAD_DIM), bf16),
            pltpu.VMEM((HEAD_DIM + 16, keys), bf16),
            pltpu.VMEM((8, LANES), f32),
        ],
        flops=4 * keys * LANES * HEAD_DIM,
    )(*kvs, q_aug, given)


def collect_kernel(*refs):
    note, *refs = refs
    refs, notes = list(refs[:-2]), refs[-1]
    rows = []
    for part in all_parts:
        for array in part:
            kv = refs.pop(0)
            for n in range(len(array)):
                rows.append(kv[n * PIECE + BLOCK : (n + 1) * PIECE].astype(f32)[0:1])
    notes[...] = (jnp.concatenate(rows, axis=0) + note[...].astype(f32)).astype(bf16)


def collect(note, kv_lists, after):
    flat = [kv for kvs in kv_lists for kv in kvs]
    return call(
        collect_kernel, "collect", [VMEM] * (len(flat) + 1) + [AFTER], shape(16, KV_COLS)
    )(note, *flat, after)


def combine_kernel(
    own_notes, sib_notes, grads, part_0, part_1, part_2, part_own, out, cot_aug, gains
):
    info = here()
    notes = own_notes[...].astype(f32) + sib_notes[...].astype(f32)
    row = iota((16, 1), 0)
    seat = jnp.zeros_like(row)
    for number, block in enumerate(block for part in all_parts for block in blocks_of(part)):
        z_here, x_here = place_of(info, block)
        seat = jnp.where(row == number, z_here * 8 + x_here * 2, seat)
    ratios = [
        notes[:, side * 8 : side * 8 + 1]
        + notes[:, side * 8 + 1 : side * 8 + 2]
        + notes[:, side * 8 + 2 : side * 8 + 3]
        for side in range(2)
    ]
    weights = []
    for sib in range(2):
        own_core = 1 - info[0] if sib else info[0]
        own_row = notes[0:1, :]
        lane = iota(own_row.shape, 1)

        def field(number):
            mask = lane == own_core * 8 + number
            return jnp.sum(jnp.where(mask, own_row, 0.0), axis=1, keepdims=True)

        ratio = field(0) + field(1) + field(2)
        partner, chosen, count = field(3), field(4), field(5)
        mate = jnp.zeros((1, 1), f32)
        for side in range(2):
            found = (seat + side).astype(f32) == partner
            mate = mate + jnp.sum(jnp.where(found, ratios[side], 0.0), axis=0, keepdims=True)
        sign = 2.0 * chosen - 1.0
        pair_weight = sign * jax.nn.sigmoid(-pair_beta * (sign * (ratio - mate)))
        token = (iota((1, TILE), 1) % TOKENS).astype(f32)
        weights.append(jnp.where(token < count, pair_weight, 0.0))

    for j in range(SUBS):
        lanes = lanes_of(j)
        parts = (part_0, part_1, part_2) + ((part_own,) if j % 2 else ())
        tops = [part[HEAD_DIM + 8 : HEAD_DIM + 9, lanes] for part in parts]
        top = functools.reduce(jnp.maximum, tops)
        factors = [jnp.exp2((one - top) * exp2_scale) for one in tops]
        length = sum(f * part[HEAD_DIM : HEAD_DIM + 1, lanes] for f, part in zip(factors, parts))
        inverse = 1.0 / length
        factors = [f * inverse for f in factors]
        rounded = sum(f * part[:HEAD_DIM, lanes] for f, part in zip(factors, parts)).astype(bf16)
        out[:, lanes] = rounded
        gains[:, lanes] = jnp.concatenate(
            factors + [jnp.zeros((8 - len(factors), TILE), f32)], axis=0
        )
        if j % 2:
            cot = (weights[j // 2] * grads[:, lanes].astype(f32)).astype(bf16)
        else:
            cot = grads[:, lanes]
        cot_aug[:HEAD_DIM, lanes] = cot
        row_dot = -jnp.sum(cot.astype(f32) * rounded.astype(f32), axis=0, keepdims=True)
        high = row_dot.astype(bf16).astype(f32)
        middle = (row_dot - high).astype(bf16).astype(f32)
        low = row_dot - high - middle
        row = iota((16, TILE), 0)
        split = jnp.where(
            row == 0, high, jnp.where(row == 1, middle, jnp.where(row == 2, low, 0.0))
        )
        cot_aug[HEAD_DIM : HEAD_DIM + 16, lanes] = split.astype(bf16)
        cot_aug[HEAD_DIM + 16 :, lanes] = jnp.zeros((HEAD_DIM - 16, TILE), bf16)


def combine(own_notes, sib_notes, grads, parts):
    return call(
        combine_kernel,
        "combine",
        [VMEM] * (3 + len(parts)),
        [shape(HEAD_DIM, LANES), shape(2 * HEAD_DIM, LANES), shape(8, LANES, dtype=f32)],
    )(own_notes, sib_notes, grads, *parts)


def value_aug_of(value_rows):
    column = iota(value_rows.shape, 1)
    return jnp.concatenate([value_rows, (column < 3).astype(f32).astype(bf16)], axis=1)


def backward_kernel(part, splits, chunk, *refs):
    kvs = refs[: len(part)]
    raised, q_aug, cot_aug, gains, after, slopes = refs[len(part) : len(part) + 6]
    grads = refs[len(part) + 6 : len(part) + 6 + len(splits)]
    value_aug, scaled_q, scaled_cot = refs[len(part) + 6 + len(splits) :]
    value_aug[...] = value_aug_of(part_rows(kvs, part, value_cols))
    for j in range(SUBS):
        lanes = lanes_of(j)
        gain = gains[chunk : chunk + 1, lanes]
        scaled_cot[:, lanes] = (cot_aug[:HEAD_DIM, lanes].astype(f32) * gain).astype(bf16)
        scaled_q[:, lanes] = (
            q_aug[:HEAD_DIM, lanes].astype(f32) * (gain * score_scale)
        ).astype(bf16)
        moved = dot(value_aug[...], cot_aug[:, lanes])
        slopes[:, lanes] = (raised[:, lanes].astype(f32) * moved).astype(bf16)
    for columns_here, left, right in (
        (value_cols, raised, scaled_cot),
        (key_cols, slopes, scaled_q),
    ):
        total = dot(left[...], right[...], 1, 1)
        for grad, (numbers, _) in zip(grads, splits):
            for n, number in enumerate(numbers):
                grad[n * BLOCK : (n + 1) * BLOCK, columns_here] = total[
                    number * BLOCK : (number + 1) * BLOCK
                ].astype(grad.dtype)


def backward(kvs, raised, q_aug, cot_aug, gains, after, part, chunk, splits):
    keys = keys_in(part)
    return call(
        functools.partial(backward_kernel, part, splits, chunk),
        "backward",
        [VMEM] * (len(part) + 4) + [AFTER],
        [shape(keys, LANES)]
        + [shape(len(numbers) * BLOCK, KV_COLS, dtype=kind) for numbers, kind in splits],
        [
            pltpu.VMEM((keys, 2 * HEAD_DIM), bf16),
            pltpu.VMEM((HEAD_DIM, LANES), bf16),
            pltpu.VMEM((HEAD_DIM, LANES), bf16),
        ],
        flops=6 * keys * LANES * HEAD_DIM,
    )(*kvs, raised, q_aug, cot_aug, gains, after)


def rows_of(turned_rows):
    rows = turned_rows.T
    return jnp.concatenate(
        [rows[g * TOKENS : (g + 1) * TOKENS] for g in range(GROUP)], axis=1
    )


def finish_kernel(*refs):
    refs = list(refs)
    kv_lists = [[refs.pop(0) for _ in part] for part in all_parts]
    all_slopes = [refs.pop(0) for _ in all_parts]
    (kv_own, kv_recv, raised, q_aug, cot_aug, gains, out, after) = refs[:8]
    (own_result, sib_result, keys) = refs[8:]
    spans, start = [], 0
    for kvs, part in zip(kv_lists, all_parts):
        span = slice(start, start + keys_in(part))
        keys[:, span] = part_rows(kvs, part, key_cols).T
        spans.append(span)
        start = span.stop
    for j in (2, 3, 0, 1):
        lanes = lanes_of(j)
        sib, resp = j // 2, j % 2
        result = sib_result if sib else own_result
        total = None
        for chunk, slopes in enumerate(all_slopes):
            part = dot(keys[:, spans[chunk]], slopes[:, lanes])
            part = part * (gains[chunk : chunk + 1, lanes] * score_scale)
            total = part if total is None else total + part
        if resp:
            gain = gains[3:4, lanes]
            rows = (kv_recv if sib else kv_own)[TOKENS:BLOCK]
            own_raised = raised[:, lanes_of(sib)]
            moved = dot(value_aug_of(rows[:, HEAD_DIM:]), cot_aug[:, lanes])
            own_slopes = (own_raised.astype(f32) * moved).astype(bf16)
            total = total + dot(rows[:, :HEAD_DIM].T, own_slopes) * (gain * score_scale)
            scaled_q = (q_aug[:HEAD_DIM, lanes].astype(f32) * (gain * score_scale)).astype(bf16)
            scaled_cot = (cot_aug[:HEAD_DIM, lanes].astype(f32) * gain).astype(bf16)
            key_grad = dot(own_slopes, scaled_q, 1, 1)
            value_grad = dot(own_raised, scaled_cot, 1, 1)
            result[:, 4 * Q_COLS :] = jnp.concatenate([key_grad, value_grad], axis=1).astype(bf16)
        result[:, resp * Q_COLS : (resp + 1) * Q_COLS] = rows_of(
            out[:, lanes].astype(f32)
        ).astype(bf16)
        result[:, (2 + resp) * Q_COLS : (3 + resp) * Q_COLS] = rows_of(total).astype(bf16)


def finish(kv_lists, slopes, kv_own, kv_recv, raised, q_aug, cot_aug, gains, out, after):
    flat = [kv for kvs in kv_lists for kv in kvs]
    return call(
        finish_kernel,
        "finish",
        [VMEM] * (len(flat) + len(slopes) + 7) + [AFTER],
        [shape(TOKENS, 4 * Q_COLS + KV_COLS)] * 2,
        [pltpu.VMEM((HEAD_DIM, 16 * BLOCK), bf16)],
        flops=6 * 4 * BLOCK * LANES * HEAD_DIM,
    )(*flat, *slopes, kv_own, kv_recv, raised, q_aug, cot_aug, gains, out, after)


def place_kernel(own, recv, prompt_out, resp_out, prompt_dq, resp_dq, resp_dkv, done, sems):
    pairs = []
    core = here()[0]
    for side, source in ((core, own), (1 - core, recv)):
        cols = columns(side, Q_COLS)
        targets = (
            prompt_out.at[:, cols],
            resp_out.at[0, :, cols],
            prompt_dq.at[:, cols],
            resp_dq.at[0, :, cols],
        )
        pairs += [
            (source.at[:, pl.ds(n * Q_COLS, Q_COLS)], target) for n, target in enumerate(targets)
        ]
        pairs.append(
            (source.at[:, pl.ds(4 * Q_COLS, KV_COLS)], resp_dkv.at[0, :, columns(side, KV_COLS)])
        )
    copies = started(pairs, sems)
    done[...] = jnp.zeros_like(done)
    waited(copies)


def place(own, recv):
    prompt = shape(TOKENS, 2 * Q_COLS)
    resp = shape(1, TOKENS, 2 * Q_COLS)
    return call(
        place_kernel,
        "place",
        [VMEM] * 2,
        [prompt, resp, prompt, resp, shape(1, TOKENS, 2 * KV_COLS), shape(8, 128, dtype=f32)],
        [pltpu.SemaphoreType.DMA((10,))],
        out_specs=[HBM] * 5 + [VMEM],
    )(own, recv)


def add_split_kernel(count, *refs):
    terms, outs = refs[:count], refs[count + 1 :]
    start = 0
    for out in outs:
        rows = slice(start, start + out.shape[0])
        total = terms[0][rows].astype(f32)
        for term in terms[1:]:
            total = total + term[rows].astype(f32)
        out[...] = total.astype(out.dtype)
        start += out.shape[0]


def add_split(terms, outs, rows, after, flops=0):
    return call(
        functools.partial(add_split_kernel, len(terms)),
        "add_split",
        [VMEM] * len(terms) + [AFTER],
        [shape(rows, KV_COLS)] * outs,
        flops=flops,
    )(*terms, after)


def sum_column_kernel(grad_z, back_far, back_1, back_2, after, to_1, to_2, to_3):
    for p, out in ((1, to_1), (2, to_2), (3, to_3)):
        rows = slice((p - 1) * BLOCK, p * BLOCK)
        total = grad_z[rows]
        for back in (back_far, back_1, back_2):
            total = total + back[rows].astype(f32)
        out[...] = total.astype(bf16)


def sum_column(*operands):
    return call(
        sum_column_kernel, "sum_column", [VMEM] * 4 + [AFTER], [shape(BLOCK, KV_COLS)] * 3
    )(*operands)


def gate_kernel(value, after, out):
    out[...] = value[...]


def gate(value, after):
    return call(gate_kernel, "gate", [VMEM, AFTER], shape(*value.shape))(value, after)


def last_kernel(kept, recv, after, out):
    core = here()[0]

    @pl.when(core == 0)
    def _():
        out[:, :KV_COLS] = kept[...]
        out[:, KV_COLS:] = recv[...]

    @pl.when(core == 1)
    def _():
        out[:, :KV_COLS] = recv[...]
        out[:, KV_COLS:] = kept[...]


def last(kept, recv, after):
    return call(
        last_kernel, "last", [VMEM] * 2 + [AFTER], shape(TOKENS, 2 * KV_COLS)
    )(kept, recv, after)


def shards(
    prompt_q,
    prompt_kv,
    resp_q,
    resp_kv,
    prompt_grad,
    resp_grad,
    resp_len,
    logratio,
    partner,
    chosen,
):
    prompt_q, prompt_kv, resp_q, resp_kv, prompt_grad, resp_grad = [
        pltpu.with_memory_space_constraint(array, pltpu.HBM)
        for array in (prompt_q, prompt_kv, resp_q, resp_kv, prompt_grad, resp_grad)
    ]
    kv_own, kv_send = pack_kv(prompt_kv, resp_kv)
    kv_recv = swap_core(kv_send)
    q_send = pack_q(prompt_q, resp_q, prompt_grad, resp_grad, kv_send)
    q_recv = swap_core(q_send)
    block = join_cores(logratio, kv_own, kv_recv, q_send)

    block_again = gate(block, q_recv)
    from_x = [shift_x(block_again, 4 - offset) for offset in offsets[1:3]]
    from_z = [shift_z(block, p) for p in (1, 2, 3)]
    q_aug, grads, raised_own, part_own = prep(
        prompt_q, resp_q, prompt_grad, resp_grad, q_recv, kv_own, kv_recv
    )
    note = facts(partner, chosen, resp_len, part_own)
    near = join(from_x, note, *from_z)
    far = join(from_z[1:], note, from_z[0], near)
    column = join([block] + from_z, note, near)
    early_kvs = [block] + from_z + [near]
    side_kvs = [shift_z(near, 1)] + [shift_x(far, 4 - offset) for offset in offsets[1:3]]
    far_kvs = [shift_x(column, 2)]
    kv_lists = [early_kvs, side_kvs, far_kvs]

    early = forward(early_kvs, q_aug, part_own, early_part)
    far_ones = forward(far_kvs, q_aug, early[1], far_part)
    side = forward(side_kvs, q_aug, far_ones[1], side_part)
    raised, packs = zip(early, side, far_ones)
    own_notes = collect(note, kv_lists, far_ones[0])
    out, cot_aug, gains = combine(
        own_notes, swap_core(own_notes), grads, [*packs, part_own]
    )

    def backward_of(chunk, splits, after):
        return backward(
            kv_lists[chunk],
            raised[chunk],
            q_aug,
            cot_aug,
            gains,
            after,
            all_parts[chunk],
            chunk,
            splits,
        )

    slopes_far, grad_far, grad_x3 = backward_of(
        2, (((1, 2, 3), bf16), ((0,), bf16)), gains
    )
    back_far = shift_x(grad_far, 2)
    slopes_side, grad_1, grad_2 = backward_of(
        1, (((0, 2, 3), bf16), ((1, 4, 5), bf16)), grad_far
    )
    back_1, back_2 = shift_x(grad_1, offsets[1]), shift_x(grad_2, offsets[2])
    slopes_early, grad_own, grad_z, *to_x = backward_of(
        0, (((0,), f32), ((1, 2, 3), f32), ((4,), bf16), ((5,), bf16)), grad_1
    )
    slopes = [slopes_early, slopes_side, slopes_far]

    to_x3 = gate(grad_x3, back_far)
    back_x = [
        shift_x(term, offset) for term, offset in zip((*to_x, to_x3), offsets[1:])
    ]
    to_z = sum_column(grad_z, back_far, back_1, back_2, to_x3)
    back_z = [shift_z(term, 4 - p) for p, term in zip((1, 2, 3), to_z)]
    own_result, sib_result = finish(
        kv_lists, slopes, kv_own, kv_recv, raised_own, q_aug, cot_aug, gains, out, grad_own
    )
    prompt_out, resp_out, prompt_dq, resp_dq, resp_dkv, placed = place(
        own_result, swap_core(sib_result)
    )
    kept, sent = add_split([grad_own] + back_z + back_x, 2, TOKENS, grad_own, 2 * 10**10)
    prompt_dkv = last(kept, swap_core(sent), placed)
    return (prompt_out, resp_out, prompt_dq, resp_dq, prompt_dkv, resp_dkv)


def solution(mesh):
    return jax.shard_map(
        shards,
        mesh=mesh,
        in_specs=(
            P(("batch", "resp"), "head"),
            P(("batch", "resp"), "head"),
            P(("batch", "resp"), None, "head"),
            P(("batch", "resp"), None, "head"),
            P(("batch", "resp"), "head"),
            P(("batch", "resp"), None, "head"),
            P(("batch", "resp")),
            P(("batch", "resp")),
            P(("batch", "resp")),
            P(("batch", "resp")),
        ),
        out_specs=(
            P(("batch", "resp"), "head"),
            P(("batch", "resp"), None, "head"),
            P(("batch", "resp"), "head"),
            P(("batch", "resp"), None, "head"),
            P(("batch", "resp"), "head"),
            P(("batch", "resp"), None, "head"),
        ),
        check_vma=False,
    )
```

```python
import functools

import jax
import jax.numpy as jnp
from jax import lax
from jax.experimental import pallas as pl
from jax.experimental.pallas import tpu as pltpu
from jax.sharding import PartitionSpec as P

HEAD_DIM = 128
GROUP = 8
TOKENS = 64
KV_COLS = 2 * HEAD_DIM
Q_COLS = GROUP * HEAD_DIM
BLOCK = 2 * TOKENS
NOTE = 16
PIECE = BLOCK + NOTE
TILE = GROUP * TOKENS
LANES = 4 * TILE
SUBS = LANES // TILE

score_scale = HEAD_DIM ** (-0.5)
exp2_scale = score_scale * 1.4426950408889634
pair_beta = 0.1
blocked_score = -(2.0**30)
no_max = -(2.0**31)

bf16 = jnp.bfloat16
f32 = jnp.float32


def params(**kw):
    return pltpu.CompilerParams(vmem_limit_bytes=16 * 2**20, **kw)


def dot(left, right, left_dim=1, right_dim=0):
    return lax.dot_general(
        left, right, (((left_dim,), (right_dim,)), ((), ())), preferred_element_type=f32
    )


def iota(shape, dim):
    return lax.broadcasted_iota(jnp.int32, shape, dim)


VMEM = pl.BlockSpec(memory_space=pltpu.VMEM)
SMEM = pl.BlockSpec(memory_space=pltpu.SMEM)
HBM = pl.BlockSpec(memory_space=pltpu.HBM)
AFTER = pl.BlockSpec(memory_space=pl.ANY)


def shape(*dims, dtype=bf16):
    return jax.ShapeDtypeStruct(dims, dtype)


def call(kernel, name, in_specs, out_shape, scratch=(), out_specs=None, flops=0):
    extra = {} if out_specs is None else {"out_specs": out_specs}
    cost = pl.CostEstimate(flops=flops, bytes_accessed=2**20, transcendentals=0)
    return pl.pallas_call(
        kernel,
        in_specs=in_specs,
        out_shape=out_shape,
        scratch_shapes=list(scratch),
        compiler_params=params(),
        cost_estimate=cost,
        name=name,
        **extra,
    )


def lanes_of(j):
    return slice(j * TILE, (j + 1) * TILE)


def swap_core(value):
    return lax.ppermute(value, "resp", [(r, r ^ 1) for r in range(32)])


def shift_z(value, step):
    pairs = [(r, ((r // 8 + step) % 4) * 8 + r % 8) for r in range(32)]
    return lax.ppermute(value, "resp", pairs)


def shift_x(value, step):
    pairs = [(r, (r // 8) * 8 + (r % 8 // 2 + step) % 4 * 2 + r % 2) for r in range(32)]
    return lax.ppermute(value, "resp", pairs)


def here():
    index = lax.axis_index("resp")
    return lax.rem(index, 2), lax.div(index, 8), lax.rem(lax.div(index, 2), 4)


def columns(core, width):
    return pl.ds(pl.multiple_of(core * width, width), width)


def run_copies(pairs, sems):
    copies = [pltpu.make_async_copy(a, b, sems.at[i]) for i, (a, b) in enumerate(pairs)]
    for copy in copies:
        copy.start()
    for copy in copies:
        copy.wait()


def columns(core, width):
    return pl.ds(pl.multiple_of(core * width, width), width)


def started(pairs, sems):
    copies = [pltpu.make_async_copy(a, b, sems.at[i]) for i, (a, b) in enumerate(pairs)]
    for copy in copies:
        copy.start()
    return copies


def waited(copies):
    for copy in copies:
        copy.wait()


def half_copies(side, pq, rq, pg, rg, target):
    cols = columns(side, Q_COLS)
    return [
        (pq.at[:, cols], target.at[0]),
        (rq.at[0, :, cols], target.at[1]),
        (pg.at[:, cols], target.at[2]),
        (rg.at[0, :, cols], target.at[3]),
    ]


def pack_kv_kernel(prompt_kv, resp_kv, own, send, sems):
    core = here()[0]
    pairs = []
    for side, out in ((core, own), (1 - core, send)):
        cols = columns(side, KV_COLS)
        pairs.append((prompt_kv.at[:, cols], out.at[pl.ds(0, TOKENS)]))
        pairs.append((resp_kv.at[0, :, cols], out.at[pl.ds(TOKENS, TOKENS)]))
    waited(started(pairs, sems))


def pack_kv(prompt_kv, resp_kv):
    return call(
        pack_kv_kernel,
        "pack_kv",
        [HBM] * 2,
        [shape(BLOCK, KV_COLS)] * 2,
        [pltpu.SemaphoreType.DMA((4,))],
    )(prompt_kv, resp_kv)


def pack_q_kernel(pq, rq, pg, rg, after, send, sems):
    waited(started(half_copies(1 - here()[0], pq, rq, pg, rg, send), sems))


def pack_q(prompt_q, resp_q, prompt_grad, resp_grad, after):
    return call(
        pack_q_kernel,
        "pack_q",
        [HBM] * 4 + [AFTER],
        shape(4, TOKENS, Q_COLS),
        [pltpu.SemaphoreType.DMA((4,))],
    )(prompt_q, resp_q, prompt_grad, resp_grad, after)


def note_of(core, first, values):
    row, lane = iota((NOTE, KV_COLS), 0), iota((NOTE, KV_COLS), 1)
    note = jnp.zeros((NOTE, KV_COLS), f32)
    for number, value in enumerate(values):
        note = jnp.where(lane == core * 8 + first + number, value, note)
    return jnp.where(row == 0, note, 0.0).astype(bf16)


def join_cores_kernel(logratio, own, recv, after, block):
    block[:TOKENS] = own[:TOKENS]
    block[TOKENS:BLOCK] = recv[:TOKENS]
    ratio = jnp.full((NOTE, KV_COLS), logratio[0], f32)
    high = ratio.astype(bf16).astype(f32)
    middle = (ratio - high).astype(bf16).astype(f32)
    block[BLOCK:] = note_of(here()[0], 0, (high, middle, ratio - high - middle))


def join_cores(logratio, own, recv, after):
    return call(
        join_cores_kernel,
        "join_cores",
        [SMEM] + [VMEM] * 2 + [AFTER],
        shape(PIECE, KV_COLS),
        flops=2 * 10**10,
    )(logratio, own, recv, after)


def facts_kernel(partner, chosen, resp_len, after, note):
    values = [ref[0].astype(f32) for ref in (partner, chosen, resp_len)]
    note[...] = note_of(here()[0], 3, values)


def facts(partner, chosen, resp_len, after):
    return call(facts_kernel, "facts", [SMEM] * 3 + [AFTER], shape(NOTE, KV_COLS))(
        partner, chosen, resp_len, after
    )


def join_kernel(count, *refs):
    pieces, chunk = refs[:count], refs[-1]
    for p, piece in enumerate(pieces):
        chunk[p * PIECE : (p + 1) * PIECE] = piece[...]


def join(pieces, *afters):
    return call(
        functools.partial(join_kernel, len(pieces)),
        "join",
        [VMEM] * len(pieces) + [AFTER] * len(afters),
        shape(len(pieces) * PIECE, KV_COLS),
    )(*pieces, *afters)


def turned(block):
    rows = jnp.concatenate(
        [block[:, g * HEAD_DIM : (g + 1) * HEAD_DIM] for g in range(GROUP)], axis=0
    )
    return rows.T


def softmax_part(scores, value_rows):
    top = jnp.max(scores, axis=0, keepdims=True)
    raised = jnp.exp2((scores - top) * exp2_scale).astype(bf16)
    total = dot(value_rows, raised)
    packed = jnp.concatenate(
        [total[: HEAD_DIM + 8], jnp.broadcast_to(top, (8, top.shape[1]))], axis=0
    )
    return raised, packed


def with_ones(value_rows):
    return jnp.concatenate([value_rows.T, jnp.ones((16, value_rows.shape[0]), bf16)], axis=0)


def prep_kernel(
    pq, rq, pg, rg, recv, kv_own, kv_recv, q_aug, grads, raised, packed, local, sems
):
    core = here()[0]
    copies = started(half_copies(core, pq, rq, pg, rg, local), sems)
    none = jnp.concatenate(
        [jnp.zeros((HEAD_DIM + 8, TILE), f32), jnp.full((8, TILE), no_max, f32)], axis=0
    )
    for j in (2, 3, 0, 1):
        lanes = lanes_of(j)
        sib, resp = j // 2, j % 2
        if j == 0:
            waited(copies)
        source = recv if sib else local
        turned_q = turned(source[resp])
        q_aug[:HEAD_DIM, lanes] = turned_q
        grads[:, lanes] = turned(source[2 + resp])
        if resp:
            q_aug[HEAD_DIM:, lanes] = jnp.zeros((HEAD_DIM, TILE), bf16)
            rows = (kv_recv if sib else kv_own)[TOKENS:BLOCK]
            scores = dot(rows[:, :HEAD_DIM], turned_q)
            token = iota(scores.shape, 1) % TOKENS
            scores = jnp.where(iota(scores.shape, 0) <= token, scores, blocked_score)
            part, info_rows = softmax_part(scores, with_ones(rows[:, HEAD_DIM:]))
            raised[:, lanes_of(sib)] = part
            packed[:, lanes] = info_rows
        else:
            own_core = 1 - core if sib else core
            token = iota((HEAD_DIM, TILE), 1) % TOKENS + own_core * TOKENS
            row = iota((HEAD_DIM, TILE), 0)
            hidden = jnp.logical_or(row == 0, row > token)
            q_aug[HEAD_DIM:, lanes] = jnp.where(hidden, blocked_score, 0.0).astype(bf16)
            packed[:, lanes] = none


def prep(prompt_q, resp_q, prompt_grad, resp_grad, recv, kv_own, kv_recv):
    return call(
        prep_kernel,
        "prep",
        [HBM] * 4 + [VMEM] * 3,
        [
            shape(2 * HEAD_DIM, LANES),
            shape(HEAD_DIM, LANES),
            shape(TOKENS, 2 * TILE),
            shape(HEAD_DIM + 16, LANES, dtype=f32),
        ],
        [pltpu.VMEM((4, TOKENS, Q_COLS), bf16), pltpu.SemaphoreType.DMA((4,))],
    )(prompt_q, resp_q, prompt_grad, resp_grad, recv, kv_own, kv_recv)


offsets = (0, 3, 1, 2)
early_part = (((0, 0),), ((1, 0),), ((2, 0),), ((3, 0),), ((0, 1), (0, 2)))
side_part = (((1, 1), (1, 2)), ((2, 1), (3, 1)), ((2, 2), (3, 2)))
far_part = (((0, 3), (1, 3), (2, 3), (3, 3)),)
all_parts = (early_part, side_part, far_part)
key_cols = slice(0, HEAD_DIM)
value_cols = slice(HEAD_DIM, KV_COLS)


def blocks_of(part):
    return [block for array in part for block in array]


def keys_in(part):
    return BLOCK * len(blocks_of(part))


def part_rows(kvs, part, cols):
    return jnp.concatenate(
        [
            kv[n * PIECE : n * PIECE + BLOCK, cols]
            for kv, array in zip(kvs, part)
            for n in range(len(array))
        ],
        axis=0,
    )


def place_of(info, block):
    p, i = block
    return (info[1] + 4 - p) % 4, (info[2] + offsets[i]) % 4


def forward_kernel(part, has_top, *refs):
    kvs = refs[: len(part)]
    q_aug, given, raised, packed, key_aug, value_rows, tops = refs[len(part) :]
    info = here()
    core, z_own, x_own = info
    row = iota((BLOCK, HEAD_DIM), 1)
    token = (iota((BLOCK, HEAD_DIM), 0) + core * TOKENS) % BLOCK
    first = (row == 0).astype(f32)
    same = jnp.logical_and(row == token, row > 0).astype(f32)
    number = 0
    for kv, array in zip(kvs, part):
        for n, block in enumerate(array):
            rows = slice(number * BLOCK, (number + 1) * BLOCK)
            z_here, x_here = place_of(info, block)
            later = jnp.logical_or(
                z_here > z_own, jnp.logical_and(z_here == z_own, x_here > x_own)
            )
            hidden = first * later.astype(f32)
            if block == (0, 0):
                hidden = same
            key_aug[rows, :HEAD_DIM] = kv[n * PIECE : n * PIECE + BLOCK, key_cols]
            key_aug[rows, HEAD_DIM:] = hidden.astype(bf16)
            number += 1
    value_rows[...] = with_ones(part_rows(kvs, part, value_cols))

    def find_tops():
        for j in range(SUBS):
            lanes = lanes_of(j)
            top = jnp.max(dot(key_aug[...], q_aug[:, lanes]), axis=0, keepdims=True)
            tops[:, lanes] = jnp.broadcast_to(top, (8, TILE))

    def weigh():
        for j in range(SUBS):
            lanes = lanes_of(j)
            scores = dot(key_aug[...], q_aug[:, lanes])
            raised[:, lanes] = jnp.exp2((scores - tops[0:1, lanes]) * exp2_scale).astype(bf16)
        total = dot(value_rows[...], raised[...])
        packed[: HEAD_DIM + 8] = total[: HEAD_DIM + 8]
        packed[HEAD_DIM + 8 :] = tops[...]

    if not has_top:
        find_tops()
        weigh()
        return
    tops[...] = given[HEAD_DIM + 8 :]
    weigh()
    largest = jnp.max(packed[HEAD_DIM : HEAD_DIM + 1, :])

    @pl.when(jnp.logical_not(largest < 2.0**40))
    def _():
        find_tops()
        weigh()


def forward(kvs, q_aug, given, part):
    keys = keys_in(part)
    has_top = part is not early_part
    return call(
        functools.partial(forward_kernel, part, has_top),
        "forward",
        [VMEM] * (len(part) + 1) + [VMEM if has_top else AFTER],
        [
            shape(keys, LANES),
            shape(HEAD_DIM + 16, LANES, dtype=f32),
        ],
        [
            pltpu.VMEM((keys, 2 * HEAD_DIM), bf16),
            pltpu.VMEM((HEAD_DIM + 16, keys), bf16),
            pltpu.VMEM((8, LANES), f32),
        ],
        flops=4 * keys * LANES * HEAD_DIM,
    )(*kvs, q_aug, given)


def collect_kernel(*refs):
    note, *refs = refs
    refs, notes = list(refs[:-2]), refs[-1]
    rows = []
    for part in all_parts:
        for array in part:
            kv = refs.pop(0)
            for n in range(len(array)):
                rows.append(kv[n * PIECE + BLOCK : (n + 1) * PIECE].astype(f32)[0:1])
    notes[...] = (jnp.concatenate(rows, axis=0) + note[...].astype(f32)).astype(bf16)


def collect(note, kv_lists, after):
    flat = [kv for kvs in kv_lists for kv in kvs]
    return call(
        collect_kernel, "collect", [VMEM] * (len(flat) + 1) + [AFTER], shape(16, KV_COLS)
    )(note, *flat, after)


def combine_kernel(
    own_notes, sib_notes, grads, part_0, part_1, part_2, part_own, out, cot_aug, gains
):
    info = here()
    notes = own_notes[...].astype(f32) + sib_notes[...].astype(f32)
    row = iota((16, 1), 0)
    seat = jnp.zeros_like(row)
    for number, block in enumerate(block for part in all_parts for block in blocks_of(part)):
        z_here, x_here = place_of(info, block)
        seat = jnp.where(row == number, z_here * 8 + x_here * 2, seat)
    ratios = [
        notes[:, side * 8 : side * 8 + 1]
        + notes[:, side * 8 + 1 : side * 8 + 2]
        + notes[:, side * 8 + 2 : side * 8 + 3]
        for side in range(2)
    ]
    weights = []
    for sib in range(2):
        own_core = 1 - info[0] if sib else info[0]
        own_row = notes[0:1, :]
        lane = iota(own_row.shape, 1)

        def field(number):
            mask = lane == own_core * 8 + number
            return jnp.sum(jnp.where(mask, own_row, 0.0), axis=1, keepdims=True)

        ratio = field(0) + field(1) + field(2)
        partner, chosen, count = field(3), field(4), field(5)
        mate = jnp.zeros((1, 1), f32)
        for side in range(2):
            found = (seat + side).astype(f32) == partner
            mate = mate + jnp.sum(jnp.where(found, ratios[side], 0.0), axis=0, keepdims=True)
        sign = 2.0 * chosen - 1.0
        pair_weight = sign * jax.nn.sigmoid(-pair_beta * (sign * (ratio - mate)))
        token = (iota((1, TILE), 1) % TOKENS).astype(f32)
        weights.append(jnp.where(token < count, pair_weight, 0.0))

    for j in range(SUBS):
        lanes = lanes_of(j)
        parts = (part_0, part_1, part_2) + ((part_own,) if j % 2 else ())
        tops = [part[HEAD_DIM + 8 : HEAD_DIM + 9, lanes] for part in parts]
        top = functools.reduce(jnp.maximum, tops)
        factors = [jnp.exp2((one - top) * exp2_scale) for one in tops]
        length = sum(f * part[HEAD_DIM : HEAD_DIM + 1, lanes] for f, part in zip(factors, parts))
        inverse = 1.0 / length
        factors = [f * inverse for f in factors]
        rounded = sum(f * part[:HEAD_DIM, lanes] for f, part in zip(factors, parts)).astype(bf16)
        out[:, lanes] = rounded
        gains[:, lanes] = jnp.concatenate(
            factors + [jnp.zeros((8 - len(factors), TILE), f32)], axis=0
        )
        if j % 2:
            cot = (weights[j // 2] * grads[:, lanes].astype(f32)).astype(bf16)
        else:
            cot = grads[:, lanes]
        cot_aug[:HEAD_DIM, lanes] = cot
        row_dot = -jnp.sum(cot.astype(f32) * rounded.astype(f32), axis=0, keepdims=True)
        high = row_dot.astype(bf16).astype(f32)
        middle = (row_dot - high).astype(bf16).astype(f32)
        low = row_dot - high - middle
        row = iota((16, TILE), 0)
        split = jnp.where(
            row == 0, high, jnp.where(row == 1, middle, jnp.where(row == 2, low, 0.0))
        )
        cot_aug[HEAD_DIM : HEAD_DIM + 16, lanes] = split.astype(bf16)
        cot_aug[HEAD_DIM + 16 :, lanes] = jnp.zeros((HEAD_DIM - 16, TILE), bf16)


def combine(own_notes, sib_notes, grads, parts):
    return call(
        combine_kernel,
        "combine",
        [VMEM] * (3 + len(parts)),
        [shape(HEAD_DIM, LANES), shape(2 * HEAD_DIM, LANES), shape(8, LANES, dtype=f32)],
    )(own_notes, sib_notes, grads, *parts)


def value_aug_of(value_rows):
    column = iota(value_rows.shape, 1)
    return jnp.concatenate([value_rows, (column < 3).astype(f32).astype(bf16)], axis=1)


def backward_kernel(part, splits, chunk, *refs):
    kvs = refs[: len(part)]
    raised, q_aug, cot_aug, gains, after, slopes = refs[len(part) : len(part) + 6]
    grads = refs[len(part) + 6 : len(part) + 6 + len(splits)]
    value_aug, scaled_q, scaled_cot = refs[len(part) + 6 + len(splits) :]
    value_aug[...] = value_aug_of(part_rows(kvs, part, value_cols))
    for j in range(SUBS):
        lanes = lanes_of(j)
        gain = gains[chunk : chunk + 1, lanes]
        scaled_cot[:, lanes] = (cot_aug[:HEAD_DIM, lanes].astype(f32) * gain).astype(bf16)
        scaled_q[:, lanes] = (
            q_aug[:HEAD_DIM, lanes].astype(f32) * (gain * score_scale)
        ).astype(bf16)
        moved = dot(value_aug[...], cot_aug[:, lanes])
        slopes[:, lanes] = (raised[:, lanes].astype(f32) * moved).astype(bf16)
    for columns_here, left, right in (
        (value_cols, raised, scaled_cot),
        (key_cols, slopes, scaled_q),
    ):
        total = dot(left[...], right[...], 1, 1)
        for grad, (numbers, _) in zip(grads, splits):
            for n, number in enumerate(numbers):
                grad[n * BLOCK : (n + 1) * BLOCK, columns_here] = total[
                    number * BLOCK : (number + 1) * BLOCK
                ].astype(grad.dtype)


def backward(kvs, raised, q_aug, cot_aug, gains, after, part, chunk, splits):
    keys = keys_in(part)
    return call(
        functools.partial(backward_kernel, part, splits, chunk),
        "backward",
        [VMEM] * (len(part) + 4) + [AFTER],
        [shape(keys, LANES)]
        + [shape(len(numbers) * BLOCK, KV_COLS, dtype=kind) for numbers, kind in splits],
        [
            pltpu.VMEM((keys, 2 * HEAD_DIM), bf16),
            pltpu.VMEM((HEAD_DIM, LANES), bf16),
            pltpu.VMEM((HEAD_DIM, LANES), bf16),
        ],
        flops=6 * keys * LANES * HEAD_DIM,
    )(*kvs, raised, q_aug, cot_aug, gains, after)


def rows_of(turned_rows):
    rows = turned_rows.T
    return jnp.concatenate(
        [rows[g * TOKENS : (g + 1) * TOKENS] for g in range(GROUP)], axis=1
    )


def finish_kernel(*refs):
    refs = list(refs)
    kv_lists = [[refs.pop(0) for _ in part] for part in all_parts]
    all_slopes = [refs.pop(0) for _ in all_parts]
    (kv_own, kv_recv, raised, q_aug, cot_aug, gains, out, after) = refs[:8]
    (own_result, sib_result, keys) = refs[8:]
    spans, start = [], 0
    for kvs, part in zip(kv_lists, all_parts):
        span = slice(start, start + keys_in(part))
        keys[:, span] = part_rows(kvs, part, key_cols).T
        spans.append(span)
        start = span.stop
    for j in (2, 3, 0, 1):
        lanes = lanes_of(j)
        sib, resp = j // 2, j % 2
        result = sib_result if sib else own_result
        total = None
        for chunk, slopes in enumerate(all_slopes):
            part = dot(keys[:, spans[chunk]], slopes[:, lanes])
            part = part * (gains[chunk : chunk + 1, lanes] * score_scale)
            total = part if total is None else total + part
        if resp:
            gain = gains[3:4, lanes]
            rows = (kv_recv if sib else kv_own)[TOKENS:BLOCK]
            own_raised = raised[:, lanes_of(sib)]
            moved = dot(value_aug_of(rows[:, HEAD_DIM:]), cot_aug[:, lanes])
            own_slopes = (own_raised.astype(f32) * moved).astype(bf16)
            total = total + dot(rows[:, :HEAD_DIM].T, own_slopes) * (gain * score_scale)
            scaled_q = (q_aug[:HEAD_DIM, lanes].astype(f32) * (gain * score_scale)).astype(bf16)
            scaled_cot = (cot_aug[:HEAD_DIM, lanes].astype(f32) * gain).astype(bf16)
            key_grad = dot(own_slopes, scaled_q, 1, 1)
            value_grad = dot(own_raised, scaled_cot, 1, 1)
            result[:, 4 * Q_COLS :] = jnp.concatenate([key_grad, value_grad], axis=1).astype(bf16)
        result[:, resp * Q_COLS : (resp + 1) * Q_COLS] = rows_of(
            out[:, lanes].astype(f32)
        ).astype(bf16)
        result[:, (2 + resp) * Q_COLS : (3 + resp) * Q_COLS] = rows_of(total).astype(bf16)


def finish(kv_lists, slopes, kv_own, kv_recv, raised, q_aug, cot_aug, gains, out, after):
    flat = [kv for kvs in kv_lists for kv in kvs]
    return call(
        finish_kernel,
        "finish",
        [VMEM] * (len(flat) + len(slopes) + 7) + [AFTER],
        [shape(TOKENS, 4 * Q_COLS + KV_COLS)] * 2,
        [pltpu.VMEM((HEAD_DIM, 16 * BLOCK), bf16)],
        flops=6 * 4 * BLOCK * LANES * HEAD_DIM,
    )(*flat, *slopes, kv_own, kv_recv, raised, q_aug, cot_aug, gains, out, after)


def place_kernel(own, recv, prompt_out, resp_out, prompt_dq, resp_dq, resp_dkv, done, sems):
    pairs = []
    core = here()[0]
    for side, source in ((core, own), (1 - core, recv)):
        cols = columns(side, Q_COLS)
        targets = (
            prompt_out.at[:, cols],
            resp_out.at[0, :, cols],
            prompt_dq.at[:, cols],
            resp_dq.at[0, :, cols],
        )
        pairs += [
            (source.at[:, pl.ds(n * Q_COLS, Q_COLS)], target) for n, target in enumerate(targets)
        ]
        pairs.append(
            (source.at[:, pl.ds(4 * Q_COLS, KV_COLS)], resp_dkv.at[0, :, columns(side, KV_COLS)])
        )
    copies = started(pairs, sems)
    done[...] = jnp.zeros_like(done)
    waited(copies)


def place(own, recv):
    prompt = shape(TOKENS, 2 * Q_COLS)
    resp = shape(1, TOKENS, 2 * Q_COLS)
    return call(
        place_kernel,
        "place",
        [VMEM] * 2,
        [prompt, resp, prompt, resp, shape(1, TOKENS, 2 * KV_COLS), shape(8, 128, dtype=f32)],
        [pltpu.SemaphoreType.DMA((10,))],
        out_specs=[HBM] * 5 + [VMEM],
    )(own, recv)


def add_split_kernel(count, *refs):
    terms, outs = refs[:count], refs[count + 1 :]
    start = 0
    for out in outs:
        rows = slice(start, start + out.shape[0])
        total = terms[0][rows].astype(f32)
        for term in terms[1:]:
            total = total + term[rows].astype(f32)
        out[...] = total.astype(out.dtype)
        start += out.shape[0]


def add_split(terms, outs, rows, after, flops=0):
    return call(
        functools.partial(add_split_kernel, len(terms)),
        "add_split",
        [VMEM] * len(terms) + [AFTER],
        [shape(rows, KV_COLS)] * outs,
        flops=flops,
    )(*terms, after)


def sum_column_kernel(grad_z, back_far, back_1, back_2, after, to_1, to_2, to_3):
    for p, out in ((1, to_1), (2, to_2), (3, to_3)):
        rows = slice((p - 1) * BLOCK, p * BLOCK)
        total = grad_z[rows]
        for back in (back_far, back_1, back_2):
            total = total + back[rows].astype(f32)
        out[...] = total.astype(bf16)


def sum_column(*operands):
    return call(
        sum_column_kernel, "sum_column", [VMEM] * 4 + [AFTER], [shape(BLOCK, KV_COLS)] * 3
    )(*operands)


def gate_kernel(value, after, out):
    out[...] = value[...]


def gate(value, after):
    return call(gate_kernel, "gate", [VMEM, AFTER], shape(*value.shape))(value, after)


def last_kernel(kept, recv, after, out):
    core = here()[0]

    @pl.when(core == 0)
    def _():
        out[:, :KV_COLS] = kept[...]
        out[:, KV_COLS:] = recv[...]

    @pl.when(core == 1)
    def _():
        out[:, :KV_COLS] = recv[...]
        out[:, KV_COLS:] = kept[...]


def last(kept, recv, after):
    return call(
        last_kernel, "last", [VMEM] * 2 + [AFTER], shape(TOKENS, 2 * KV_COLS)
    )(kept, recv, after)


def shards(
    prompt_q,
    prompt_kv,
    resp_q,
    resp_kv,
    prompt_grad,
    resp_grad,
    resp_len,
    logratio,
    partner,
    chosen,
):
    prompt_q, prompt_kv, resp_q, resp_kv, prompt_grad, resp_grad = [
        pltpu.with_memory_space_constraint(array, pltpu.HBM)
        for array in (prompt_q, prompt_kv, resp_q, resp_kv, prompt_grad, resp_grad)
    ]
    kv_own, kv_send = pack_kv(prompt_kv, resp_kv)
    kv_recv = swap_core(kv_send)
    q_send = pack_q(prompt_q, resp_q, prompt_grad, resp_grad, kv_send)
    q_recv = swap_core(q_send)
    block = join_cores(logratio, kv_own, kv_recv, q_send)

    block_again = gate(block, q_recv)
    from_x = [shift_x(block_again, 4 - offset) for offset in offsets[1:3]]
    from_z = [shift_z(block, p) for p in (1, 2, 3)]
    q_aug, grads, raised_own, part_own = prep(
        prompt_q, resp_q, prompt_grad, resp_grad, q_recv, kv_own, kv_recv
    )
    near = join(from_x, part_own, *from_z)
    far = join(from_z[1:], part_own, from_z[0], near)
    column = join([block] + from_z, part_own, near)
    early_kvs = [block] + from_z + [near]
    side_kvs = [shift_z(near, 1)] + [shift_x(far, 4 - offset) for offset in offsets[1:3]]
    far_kvs = [shift_x(column, 2)]
    kv_lists = [early_kvs, side_kvs, far_kvs]

    early = forward(early_kvs, q_aug, part_own, early_part)
    note = facts(partner, chosen, resp_len, early[0])
    far_ones = forward(far_kvs, q_aug, early[1], far_part)
    side = forward(side_kvs, q_aug, far_ones[1], side_part)
    raised, packs = zip(early, side, far_ones)
    own_notes = collect(note, kv_lists, far_ones[0])
    out, cot_aug, gains = combine(
        own_notes, swap_core(own_notes), grads, [*packs, part_own]
    )

    def backward_of(chunk, splits, after):
        return backward(
            kv_lists[chunk],
            raised[chunk],
            q_aug,
            cot_aug,
            gains,
            after,
            all_parts[chunk],
            chunk,
            splits,
        )

    slopes_far, grad_far, grad_x3 = backward_of(
        2, (((1, 2, 3), bf16), ((0,), bf16)), gains
    )
    back_far = shift_x(grad_far, 2)
    slopes_side, grad_1, grad_2 = backward_of(
        1, (((0, 2, 3), bf16), ((1, 4, 5), bf16)), grad_far
    )
    back_1, back_2 = shift_x(grad_1, offsets[1]), shift_x(grad_2, offsets[2])
    slopes_early, grad_own, grad_z, *to_x = backward_of(
        0, (((0,), f32), ((1, 2, 3), f32), ((4,), bf16), ((5,), bf16)), grad_1
    )
    slopes = [slopes_early, slopes_side, slopes_far]

    to_x3 = gate(grad_x3, back_far)
    back_x = [
        shift_x(term, offset) for term, offset in zip((*to_x, to_x3), offsets[1:])
    ]
    to_z = sum_column(grad_z, back_far, back_1, back_2, to_x3)
    back_z = [shift_z(term, 4 - p) for p, term in zip((1, 2, 3), to_z)]
    own_result, sib_result = finish(
        kv_lists, slopes, kv_own, kv_recv, raised_own, q_aug, cot_aug, gains, out, grad_own
    )
    prompt_out, resp_out, prompt_dq, resp_dq, resp_dkv, placed = place(
        own_result, swap_core(sib_result)
    )
    kept, sent = add_split([grad_own] + back_z + back_x, 2, TOKENS, grad_own, 2 * 10**10)
    prompt_dkv = last(kept, swap_core(sent), placed)
    return (prompt_out, resp_out, prompt_dq, resp_dq, prompt_dkv, resp_dkv)


def solution(mesh):
    return jax.shard_map(
        shards,
        mesh=mesh,
        in_specs=(
            P(("batch", "resp"), "head"),
            P(("batch", "resp"), "head"),
            P(("batch", "resp"), None, "head"),
            P(("batch", "resp"), None, "head"),
            P(("batch", "resp"), "head"),
            P(("batch", "resp"), None, "head"),
            P(("batch", "resp")),
            P(("batch", "resp")),
            P(("batch", "resp")),
            P(("batch", "resp")),
        ),
        out_specs=(
            P(("batch", "resp"), "head"),
            P(("batch", "resp"), None, "head"),
            P(("batch", "resp"), "head"),
            P(("batch", "resp"), None, "head"),
            P(("batch", "resp"), "head"),
            P(("batch", "resp"), None, "head"),
        ),
        check_vma=False,
    )
```
